128 devices in a mesh: group: 4 (over z), tile: 32 (over y, x, core).
Axes of the slice: x: 4, y: 4, z: 4, core: 2. Of those that a mesh axis runs over, the one named last changes fastest.
Arguments:
- loads: float32 [1024, 8, 384], P(('group', 'tile')), may hold values from -6 to 6
- local_inverse: float32 [1024, 384, 384], P(('group', 'tile')), as said below
- schur: float32 [1024, 384, 384], P(('group', 'tile')), as said below
- corner_map: float32 [1024, 8, 384], P(('group', 'tile')), may hold values from -0.6 to 0.6
- corner_index: int32 [1024, 8], P(('group', 'tile')), may hold values from 0 to 8191, as said below
- partner: int32 [1024, 12], P(('group', 'tile')), may hold values from 0 to 287, as said below
- coarse_inverse: float32 [8192, 64], P(('group', 'tile')), as said below
Outputs:
- multipliers: float32 [1024, 8, 384], P(('group', 'tile'))
- residual: float32 [1024, 8, 384], P(('group', 'tile'))
- preconditioned: float32 [1024, 8, 384], P(('group', 'tile'))
The draws below stay inside these ranges and needn't reach their ends.
Inputs may be any that keep to these rules, and one draw needn't show every extreme that they name: `partner`: the pairing of contact faces is symmetric: the mate of a face's mate is the face itself; every face has a mate on its own device or on the device of the tile one below or one above in the same group, tiles counted around the group; at most 2 * (12) faces of one device have mates on the tile above, and as many on the tile below, and some device reaches that number. `corner_index`: the corner dofs of one device name at most 4 coarse rows (counted with repeats) in the block of 64 rows of any one owner device; one owner block receives exactly 4 from every device. `local_inverse`: each block is symmetric and strictly diagonally dominant with a positive diagonal. `schur`: each block is symmetric and strictly diagonally dominant with a positive diagonal. `coarse_inverse`: each block of 64 rows is symmetric and strictly diagonally dominant with a positive diagonal.
All inputs are finite; a program needn't handle non-finite values.
Results may differ from the reference program's by a relative error of at most 0.0003.
Values sent between devices are 32-bit elements; how exact they have to be, the bound alone decides.
No kernel may reach another device: no remote copies, remote signals or barrier semaphores. Data moves between devices by JAX's collectives and lax.ppermute only.
A program may use at most 64 MiB of HBM per device.

```python
import jax
import jax.numpy as jnp
from jax import lax

PDEV = 8
CONTACTS = 12
BLOCK = 32
IFACE = 384
CASES = 8
CORNERS = 8
CAPC = 4
CROWS_DEV = 64
ITERS = 2
PARTICLES = 1024
COARSE = 8192
N_GROUP = 4
N_TILE = 32


def dominant_blocks(key, count, width, lowest, highest_diag):
    uniform_part = jax.random.uniform(key, (count, width, width), jnp.float32, -1.0, 1.0)
    offdiag = (uniform_part + jnp.swapaxes(uniform_part, 1, 2)) * (0.45 / width)
    diagonal = jax.random.uniform(jax.random.fold_in(key, 3), (count, width), jnp.float32, lowest, highest_diag)
    identity = jnp.eye(width, dtype=jnp.float32)
    return offdiag * (1.0 - identity) + identity * diagonal[:, :, None]


def draw_local_inverse(key, part):
    return dominant_blocks(jax.random.fold_in(key, 1), N_GROUP * N_TILE * PDEV, CONTACTS * BLOCK, 1.0, 2.0)


def draw_schur(key, part):
    return dominant_blocks(jax.random.fold_in(key, 2), N_GROUP * N_TILE * PDEV, CONTACTS * BLOCK, 1.0, 3.0)


def draw_coarse_inverse(key, part):
    blocks = dominant_blocks(jax.random.fold_in(key, 5), N_GROUP * N_TILE, CROWS_DEV, 1.0, 2.0)
    return blocks.reshape(N_GROUP * N_TILE * CROWS_DEV, CROWS_DEV)


def draw_corner_index(key, part):
    device_count = N_GROUP * N_TILE
    row_count = PDEV * CORNERS
    buckets = row_count // CAPC
    spare = device_count - buckets
    center = jax.random.randint(jax.random.fold_in(key, 21), (), 0, device_count).astype(jnp.int32)

    def one_device(sub_key):
        keys = jax.random.split(sub_key, 4)
        order = 1 + jax.random.permutation(keys[0], device_count - 1).astype(jnp.int32)
        owner_list = jnp.concatenate([center[None], (center + order) % device_count]).astype(jnp.int32)
        positions = jnp.arange(row_count, dtype=jnp.int32)
        grouped = (jax.random.randint(keys[1], (row_count,), 0, 2) == 1) | (positions < CAPC)
        chosen = jnp.where(grouped, owner_list[positions // CAPC], owner_list[buckets + positions % spare])
        chosen = chosen[jax.random.permutation(keys[2], row_count)]
        local_rows = jax.random.randint(keys[3], (row_count,), 0, CROWS_DEV).astype(jnp.int32)
        return (chosen * CROWS_DEV + local_rows).astype(jnp.int32)
    device_keys = jax.random.split(jax.random.fold_in(key, 23), device_count)
    result = jax.vmap(one_device)(device_keys)
    return result.reshape(device_count * PDEV, CORNERS).astype(jnp.int32)


def draw_partner(key, part):
    faces = PDEV * CONTACTS
    device_count = N_GROUP * N_TILE
    device_keys = jax.random.split(jax.random.fold_in(key, 7), device_count)
    orders = jax.vmap(lambda k: jax.random.permutation(k, faces))(device_keys)
    orders = orders.reshape(N_GROUP, N_TILE, faces).astype(jnp.int32)
    upward = 2 * jax.random.randint(jax.random.fold_in(key, 11), (N_GROUP, N_TILE), 1, faces // 8 + 1).astype(jnp.int32)
    upward = upward.at[:, 0].set(2 * (faces // 8))
    downward = jnp.roll(upward, 1, axis=1)
    ranking = jnp.argsort(orders, axis=-1).astype(jnp.int32)
    up_count = upward[:, :, None]
    down_count = downward[:, :, None]
    next_orders = jnp.roll(orders, -1, axis=1)
    next_up = jnp.roll(upward, -1, axis=1)[:, :, None]
    prev_orders = jnp.roll(orders, 1, axis=1)
    to_upper = jnp.take_along_axis(next_orders, jnp.clip(next_up + ranking, 0, faces - 1), axis=-1) + 2 * faces
    to_lower = jnp.take_along_axis(prev_orders, jnp.clip(ranking - up_count, 0, faces - 1), axis=-1)
    local_rank = jnp.clip(ranking - up_count - down_count, 0, faces - 1)
    mate_rank = jnp.clip(up_count + down_count + jnp.bitwise_xor(local_rank, 1), 0, faces - 1)
    to_self = jnp.take_along_axis(orders, mate_rank, axis=-1) + faces
    result = jnp.where(ranking < up_count, to_upper, jnp.where(ranking < up_count + down_count, to_lower, to_self))
    return result.reshape(device_count * PDEV, CONTACTS).astype(jnp.int32)


def block_scale(key, shape, cuts, smallest, top_value):
    def one(axis_at, blocks):
        heights = jax.random.uniform(jax.random.fold_in(jax.random.fold_in(key, 6), axis_at), (blocks,), jnp.float32, smallest / len(cuts), top_value / len(cuts))
        return jnp.repeat(jnp.exp(heights), shape[axis_at] // blocks).reshape((-1,) + (1,) * (len(shape) - axis_at - 1))

    gain = one(*cuts[0])
    for cut in cuts[1:]:
        gain = gain * one(*cut)
    return gain


def bell_draw(stream_key, dims, spread, reach, shards=(), held_as=jnp.bfloat16):
    factor_of = block_scale(stream_key, dims, shards, -0.22, 0.18) if shards else 1.0
    drawn = jax.random.normal(stream_key, dims, jnp.float32) * spread * factor_of
    return jnp.minimum(jnp.maximum(drawn, -reach), reach).astype(held_as)


def setup_inputs(seed: int = 0) -> dict:
    splits = jax.random.split(jax.random.key(seed), 8)
    loads = bell_draw(splits[0], (PARTICLES, CASES, IFACE), 1.0, 6.0, ((0, 128),), jnp.float32)
    local_inverse = draw_local_inverse(jax.random.fold_in(splits[7], 71), 0)
    schur = draw_schur(jax.random.fold_in(splits[7], 71), 0)
    corner_map = bell_draw(splits[3], (PARTICLES, CORNERS, IFACE), 0.1, 0.6, ((0, 128),), jnp.float32)
    corner_index = draw_corner_index(jax.random.fold_in(splits[7], 71), 0)
    partner = draw_partner(jax.random.fold_in(splits[7], 71), 0)
    coarse_inverse = draw_coarse_inverse(jax.random.fold_in(splits[7], 71), 0)
    return dict(loads=loads, local_inverse=local_inverse, schur=schur, corner_map=corner_map, corner_index=corner_index, partner=partner, coarse_inverse=coarse_inverse)


highest = lax.Precision.HIGHEST


def apply_blocks(matrices, vectors):
    return jnp.einsum("pij,pkj->pki", matrices, vectors, precision=highest)


def global_mates(partner):
    device_index = jnp.arange(PARTICLES, dtype=jnp.int32) // PDEV
    group_index = device_index // N_TILE
    tile_index = device_index % N_TILE
    region = partner // (PDEV * CONTACTS)
    within = partner % (PDEV * CONTACTS)
    mate_tile = (tile_index[:, None] + region - 1) % N_TILE
    global_face = (group_index[:, None] * N_TILE + mate_tile) * (PDEV * CONTACTS) + within
    return (global_face // CONTACTS).astype(jnp.int32), (global_face % CONTACTS).astype(jnp.int32)


def contact_jump(field, mate_particle, mate_face):
    blocked = field.reshape(PARTICLES, CASES, CONTACTS, BLOCK)
    other = blocked[mate_particle, :, mate_face, :]
    return field - jnp.transpose(other, (0, 2, 1, 3)).reshape(field.shape)


def coarse_term(field, corner_map, corner_index, coarse_inverse):
    contrib = jnp.einsum("pci,pki->pck", corner_map, field, precision=highest)
    total = jnp.zeros((COARSE, CASES), jnp.float32).at[corner_index.reshape(-1)].add(contrib.reshape(-1, CASES))
    blocks = coarse_inverse.reshape(COARSE // CROWS_DEV, CROWS_DEV, CROWS_DEV)
    solved = jnp.einsum("bij,bjk->bik", blocks, total.reshape(COARSE // CROWS_DEV, CROWS_DEV, CASES), precision=highest)
    picked = solved.reshape(COARSE, CASES)[corner_index]
    return jnp.einsum("pci,pck->pki", corner_map, picked, precision=highest)


def reference(loads, local_inverse, schur, corner_map, corner_index, partner, coarse_inverse):
    mate_particle, mate_face = global_mates(partner)

    def operate(vectors):
        return contact_jump(apply_blocks(local_inverse, vectors), mate_particle, mate_face)

    def precondition(vectors):
        primal = apply_blocks(schur, vectors) + coarse_term(vectors, corner_map, corner_index, coarse_inverse)
        return 0.5 * contact_jump(primal, mate_particle, mate_face)

    def inner(first, second):
        return jnp.sum(first * second, axis=(0, 2))

    rhs = operate(loads)
    multipliers = jnp.zeros_like(rhs)
    residual = rhs
    preconditioned = precondition(residual)
    direction = preconditioned
    energy_now = inner(residual, preconditioned)
    for iteration in range(ITERS):
        image = operate(direction)
        step_size = energy_now / inner(direction, image)
        multipliers = multipliers + step_size[None, :, None] * direction
        residual = residual - step_size[None, :, None] * image
        preconditioned = precondition(residual)
        if iteration + 1 < ITERS:
            energy_new = inner(residual, preconditioned)
            direction = preconditioned + (energy_new / energy_now)[None, :, None] * direction
            energy_now = energy_new
    return multipliers, residual, preconditioned
```

```python
import jax
import jax.numpy as jnp
from jax import lax
from jax.sharding import PartitionSpec as P

highest = lax.Precision.HIGHEST
GT = ("group", "tile")


def swap_lists(tiles):
    inner_swap = [(i, i ^ 1) for i in range(tiles)]
    outer_swap = [(i, (i - 1) % tiles if i % 2 == 0 else (i + 1) % tiles) for i in range(tiles)]
    return inner_swap, outer_swap


def apply_blocks(matrices, vectors):
    return jnp.einsum("pij,pkj->pki", matrices, vectors, precision=highest)


def inner(first, second):
    return jnp.sum(first * second, axis=(0, 2))


def shards(loads, local_inverse, schur, corner_map, corner_index, partner, coarse_inverse):
    count, cases, width = loads.shape
    faces = partner.shape[1]
    corners = corner_index.shape[1]
    slots = count * corners
    rows = coarse_inverse.shape[0]
    tiles = lax.axis_size("tile")
    devices = lax.axis_size(GT)
    inner_swap, outer_swap = swap_lists(tiles)
    same_core = [[2 * i + c for i in range(devices // 2)] for c in range(2)]
    tile = lax.axis_index("tile")
    core = tile % 2
    me = lax.axis_index("group") * tiles + tile

    def pool(x):
        a = lax.ppermute(x, "tile", inner_swap)
        b = lax.ppermute(x, "tile", outer_swap)
        return jnp.concatenate([a, x, b], axis=0)

    region = partner // (count * faces)
    region = jnp.where(core == 1, region, 2 - region)
    within = partner % (count * faces)
    mate_particle = region * count + within // faces
    mate_face = within % faces

    def jump(pooled):
        blocked = pooled.reshape(3 * count, cases, faces, width // faces)
        other = blocked[mate_particle, :, mate_face, :]
        return pooled[count : 2 * count] - jnp.transpose(other, (0, 2, 1, 3)).reshape(count, cases, width)

    card = jnp.concatenate(
        [coarse_inverse.reshape(-1), corner_index.reshape(-1).astype(jnp.float32), jnp.zeros((64,), jnp.float32)]
    )
    half = lax.all_to_all(
        jnp.broadcast_to(card[None], (devices // 2, card.shape[0])), GT, 0, 0, tiled=True, axis_index_groups=same_core
    )
    other_half = lax.ppermute(half, "tile", inner_swap)
    first = jnp.where(core == 0, half, other_half)
    second = jnp.where(core == 0, other_half, half)
    cards = jnp.stack([first, second], axis=1).reshape(devices, -1)
    all_inverse = cards[:, : rows * rows].reshape(devices * rows, rows)
    all_index = cards[:, rows * rows : rows * rows + slots].astype(jnp.int32)
    base = me - tile
    inner_tile = jnp.where(core == 0, tile + 1, tile - 1)
    outer_tile = jnp.where(core == 0, (tile + tiles - 1) % tiles, (tile + 1) % tiles)
    wanted = jnp.concatenate([all_index[base + inner_tile], all_index[me], all_index[base + outer_tile]])
    flat = all_index.reshape(-1)
    inverse_rows = all_inverse[wanted]
    onehot = (lax.iota(jnp.int32, rows)[:, None] == (flat % rows)[None, :]).astype(jnp.float32)
    spread = jnp.dot(inverse_rows, onehot, precision=highest)
    weights = jnp.where((wanted // rows)[:, None] == (flat // rows)[None, :], spread, 0.0)
    map_pool = pool(corner_map)

    def gather(field, sums):
        contrib = jnp.einsum("pci,pki->kpc", corner_map, field, precision=highest).reshape(-1)
        parts = jnp.concatenate([contrib] + sums + [jnp.zeros((128 - cases * len(sums),), jnp.float32)])
        got = lax.all_to_all(jnp.broadcast_to(parts[None], (devices, parts.shape[0])), GT, 0, 0, tiled=True)
        body = got[:, : cases * slots].reshape(devices, cases, slots)
        totals = jnp.sum(got[:, cases * slots :], axis=0)
        return body, [totals[i * cases : (i + 1) * cases] for i in range(len(sums))]

    def precondition(field, sums):
        body, totals = gather(field, sums)
        pooled = pool(apply_blocks(schur, field))
        g = jnp.transpose(body, (0, 2, 1)).reshape(devices * slots, cases)
        sol = jnp.dot(weights, g, precision=highest).reshape(3 * count, corners, cases)
        pooled = pooled + jnp.einsum("pci,pck->pki", map_pool, sol, precision=highest)
        return 0.5 * jump(pooled), totals

    def operate(field):
        return jump(pool(apply_blocks(local_inverse, field)))

    def by(s, x):
        return s[None, :, None] * x

    r0 = operate(loads)
    z0, _ = precondition(r0, [])
    w0 = operate(z0)
    y0, (rz0, pw0) = precondition(w0, [inner(r0, z0), inner(z0, w0)])
    a0 = rz0 / pw0
    r1 = r0 - by(a0, w0)
    z1 = z0 - by(a0, y0)
    v1 = operate(z1)
    y1, (rz1, zv, pv, zw) = precondition(v1, [inner(r1, z1), inner(z1, v1), inner(z0, v1), inner(z1, w0)])
    b0 = rz1 / rz0
    a1 = rz1 / (zv + b0 * (pv + zw) + b0 * b0 * pw0)
    multipliers = by(a0, z0) + by(a1, z1 + by(b0, z0))
    residual = r1 - by(a1, v1 + by(b0, w0))
    preconditioned = z1 - by(a1, y1 + by(b0, y0))
    return multipliers, residual, preconditioned


def solution(mesh):
    three = P(GT, None, None)
    two = P(GT, None)
    return jax.shard_map(
        shards,
        mesh=mesh,
        in_specs=(three, three, three, three, two, two, two),
        out_specs=(three, three, three),
        check_vma=False,
    )
```

```python
import functools

import jax
import jax.numpy as jnp
from jax import lax
from jax.experimental import pallas as pl
from jax.experimental.pallas import tpu as pltpu
from jax.sharding import PartitionSpec as P

GT = ("group", "tile")
F32 = jnp.float32
BF16 = jnp.bfloat16
NT = (((1,), (1,)), ((), ()))
VMEM = pl.BlockSpec(memory_space=pltpu.VMEM)
SMEM = pl.BlockSpec(memory_space=pltpu.SMEM)
PARAMS = pltpu.CompilerParams(vmem_limit_bytes=24 << 20)

COUNT, CASES, WIDTH, CORNERS, ROWS, FACES = 8, 8, 384, 8, 64, 12
CHUNKS = WIDTH // 128
TILES = COUNT * CHUNKS
SLOTS = COUNT * CORNERS
CARD = 40
PAY = 8


def call(kernel, outs, specs, scratch=()):
    return pl.pallas_call(
        kernel,
        in_specs=specs,
        out_specs=[VMEM] * len(outs),
        out_shape=outs,
        scratch_shapes=list(scratch),
        compiler_params=PARAMS,
    )


def shape(*dims):
    return jax.ShapeDtypeStruct(dims, F32)


def halves(x):
    high = x.astype(BF16)
    return high, (x - high.astype(F32)).astype(BF16)


def product(vector, matrix):
    vh, vl = halves(vector)
    mh, ml = halves(matrix)
    first = jnp.dot(jnp.concatenate([vh, vl], 0), mh, preferred_element_type=F32)
    return first[:8] + first[8:] + jnp.dot(vh, ml, preferred_element_type=F32)


def lanes(shape_=(8, 128)):
    return lax.broadcasted_iota(jnp.int32, shape_, 1)


def sublanes(shape_=(8, 128)):
    return lax.broadcasted_iota(jnp.int32, shape_, 0)


def put_tiles(ref, p, row):
    for c in range(CHUNKS):
        ref[p * CHUNKS + c] = row[:, c * 128 : (c + 1) * 128]


def get_row(tiles, p):
    return jnp.concatenate([tiles[p * CHUNKS + c] for c in range(CHUNKS)], axis=1)


def jump(pool, table):
    quarter = lanes() // 32
    out = []
    for t in range(TILES):
        p, c = divmod(t, CHUNKS)
        other = None
        for q in range(4):
            f = p * FACES + c * 4 + q
            face = pltpu.roll(pool[table[0, f]], table[1, f], 1)
            other = face if other is None else jnp.where(quarter == q, face, other)
        out.append(pool[TILES + t] - other)
    return out


def fill_pool(pool, a_ref, x_ref, b_ref):
    for e, ref in enumerate((a_ref, x_ref, b_ref)):
        for t in range(TILES):
            pool[e * TILES + t] = ref[t]


def card_kernel(inverse_ref, index_ref, card_ref):
    inverse = inverse_ref[...]
    block = jnp.concatenate([inverse[:32], inverse[32:]], axis=1)
    card_ref[:, 0:32, :] = jnp.broadcast_to(block[None], (card_ref.shape[0], 32, 128))
    row = index_row(index_ref)
    card_ref[:, 32:40, :] = jnp.broadcast_to(row[None], (card_ref.shape[0], 8, 128))


def index_row(index_ref):
    index = index_ref[...].astype(F32)
    wide = jnp.concatenate([index] * 16, axis=1)
    keep = lanes() // 8 == sublanes()
    return jnp.broadcast_to(jnp.sum(jnp.where(keep, wide, 0.0), axis=0, keepdims=True), (8, 128))


def start_kernel(loads_ref, index_ref, inverse_ref, out_ref):
    for p in range(COUNT):
        put_tiles(out_ref, p, product(loads_ref[p], inverse_ref[p]))
    out_ref[TILES] = index_row(index_ref)


def column_to_row(columns):
    lane, sub = lanes(), sublanes()
    row = jnp.zeros((8, 128), F32)
    for i, column in enumerate(columns):
        row = jnp.where(lane == i * 8 + sub, jnp.broadcast_to(column, (8, 128)), row)
    return jnp.sum(row, axis=0, keepdims=True)


def case_sum(first, second):
    total = first[0] * second[0]
    for t in range(1, TILES):
        total = total + first[t] * second[t]
    return jnp.sum(total, axis=1, keepdims=True)


def send(r, map_ref, columns, pay_ref):
    lane, sub = lanes(), sublanes()
    contrib = jnp.zeros((8, 128), F32)
    for p in range(COUNT):
        for j in range(CORNERS):
            part = r[p * CHUNKS] * map_ref[p, j : j + 1, 0:128]
            for c in range(1, CHUNKS):
                part = part + r[p * CHUNKS + c] * map_ref[p, j : j + 1, c * 128 : (c + 1) * 128]
            total = jnp.sum(part, axis=1, keepdims=True)
            contrib = jnp.where(lane == p * CORNERS + j, jnp.broadcast_to(total, (8, 128)), contrib)
    turned = pltpu.roll(pltpu.roll(contrib, 64, 1), 4, 0)
    pay = jnp.where(lane < 64, contrib, turned)
    if columns:
        pay = jnp.where(sub < 4, pay, jnp.broadcast_to(column_to_row(columns), (8, 128)))
    pay_ref[...] = jnp.broadcast_to(pay[None], pay_ref.shape)


def send_first_kernel(table, a_ref, x_ref, b_ref, map_ref, r_ref, pay_ref, pool):
    fill_pool(pool, a_ref, x_ref, b_ref)
    r = jump(pool, table)
    for t in range(TILES):
        r_ref[t] = r[t]
    send(r, map_ref, [], pay_ref)


def send_second_kernel(table, a_ref, x_ref, b_ref, map_ref, r0_ref, z0_ref, w_ref, pay_ref, pool):
    fill_pool(pool, a_ref, x_ref, b_ref)
    w = jump(pool, table)
    for t in range(TILES):
        w_ref[t] = w[t]
    send(w, map_ref, [case_sum(r0_ref, z0_ref), case_sum(z0_ref, w)], pay_ref)


def send_third_kernel(
    table, a_ref, x_ref, b_ref, map_ref, r1_ref, z1_ref, z0_ref, w0_ref, v_ref, pay_ref, pool
):
    fill_pool(pool, a_ref, x_ref, b_ref)
    v = jump(pool, table)
    for t in range(TILES):
        v_ref[t] = v[t]
    columns = [case_sum(r1_ref, z1_ref), case_sum(z1_ref, v), case_sum(z0_ref, v), case_sum(z1_ref, w0_ref)]
    send(v, map_ref, columns, pay_ref)


def product_kernel(x_ref, matrix_ref, out_ref):
    for p in range(COUNT):
        put_tiles(out_ref, p, product(get_row(x_ref, p), matrix_ref[p]))


def weights_kernel(core, wanted, own_ref, other_ref, out_ref, rows, names, index):
    mine = core[0]

    def pick(j, carry):
        row = wanted[j]
        owner = row // ROWS
        at = (owner // 2) * CARD + row % 32
        same = (owner % 2) == mine
        here = own_ref[pl.ds(at, 1), :]
        there = other_ref[pl.ds(at, 1), :]
        rows[pl.ds(j, 1), :] = jnp.where(same, here, there)
        names[pl.ds(j, 1), :] = jnp.full((1, 128), row, jnp.int32)
        return carry

    lax.fori_loop(0, 3 * SLOTS, pick, 0, unroll=8)
    chips = own_ref.shape[0] // CARD
    own = own_ref[pl.ds(32, chips, stride=CARD), :]
    other = other_ref[pl.ds(32, chips, stride=CARD), :]
    first = jnp.where(mine == 0, own, other)
    second = jnp.where(mine == 0, other, own)
    wide = lanes((chips, 128))
    index[...] = jnp.where(wide < 64, first, pltpu.roll(second, 64, 1)).astype(jnp.int32)
    lane = lanes((3 * SLOTS, 128))
    upper = (names[...] % ROWS) >= 32
    kept = jnp.where(upper == (lane >= 64), rows[...], 0.0)
    high, low = halves(kept)
    both = jnp.concatenate([high, low], axis=0)
    blocks = names[...] // ROWS

    def spread(q, carry):
        row = index[pl.ds(q, 1), :]
        onehot = (sublanes((128, 128)) % ROWS == row % ROWS).astype(F32).astype(BF16)
        full = jnp.dot(both, onehot, preferred_element_type=F32)
        hit = blocks == row // ROWS
        hit = jnp.concatenate([hit, hit], axis=0)
        at = pl.ds(pl.multiple_of(q * 128, 128), 128)
        out_ref[:, at] = jnp.where(hit, full, 0.0).astype(BF16)
        return carry

    lax.fori_loop(0, chips, spread, 0)


def coarse_into_pool(got_ref, weights_ref, maps, pool, gathered):
    lane, sub = lanes(), sublanes()
    straight = (sub < 4) == (lane < 64)
    sums = jnp.zeros((8, 128), F32)
    for q in range(got_ref.shape[0] // (2 * PAY)):
        first = got_ref[2 * q * PAY : 2 * q * PAY + 8, :]
        second = got_ref[(2 * q + 1) * PAY : (2 * q + 1) * PAY + 8, :]
        sums = sums + first + second
        pair = jnp.where(sub < 4, first, pltpu.roll(second, 4, 0))
        tile = jnp.where(straight, pair, pltpu.roll(pltpu.roll(pair, 64, 1), 4, 0))
        high, low = halves(tile)
        gathered[:, q * 128 : (q + 1) * 128] = jnp.concatenate([high, low], axis=0)
    out = lax.dot_general(weights_ref[...], gathered[...], NT, preferred_element_type=F32)
    count = 3 * SLOTS
    sol = out[:count] + out[count:]
    sol = sol.T
    sol = sol[:8] + sol[8:]
    own = lax.broadcasted_iota(jnp.int32, (64, 64), 0) // 8 == lax.broadcasted_iota(jnp.int32, (64, 64), 1) // 8
    for e, map_ref in enumerate(maps):
        part = sol[:, e * SLOTS : (e + 1) * SLOTS]
        spread = jnp.where(own, jnp.concatenate([part] * COUNT, axis=0), 0.0)
        sh, sl = halves(spread)
        ch, cl = halves(map_ref[...].reshape(SLOTS, WIDTH))
        two = jnp.dot(jnp.concatenate([sh, sl], axis=0), ch, preferred_element_type=F32)
        full = two[:64] + two[64:] + jnp.dot(sh, cl, preferred_element_type=F32)
        for p in range(COUNT):
            for c in range(CHUNKS):
                t = e * TILES + p * CHUNKS + c
                pool[t] = pool[t] + full[p * 8 : (p + 1) * 8, c * 128 : (c + 1) * 128]
    return sums


def totals(sums, count):
    lane, sub = lanes(), sublanes()
    row = jnp.broadcast_to(sums[4:5], (8, 128))
    return [
        jnp.broadcast_to(jnp.sum(jnp.where(lane == i * 8 + sub, row, 0.0), axis=1, keepdims=True), (8, 128))
        for i in range(count)
    ]


def solve_first_kernel(
    table, got_ref, weights_ref, am_ref, m_ref, bm_ref, a_ref, x_ref, b_ref, inverse_ref, z_ref, u_ref, pool, gathered
):
    fill_pool(pool, a_ref, x_ref, b_ref)
    coarse_into_pool(got_ref, weights_ref, (am_ref, m_ref, bm_ref), pool, gathered)
    z = [0.5 * t for t in jump(pool, table)]
    for t in range(TILES):
        z_ref[t] = z[t]
    for p in range(COUNT):
        put_tiles(u_ref, p, product(get_row(z, p), inverse_ref[p]))


def solve_second_kernel(
    table, got_ref, weights_ref, am_ref, m_ref, bm_ref, a_ref, x_ref, b_ref, inverse_ref, r0_ref, z0_ref, w0_ref,
    y_ref, r_ref, z_ref, scale_ref, u_ref, pool, gathered,
):
    fill_pool(pool, a_ref, x_ref, b_ref)
    sums = coarse_into_pool(got_ref, weights_ref, (am_ref, m_ref, bm_ref), pool, gathered)
    energy, curve = totals(sums, 2)
    step = energy / curve
    scale_ref[0] = energy
    scale_ref[1] = curve
    scale_ref[2] = step
    y = jump(pool, table)
    z = []
    for t in range(TILES):
        half = 0.5 * y[t]
        y_ref[t] = half
        r_ref[t] = r0_ref[t] - step * w0_ref[t]
        z.append(z0_ref[t] - step * half)
        z_ref[t] = z[t]
    for p in range(COUNT):
        put_tiles(u_ref, p, product(get_row(z, p), inverse_ref[p]))


def solve_third_kernel(
    table, got_ref, weights_ref, am_ref, m_ref, bm_ref, a_ref, x_ref, b_ref,
    scale_ref, z0_ref, w0_ref, y0_ref, r1_ref, z1_ref, v1_ref, multipliers_ref, residual_ref, preconditioned_ref,
    pool, gathered,
):
    fill_pool(pool, a_ref, x_ref, b_ref)
    sums = coarse_into_pool(got_ref, weights_ref, (am_ref, m_ref, bm_ref), pool, gathered)
    energy, zv, pv, zw = totals(sums, 4)
    first = scale_ref[2]
    grow = energy / scale_ref[0]
    second = energy / (zv + grow * (pv + zw) + grow * grow * scale_ref[1])
    y = jump(pool, table)
    for p in range(COUNT):
        for c in range(CHUNKS):
            t = p * CHUNKS + c
            at = slice(c * 128, (c + 1) * 128)
            multipliers_ref[p, :, at] = first * z0_ref[t] + second * (z1_ref[t] + grow * z0_ref[t])
            residual_ref[p, :, at] = r1_ref[t] - second * (v1_ref[t] + grow * w0_ref[t])
            preconditioned_ref[p, :, at] = z1_ref[t] - second * (0.5 * y[t] + grow * y0_ref[t])


def shards(loads, local_inverse, schur, corner_map, corner_index, partner, coarse_inverse):
    tiles = lax.axis_size("tile")
    devices = lax.axis_size(GT)
    inner_swap = [(i, i ^ 1) for i in range(tiles)]
    outer_swap = [(i, (i - 1) % tiles if i % 2 == 0 else (i + 1) % tiles) for i in range(tiles)]
    same_core = [[2 * i + c for i in range(devices // 2)] for c in range(2)]
    core = lax.axis_index("tile") % 2

    def both(x):
        return lax.ppermute(x, "tile", inner_swap), lax.ppermute(x, "tile", outer_swap)

    region = partner // (COUNT * FACES)
    region = jnp.where(core == 1, region, 2 - region)
    within = partner % (COUNT * FACES)
    face = within % FACES
    source = region * TILES + (within // FACES) * CHUNKS + face // 4
    turn = ((lax.iota(jnp.int32, FACES)[None, :] - face) % 4) * 32
    table = jnp.stack([source.reshape(-1), turn.reshape(-1)])

    field = shape(TILES, 8, 128)
    pool = pltpu.VMEM((3 * TILES, 8, 128), F32)
    gathered = pltpu.VMEM((16, devices * SLOTS), BF16)
    pay = shape(devices, PAY, 128)

    (card,) = call(card_kernel, [shape(devices // 2, CARD, 128)], [VMEM] * 2)(coarse_inverse, corner_index)
    own_cards = lax.all_to_all(card, GT, 0, 0, tiled=True, axis_index_groups=same_core)
    (u,) = call(start_kernel, [shape(TILES + 1, 8, 128)], [VMEM] * 3)(loads, corner_index, local_inverse)
    ua, ub = both(u)
    ma, mb = both(corner_map)
    maps = (ma, corner_map, mb)
    other_cards = lax.ppermute(own_cards, "tile", inner_swap)

    def spread(x):
        return lax.all_to_all(x, GT, 0, 0, tiled=True).reshape(devices * PAY, 128)

    def through(x):
        (q,) = call(product_kernel, [field], [VMEM] * 2)(x, schur)
        qa, qb = both(q)
        return qa, q, qb

    r0, parts = call(send_first_kernel, [field, pay], [SMEM] + [VMEM] * 4, [pool])(table, ua, u, ub, corner_map)
    got = spread(parts)
    wanted = jnp.concatenate(
        [ua[TILES, 0, :SLOTS].astype(jnp.int32), corner_index.reshape(-1), ub[TILES, 0, :SLOTS].astype(jnp.int32)]
    )
    (weights,) = call(
        lambda *refs: weights_kernel(*refs),
        [jax.ShapeDtypeStruct((6 * SLOTS, devices * SLOTS), BF16)],
        [SMEM] * 2 + [VMEM] * 2,
        [pltpu.VMEM((3 * SLOTS, 128), F32), pltpu.VMEM((3 * SLOTS, 128), jnp.int32),
         pltpu.VMEM((devices // 2, 128), jnp.int32)],
    )(core.reshape(1), wanted, own_cards.reshape(-1, 128), other_cards.reshape(-1, 128))
    pooled = through(r0)
    z0, u = call(solve_first_kernel, [field] * 2, [SMEM] + [VMEM] * 9, [pool, gathered])(
        table, got, weights, *maps, *pooled, local_inverse
    )
    ua, ub = both(u)
    w0, parts = call(send_second_kernel, [field, pay], [SMEM] + [VMEM] * 6, [pool])(
        table, ua, u, ub, corner_map, r0, z0
    )
    got = spread(parts)
    pooled = through(w0)
    y0, r1, z1, scale, u = call(
        solve_second_kernel, [field, field, field, shape(3, 8, 128), field], [SMEM] + [VMEM] * 12, [pool, gathered]
    )(table, got, weights, *maps, *pooled, local_inverse, r0, z0, w0)
    ua, ub = both(u)
    v1, parts = call(send_third_kernel, [field, pay], [SMEM] + [VMEM] * 8, [pool])(
        table, ua, u, ub, corner_map, r1, z1, z0, w0
    )
    got = spread(parts)
    pooled = through(v1)
    return tuple(
        call(solve_third_kernel, [shape(COUNT, CASES, WIDTH)] * 3, [SMEM] + [VMEM] * 15, [pool, gathered])(
            table, got, weights, *maps, *pooled, scale, z0, w0, y0, r1, z1, v1
        )
    )


def solution(mesh):
    three = P(GT, None, None)
    two = P(GT, None)
    return jax.shard_map(
        shards,
        mesh=mesh,
        in_specs=(three, three, three, three, two, two, two),
        out_specs=(three, three, three),
        check_vma=False,
    )
```

```python
import jax
import jax.numpy as jnp
from jax import lax
from jax.experimental import pallas as pl
from jax.experimental.pallas import tpu as pltpu
from jax.sharding import PartitionSpec as P

GT = ("group", "tile")
F32 = jnp.float32
BF16 = jnp.bfloat16
NT = (((1,), (1,)), ((), ()))
VMEM = pl.BlockSpec(memory_space=pltpu.VMEM)
SMEM = pl.BlockSpec(memory_space=pltpu.SMEM)
ANY = pl.BlockSpec(memory_space=pl.ANY)
PARAMS = pltpu.CompilerParams(vmem_limit_bytes=24 << 20)

COUNT, CASES, WIDTH, CORNERS, ROWS, FACES = 8, 8, 384, 8, 64, 12
CHUNKS = WIDTH // 128
TILES = COUNT * CHUNKS
SLOTS = COUNT * CORNERS
CARD = 40
PARTS, PART = 8, 1024


def call(kernel, outs, specs, scratch=(), us=2):
    return pl.pallas_call(
        kernel,
        in_specs=specs,
        out_specs=[VMEM] * len(outs),
        out_shape=outs,
        scratch_shapes=list(scratch),
        compiler_params=PARAMS,
        cost_estimate=pl.CostEstimate(flops=us * 500_000_000, bytes_accessed=us * 3_000_000, transcendentals=0),
    )


def in_hbm(x):
    return pltpu.with_memory_space_constraint(x, pltpu.HBM)


def shape(*dims):
    return jax.ShapeDtypeStruct(dims, F32)


def halves(x):
    high = x.astype(BF16)
    return high, (x - high.astype(F32)).astype(BF16)


def product(vector, matrix):
    vh, vl = halves(vector)
    mh, ml = halves(matrix)
    first = jnp.dot(jnp.concatenate([vh, vl], 0), mh, preferred_element_type=F32)
    return first[:8] + first[8:] + jnp.dot(vh, ml, preferred_element_type=F32)


def lanes(shape_=(8, 128)):
    return lax.broadcasted_iota(jnp.int32, shape_, 1)


def sublanes(shape_=(8, 128)):
    return lax.broadcasted_iota(jnp.int32, shape_, 0)


def put_tiles(ref, p, row):
    for c in range(CHUNKS):
        ref[p * CHUNKS + c] = row[:, c * 128 : (c + 1) * 128]


def get_row(tiles, p):
    return jnp.concatenate([tiles[p * CHUNKS + c] for c in range(CHUNKS)], axis=1)


def jump(pool, table):
    quarter = lanes() // 32
    out = []
    for t in range(TILES):
        p, c = divmod(t, CHUNKS)
        other = None
        for q in range(4):
            f = c * 4 + q
            face = pltpu.roll(pool[table[p, f]], table[8 + p, f], 1)
            other = face if other is None else jnp.where(quarter == q, face, other)
        out.append(pool[TILES + t] - other)
    return out


def fill_pool(pool, a_ref, x_ref, b_ref):
    for e, ref in enumerate((a_ref, x_ref, b_ref)):
        for t in range(TILES):
            pool[e * TILES + t] = ref[t]


def card_kernel(core, inverse_ref, index_ref, partner_ref, card_ref, table_ref):
    inverse = inverse_ref[...]
    block = jnp.concatenate([inverse[:32], inverse[32:]], axis=1)
    card_ref[:, 0:32, :] = jnp.broadcast_to(block[None], (card_ref.shape[0], 32, 128))
    row = index_row(index_ref)
    card_ref[:, 32:40, :] = jnp.broadcast_to(row[None], (card_ref.shape[0], 8, 128))
    partner = partner_ref[...]
    region = (partner >= COUNT * FACES).astype(jnp.int32) + (partner >= 2 * COUNT * FACES).astype(jnp.int32)
    within = partner - region * (COUNT * FACES)
    particle = jnp.zeros_like(within)
    for p in range(1, COUNT):
        particle = particle + (within >= p * FACES).astype(jnp.int32)
    face = within - particle * FACES
    region = jnp.where(core[0] == 1, region, 2 - region)
    table_ref[0:8, 0:FACES] = region * TILES + particle * CHUNKS + (face >> 2)
    table_ref[8:16, 0:FACES] = ((lanes((COUNT, FACES)) - face) & 3) * 32


def index_row(index_ref):
    index = index_ref[...].astype(F32)
    wide = jnp.concatenate([index] * 16, axis=1)
    keep = lanes() // 8 == sublanes()
    return jnp.broadcast_to(jnp.sum(jnp.where(keep, wide, 0.0), axis=0, keepdims=True), (8, 128))


def fetch(source, held, sems, first=0):
    copies = [pltpu.make_async_copy(source.at[i], held.at[i], sems.at[first + i]) for i in range(source.shape[0])]
    for copy in copies:
        copy.start()
    return copies


def multiply(x, copies, held, out_ref):
    for p in range(COUNT):
        copies[p].wait()
        put_tiles(out_ref, p, product(get_row(x, p), held[p]))


def start_kernel(loads_ref, index_ref, inverse_ref, out_ref, held, sems):
    copies = fetch(inverse_ref, held, sems)
    out_ref[TILES] = index_row(index_ref)
    for p in range(COUNT):
        copies[p].wait()
        put_tiles(out_ref, p, product(loads_ref[p], held[p]))


def product_kernel(x_ref, matrix_ref, out_ref, held, sems):
    copies = fetch(matrix_ref, held, sems)
    multiply(x_ref, copies, held, out_ref)


def column_to_row(columns):
    lane, sub = lanes(), sublanes()
    row = jnp.zeros((8, 128), F32)
    for i, column in enumerate(columns):
        row = jnp.where(lane == i * 8 + sub, jnp.broadcast_to(column, (8, 128)), row)
    return jnp.sum(row, axis=0, keepdims=True)


def case_sum(first, second):
    total = first[0] * second[0]
    for t in range(1, TILES):
        total = total + first[t] * second[t]
    return jnp.sum(total, axis=1, keepdims=True)


def send(r, map_ref, columns, pay_ref):
    lane, sub = lanes(), sublanes()
    contrib = jnp.zeros((8, 128), F32)
    for p in range(COUNT):
        for j in range(CORNERS):
            part = r[p * CHUNKS] * map_ref[p, j : j + 1, 0:128]
            for c in range(1, CHUNKS):
                part = part + r[p * CHUNKS + c] * map_ref[p, j : j + 1, c * 128 : (c + 1) * 128]
            total = jnp.sum(part, axis=1, keepdims=True)
            contrib = jnp.where(lane == p * CORNERS + j, jnp.broadcast_to(total, (8, 128)), contrib)
    turned = pltpu.roll(pltpu.roll(contrib, 64, 1), 4, 0)
    pay = jnp.where(lane < 64, contrib, turned)
    if not columns:
        pair = jnp.where(sub < 4, pay, pltpu.roll(pay, 4, 0))
        for at in range(0, pay_ref.shape[0], 8):
            pay_ref[at : at + 8, :] = pair
        return
    pay = jnp.where(sub < 4, pay, jnp.broadcast_to(column_to_row(columns), (8, 128)))[0:5]
    for at in range(0, pay_ref.shape[0], 5):
        pay_ref[at : at + 5, :] = pay


def send_first_kernel(table, a_ref, x_ref, b_ref, map_ref, r_ref, pay_ref, pool):
    fill_pool(pool, a_ref, x_ref, b_ref)
    r = jump(pool, table)
    for t in range(TILES):
        r_ref[t] = r[t]
    send(r, map_ref, [], pay_ref)


def send_second_kernel(table, a_ref, x_ref, b_ref, map_ref, r0_ref, z0_ref, w_ref, pay_ref, pool):
    fill_pool(pool, a_ref, x_ref, b_ref)
    w = jump(pool, table)
    for t in range(TILES):
        w_ref[t] = w[t]
    send(w, map_ref, [case_sum(r0_ref, z0_ref), case_sum(z0_ref, w)], pay_ref)


def send_third_kernel(
    table, a_ref, x_ref, b_ref, map_ref, r1_ref, z1_ref, z0_ref, w0_ref, v_ref, pay_ref, pool
):
    fill_pool(pool, a_ref, x_ref, b_ref)
    v = jump(pool, table)
    for t in range(TILES):
        v_ref[t] = v[t]
    columns = [case_sum(r1_ref, z1_ref), case_sum(z1_ref, v), case_sum(z0_ref, v), case_sum(z1_ref, w0_ref)]
    send(v, map_ref, columns, pay_ref)


def weights_kernel(core, a_ref, x_ref, b_ref, own_ref, other_ref, out_ref, rows, names, index, wanted, built, sems):
    mine = core[0]
    copies = [
        pltpu.make_async_copy(ref.at[TILES], wanted.at[e], sems.at[e]) for e, ref in enumerate((a_ref, x_ref, b_ref))
    ]
    for copy in copies:
        copy.start()
    for copy in copies:
        copy.wait()

    def pick(j, carry):
        row = wanted[j >> 6, 0, j & 63].astype(jnp.int32)
        owner = row >> 6
        at = (owner >> 1) * CARD + (row & 31)
        same = (owner & 1) == mine
        here = own_ref[pl.ds(at, 1), :]
        there = other_ref[pl.ds(at, 1), :]
        rows[pl.ds(j, 1), :] = jnp.where(same, here, there)
        names[pl.ds(j, 1), :] = jnp.full((1, 128), row, jnp.int32)
        return carry

    lax.fori_loop(0, 3 * SLOTS, pick, 0, unroll=16)
    chips = own_ref.shape[0] // CARD
    own = own_ref[pl.ds(32, chips, stride=CARD), :]
    other = other_ref[pl.ds(32, chips, stride=CARD), :]
    first = jnp.where(mine == 0, own, other)
    second = jnp.where(mine == 0, other, own)
    wide = lanes((chips, 128))
    merged = jnp.where(wide < 64, first, pltpu.roll(second, 64, 1)).astype(jnp.int32)
    index[...] = merged
    lane = lanes((3 * SLOTS, 128))
    upper = (names[...] & 63) >= 32
    kept = jnp.where(upper == (lane >= 64), rows[...], 0.0)
    high, low = halves(kept)
    both = jnp.concatenate([high, low], axis=0)
    names[...] = names[...] >> 6
    place = sublanes((128, 256)) & 63

    def spread(q, carry):
        row = jnp.concatenate([index[pl.ds(2 * q, 1), :], index[pl.ds(2 * q + 1, 1), :]], axis=1)
        onehot = (place == (row & 63)).astype(F32).astype(BF16)
        full = jnp.dot(both, onehot, preferred_element_type=F32)
        block = row >> 6
        named = names[...]
        hit = jnp.concatenate([named, named], axis=1) == block
        at = pl.ds(pl.multiple_of((q & 3) * 256, 256), 256)
        built[q >> 2, 0 : 3 * SLOTS, at] = jnp.where(hit, full[: 3 * SLOTS], 0.0).astype(BF16)
        built[q >> 2, 3 * SLOTS :, at] = jnp.where(hit, full[3 * SLOTS :], 0.0).astype(BF16)
        return carry

    copies = []
    for part in range(PARTS):
        lax.fori_loop(part * 4, part * 4 + 4, spread, 0, unroll=4)
        copy = pltpu.make_async_copy(built.at[part], out_ref.at[part], sems.at[3 + part])
        copy.start()
        copies.append(copy)
    for copy in copies:
        copy.wait()


def coarse_into_pool(got_ref, copies, weights, maps, pool, gathered):
    lane, sub = lanes(), sublanes()
    straight = (sub < 4) == (lane < 64)
    sums = None
    senders = PARTS * PART // SLOTS
    rows = got_ref.shape[0] // senders
    if rows == 5:
        sums = jnp.sum(got_ref[pl.ds(4, senders, stride=5), :], axis=0, keepdims=True)
    for q in range(senders // 2):
        at = 2 * q * rows
        if rows == 4:
            pair = got_ref[at : at + 8, :]
        else:
            pair = jnp.concatenate([got_ref[at : at + 4, :], got_ref[at + 5 : at + 9, :]], axis=0)
        tile = jnp.where(straight, pair, pltpu.roll(pltpu.roll(pair, 64, 1), 4, 0))
        high, low = halves(tile)
        gathered[:, q * 128 : (q + 1) * 128] = jnp.concatenate([high, low], axis=0)
    out = None
    for c in range(PARTS):
        copies[c].wait()
        term = lax.dot_general(
            weights[c], gathered[:, c * PART : (c + 1) * PART], NT, preferred_element_type=F32
        )
        out = term if out is None else out + term
    count = 3 * SLOTS
    sol = out[:count] + out[count:]
    sol = sol.T
    sol = sol[:8] + sol[8:]
    own = lax.broadcasted_iota(jnp.int32, (64, 64), 0) // 8 == lax.broadcasted_iota(jnp.int32, (64, 64), 1) // 8
    for e, map_ref in enumerate(maps):
        part = sol[:, e * SLOTS : (e + 1) * SLOTS]
        spread = jnp.where(own, jnp.concatenate([part] * COUNT, axis=0), 0.0)
        sh, sl = halves(spread)
        ch, cl = halves(map_ref[...].reshape(SLOTS, WIDTH))
        two = jnp.dot(jnp.concatenate([sh, sl], axis=0), ch, preferred_element_type=F32)
        full = two[:64] + two[64:] + jnp.dot(sh, cl, preferred_element_type=F32)
        for p in range(COUNT):
            for c in range(CHUNKS):
                t = e * TILES + p * CHUNKS + c
                pool[t] = pool[t] + full[p * 8 : (p + 1) * 8, c * 128 : (c + 1) * 128]
    return sums


def totals(sums, count):
    lane, sub = lanes(), sublanes()
    row = jnp.broadcast_to(sums, (8, 128))
    return [
        jnp.broadcast_to(jnp.sum(jnp.where(lane == i * 8 + sub, row, 0.0), axis=1, keepdims=True), (8, 128))
        for i in range(count)
    ]


def solve_first_kernel(
    table, got_ref, weights_ref, am_ref, m_ref, bm_ref, a_ref, x_ref, b_ref, inverse_ref, z_ref, u_ref,
    pool, gathered, weights, held, sems,
):
    parts = fetch(weights_ref, weights, sems, COUNT)
    copies = fetch(inverse_ref, held, sems)
    fill_pool(pool, a_ref, x_ref, b_ref)
    coarse_into_pool(got_ref, parts, weights, (am_ref, m_ref, bm_ref), pool, gathered)
    z = [0.5 * t for t in jump(pool, table)]
    for t in range(TILES):
        z_ref[t] = z[t]
    multiply(z, copies, held, u_ref)


def solve_second_kernel(
    table, got_ref, weights_ref, am_ref, m_ref, bm_ref, a_ref, x_ref, b_ref, inverse_ref, r0_ref, z0_ref, w0_ref,
    y_ref, r_ref, z_ref, scale_ref, u_ref, pool, gathered, weights, held, sems,
):
    parts = fetch(weights_ref, weights, sems, COUNT)
    copies = fetch(inverse_ref, held, sems)
    fill_pool(pool, a_ref, x_ref, b_ref)
    sums = coarse_into_pool(got_ref, parts, weights, (am_ref, m_ref, bm_ref), pool, gathered)
    energy, curve = totals(sums, 2)
    step = energy / curve
    scale_ref[0] = energy
    scale_ref[1] = curve
    scale_ref[2] = step
    y = jump(pool, table)
    z = []
    for t in range(TILES):
        half = 0.5 * y[t]
        y_ref[t] = half
        r_ref[t] = r0_ref[t] - step * w0_ref[t]
        z.append(z0_ref[t] - step * half)
        z_ref[t] = z[t]
    multiply(z, copies, held, u_ref)


def solve_third_kernel(
    table, got_ref, weights_ref, am_ref, m_ref, bm_ref, a_ref, x_ref, b_ref,
    scale_ref, z0_ref, w0_ref, y0_ref, r1_ref, z1_ref, v1_ref, multipliers_ref, residual_ref, preconditioned_ref,
    pool, gathered, weights, sems,
):
    parts = fetch(weights_ref, weights, sems)
    fill_pool(pool, a_ref, x_ref, b_ref)
    sums = coarse_into_pool(got_ref, parts, weights, (am_ref, m_ref, bm_ref), pool, gathered)
    energy, zv, pv, zw = totals(sums, 4)
    first = scale_ref[2]
    grow = energy / scale_ref[0]
    second = energy / (zv + grow * (pv + zw) + grow * grow * scale_ref[1])
    y = jump(pool, table)
    for p in range(COUNT):
        for c in range(CHUNKS):
            t = p * CHUNKS + c
            at = slice(c * 128, (c + 1) * 128)
            multipliers_ref[p, :, at] = first * z0_ref[t] + second * (z1_ref[t] + grow * z0_ref[t])
            residual_ref[p, :, at] = r1_ref[t] - second * (v1_ref[t] + grow * w0_ref[t])
            preconditioned_ref[p, :, at] = z1_ref[t] - second * (0.5 * y[t] + grow * y0_ref[t])


def shards(loads, local_inverse, schur, corner_map, corner_index, partner, coarse_inverse):
    tiles = lax.axis_size("tile")
    devices = lax.axis_size(GT)
    inner_swap = [(i, i ^ 1) for i in range(tiles)]
    outer_swap = [(i, (i - 1) % tiles if i % 2 == 0 else (i + 1) % tiles) for i in range(tiles)]
    same_core = [[2 * i + c for i in range(devices // 2)] for c in range(2)]
    core = lax.axis_index("tile") % 2

    def both(x):
        return lax.ppermute(x, "tile", inner_swap), lax.ppermute(x, "tile", outer_swap)

    field = shape(TILES, 8, 128)
    pool = pltpu.VMEM((3 * TILES, 8, 128), F32)
    gathered = pltpu.VMEM((16, devices * SLOTS), BF16)
    pay = shape(devices * 5, 128)
    sems = pltpu.SemaphoreType.DMA((COUNT,))

    core = core.astype(jnp.int32).reshape(1)
    card, table = call(
        card_kernel,
        [shape(devices // 2, CARD, 128), jax.ShapeDtypeStruct((16, 128), jnp.int32)],
        [SMEM] + [VMEM] * 3,
        us=1,
    )(core, coarse_inverse, corner_index, partner)
    own_cards = lax.all_to_all(card, GT, 0, 0, tiled=True, axis_index_groups=same_core)
    held = pltpu.VMEM((COUNT, WIDTH, WIDTH), F32)
    solver = pltpu.VMEM((PARTS, 6 * SLOTS, PART), BF16)
    inverse, stiff = in_hbm(local_inverse), in_hbm(schur)
    (u,) = call(start_kernel, [shape(TILES + 1, 8, 128)], [VMEM, VMEM, ANY], [held, sems], us=4)(
        loads, corner_index, inverse
    )
    ua, ub = both(u)
    ma, mb = both(corner_map)
    maps = (ma, corner_map, mb)

    def spread(x):
        return lax.all_to_all(x.reshape(devices, -1), GT, 0, 0, tiled=True).reshape(-1, 128)

    def through(x):
        (q,) = call(product_kernel, [field], [VMEM, ANY], [held, sems], us=3)(x, stiff)
        qa, qb = both(q)
        return qa, q, qb

    r0, parts = call(send_first_kernel, [field, shape(devices * 4, 128)], [SMEM] + [VMEM] * 4, [pool])(
        table, ua, u, ub, corner_map
    )
    own_cards, parts = lax.optimization_barrier((own_cards, parts))
    other_cards = lax.ppermute(own_cards, "tile", inner_swap)
    got = spread(parts)
    pooled = through(r0)
    weights = pl.pallas_call(
        weights_kernel,
        in_specs=[SMEM] + [ANY] * 3 + [VMEM] * 2,
        out_specs=ANY,
        out_shape=pltpu.HBM((PARTS, 6 * SLOTS, PART), BF16),
        scratch_shapes=[
            pltpu.VMEM((3 * SLOTS, 128), F32),
            pltpu.VMEM((3 * SLOTS, 128), jnp.int32),
            pltpu.VMEM((devices // 2, 128), jnp.int32),
            pltpu.SMEM((3, 8, 128), F32),
            solver,
            pltpu.SemaphoreType.DMA((3 + PARTS,)),
        ],
        compiler_params=PARAMS,
        cost_estimate=pl.CostEstimate(flops=2_000_000_000, bytes_accessed=12_000_000, transcendentals=0),
    )(core, ua, u, ub, own_cards.reshape(-1, 128), other_cards.reshape(-1, 128))
    weights = in_hbm(weights)
    solve_sems = pltpu.SemaphoreType.DMA((COUNT + PARTS,))
    solve_scratch = [pool, gathered, solver, held, solve_sems]
    z0, u = call(
        solve_first_kernel, [field] * 2, [SMEM, VMEM, ANY] + [VMEM] * 6 + [ANY], solve_scratch, us=6
    )(table, got, weights, *maps, *pooled, inverse)
    ua, ub = both(u)
    w0, parts = call(send_second_kernel, [field, pay], [SMEM] + [VMEM] * 6, [pool])(
        table, ua, u, ub, corner_map, r0, z0
    )
    got = spread(parts)
    pooled = through(w0)
    y0, r1, z1, scale, u = call(
        solve_second_kernel,
        [field, field, field, shape(3, 8, 128), field],
        [SMEM, VMEM, ANY] + [VMEM] * 6 + [ANY] + [VMEM] * 3,
        solve_scratch,
        us=6,
    )(table, got, weights, *maps, *pooled, inverse, r0, z0, w0)
    ua, ub = both(u)
    v1, parts = call(send_third_kernel, [field, pay], [SMEM] + [VMEM] * 8, [pool])(
        table, ua, u, ub, corner_map, r1, z1, z0, w0
    )
    got = spread(parts)
    pooled = through(v1)
    return tuple(
        call(
            solve_third_kernel,
            [shape(COUNT, CASES, WIDTH)] * 3,
            [SMEM, VMEM, ANY] + [VMEM] * 13,
            [pool, gathered, solver, pltpu.SemaphoreType.DMA((PARTS,))],
            us=5,
        )(table, got, weights, *maps, *pooled, scale, z0, w0, y0, r1, z1, v1)
    )


def solution(mesh):
    three = P(GT, None, None)
    two = P(GT, None)
    return jax.shard_map(
        shards,
        mesh=mesh,
        in_specs=(three, three, three, three, two, two, two),
        out_specs=(three, three, three),
        check_vma=False,
    )
```

```python
import jax
import jax.numpy as jnp
from jax import lax
from jax.experimental import pallas as pl
from jax.experimental.pallas import tpu as pltpu
from jax.sharding import PartitionSpec as P

GT = ("group", "tile")
F32 = jnp.float32
BF16 = jnp.bfloat16
NT = (((1,), (1,)), ((), ()))
VMEM = pl.BlockSpec(memory_space=pltpu.VMEM)
SMEM = pl.BlockSpec(memory_space=pltpu.SMEM)
ANY = pl.BlockSpec(memory_space=pl.ANY)
PARAMS = pltpu.CompilerParams(vmem_limit_bytes=24 << 20)

COUNT, CASES, WIDTH, CORNERS, ROWS, FACES = 8, 8, 384, 8, 64, 12
CHUNKS = WIDTH // 128
TILES = COUNT * CHUNKS
SLOTS = COUNT * CORNERS
CARD = 37
PARTS, PART = 8, 1024


def call(kernel, outs, specs, scratch=(), us=2):
    return pl.pallas_call(
        kernel,
        in_specs=specs,
        out_specs=[VMEM] * len(outs),
        out_shape=outs,
        scratch_shapes=list(scratch),
        compiler_params=PARAMS,
        cost_estimate=pl.CostEstimate(flops=us * 500_000_000, bytes_accessed=us * 3_000_000, transcendentals=0),
    )


def in_hbm(x):
    return pltpu.with_memory_space_constraint(x, pltpu.HBM)


def shape(*dims):
    return jax.ShapeDtypeStruct(dims, F32)


def halves(x):
    high = x.astype(BF16)
    return high, (x - high.astype(F32)).astype(BF16)


def product(vector, matrix):
    vh, vl = halves(vector)
    mh, ml = halves(matrix)
    first = jnp.dot(jnp.concatenate([vh, vl], 0), mh, preferred_element_type=F32)
    return first[:8] + first[8:] + jnp.dot(vh, ml, preferred_element_type=F32)


def lanes(shape_=(8, 128)):
    return lax.broadcasted_iota(jnp.int32, shape_, 1)


def sublanes(shape_=(8, 128)):
    return lax.broadcasted_iota(jnp.int32, shape_, 0)


def put_tiles(ref, p, row):
    for c in range(CHUNKS):
        ref[p * CHUNKS + c] = row[:, c * 128 : (c + 1) * 128]


def get_row(tiles, p):
    return jnp.concatenate([tiles[p * CHUNKS + c] for c in range(CHUNKS)], axis=1)


def jump(pool, table):
    quarter = lanes() // 32
    out = []
    for t in range(TILES):
        p, c = divmod(t, CHUNKS)
        other = None
        for q in range(4):
            f = c * 4 + q
            face = pltpu.roll(pool[table[p, f]], table[8 + p, f], 1)
            other = face if other is None else jnp.where(quarter == q, face, other)
        out.append(pool[TILES + t] - other)
    return out


def fill_pool(pool, a_ref, x_ref, b_ref):
    for e, ref in enumerate((a_ref, x_ref, b_ref)):
        for t in range(TILES):
            pool[e * TILES + t] = ref[t]


def mate_places(core, partner, table_ref):
    region = (partner >= COUNT * FACES).astype(jnp.int32) + (partner >= 2 * COUNT * FACES).astype(jnp.int32)
    within = partner - region * (COUNT * FACES)
    particle = jnp.zeros_like(within)
    for p in range(1, COUNT):
        particle = particle + (within >= p * FACES).astype(jnp.int32)
    face = within - particle * FACES
    region = jnp.where(core[0] == 1, region, 2 - region)
    table_ref[0:8, 0:FACES] = region * TILES + particle * CHUNKS + (face >> 2)
    table_ref[8:16, 0:FACES] = ((lanes((COUNT, FACES)) - face) & 3) * 32


def index_row(index):
    wide = jnp.concatenate([index.astype(F32)] * 16, axis=1)
    keep = lanes() // 8 == sublanes()
    return jnp.broadcast_to(jnp.sum(jnp.where(keep, wide, 0.0), axis=0, keepdims=True), (8, 128))


def copies_of(source, held, sems, first=0):
    return [pltpu.make_async_copy(source.at[i], held.at[i], sems.at[first + i]) for i in range(source.shape[0])]


def fetch(source, held, sems, first=0):
    copies = copies_of(source, held, sems, first)
    for copy in copies:
        copy.start()
    return copies


def multiply(x, copies, held, out_ref):
    for p in range(COUNT):
        copies[p].wait()
        put_tiles(out_ref, p, product(get_row(x, p), held[p]))


def start_kernel(
    core, loads_ref, index_ref, partner_ref, inverse_ref, out_ref, table_ref, loads, index, partner, held, sems
):
    small = [
        pltpu.make_async_copy(source, to, sems.at[COUNT + i])
        for i, (source, to) in enumerate(((loads_ref, loads), (index_ref, index), (partner_ref, partner)))
    ]
    for copy in small:
        copy.start()
    copies = fetch(inverse_ref, held, sems)
    for copy in small:
        copy.wait()
    out_ref[TILES] = index_row(index[...])
    mate_places(core, partner[...], table_ref)
    for p in range(COUNT):
        copies[p].wait()
        put_tiles(out_ref, p, product(loads[p], held[p]))


def product_kernel(x_ref, matrix_ref, out_ref, held, sems):
    copies = fetch(matrix_ref, held, sems)
    multiply(x_ref, copies, held, out_ref)


def column_to_row(columns):
    lane, sub = lanes(), sublanes()
    row = jnp.zeros((8, 128), F32)
    for i, column in enumerate(columns):
        row = jnp.where(lane == i * 8 + sub, jnp.broadcast_to(column, (8, 128)), row)
    return jnp.sum(row, axis=0, keepdims=True)


def case_sum(first, second):
    total = first[0] * second[0]
    for t in range(1, TILES):
        total = total + first[t] * second[t]
    return jnp.sum(total, axis=1, keepdims=True)


def contributions(r, map_ref):
    lane = lanes()
    contrib = jnp.zeros((8, 128), F32)
    for p in range(COUNT):
        for j in range(CORNERS):
            part = r[p * CHUNKS] * map_ref[p, j : j + 1, 0:128]
            for c in range(1, CHUNKS):
                part = part + r[p * CHUNKS + c] * map_ref[p, j : j + 1, c * 128 : (c + 1) * 128]
            total = jnp.sum(part, axis=1, keepdims=True)
            contrib = jnp.where(lane == p * CORNERS + j, jnp.broadcast_to(total, (8, 128)), contrib)
    turned = pltpu.roll(pltpu.roll(contrib, 64, 1), 4, 0)
    return jnp.where(lane < 64, contrib, turned)


def send(r, map_ref, columns, pay_ref):
    pay = contributions(r, map_ref)
    pay = jnp.where(sublanes() < 4, pay, jnp.broadcast_to(column_to_row(columns), (8, 128)))[0:5]
    for at in range(0, pay_ref.shape[0], 5):
        pay_ref[at : at + 5, :] = pay


def send_first_kernel(table, a_ref, x_ref, b_ref, map_ref, inverse_ref, r_ref, card_ref, pool):
    fill_pool(pool, a_ref, x_ref, b_ref)
    r = jump(pool, table)
    for t in range(TILES):
        r_ref[t] = r[t]
    inverse = inverse_ref[...]
    pay = contributions(r, map_ref)
    card = jnp.concatenate([inverse[:32], inverse[32:]], axis=1)
    tail = jnp.where(sublanes() < 1, x_ref[TILES], pltpu.roll(pay, 1, 0))[0:5]
    for at in range(0, card_ref.shape[0], CARD):
        card_ref[at : at + 32, :] = card
        card_ref[at + 32 : at + CARD, :] = tail


def send_second_kernel(table, a_ref, x_ref, b_ref, map_ref, r0_ref, z0_ref, w_ref, pay_ref, pool):
    fill_pool(pool, a_ref, x_ref, b_ref)
    w = jump(pool, table)
    for t in range(TILES):
        w_ref[t] = w[t]
    send(w, map_ref, [case_sum(r0_ref, z0_ref), case_sum(z0_ref, w)], pay_ref)


def send_third_kernel(
    table, a_ref, x_ref, b_ref, map_ref, r1_ref, z1_ref, z0_ref, w0_ref, v_ref, pay_ref, pool
):
    fill_pool(pool, a_ref, x_ref, b_ref)
    v = jump(pool, table)
    for t in range(TILES):
        v_ref[t] = v[t]
    columns = [case_sum(r1_ref, z1_ref), case_sum(z1_ref, v), case_sum(z0_ref, v), case_sum(z1_ref, w0_ref)]
    send(v, map_ref, columns, pay_ref)


def gather_rows(mine, ids, own_ref, other_ref, rows, names):
    def pick(j, carry):
        row = ids[j >> 6, 0, j & 63].astype(jnp.int32)
        owner = row >> 6
        at = (owner >> 1) * CARD + (row & 31)
        same = (owner & 1) == mine
        here = own_ref[pl.ds(at, 1), :]
        there = other_ref[pl.ds(at, 1), :]
        rows[pl.ds(j, 1), :] = jnp.where(same, here, there)
        names[pl.ds(j, 1), :] = jnp.full((1, 128), row, jnp.int32)
        return carry

    lax.fori_loop(0, 3 * SLOTS, pick, 0, unroll=16)


def place(pair, q, gathered):
    straight = (sublanes() < 4) == (lanes() < 64)
    tile = jnp.where(straight, pair, pltpu.roll(pltpu.roll(pair, 64, 1), 4, 0))
    high, low = halves(tile)
    gathered[:, q * 128 : (q + 1) * 128] = jnp.concatenate([high, low], axis=0)


def unpack(got_ref, gathered):
    for q in range(PARTS * PART // 128):
        at = 10 * q
        place(jnp.concatenate([got_ref[at : at + 4, :], got_ref[at + 5 : at + 9, :]], axis=0), q, gathered)
    return jnp.sum(got_ref[pl.ds(4, PARTS * PART // SLOTS, stride=5), :], axis=0, keepdims=True)


def partial_solve(weights, gathered, c):
    return lax.dot_general(weights[c], gathered[:, c * PART : (c + 1) * PART], NT, preferred_element_type=F32)


def into_pool(out, maps, pool):
    count = 3 * SLOTS
    sol = out[:count] + out[count:]
    sol = sol.T
    sol = sol[:8] + sol[8:]
    own = sublanes((64, 64)) // 8 == lanes((64, 64)) // 8
    for e, map_ref in enumerate(maps):
        part = sol[:, e * SLOTS : (e + 1) * SLOTS]
        spread = jnp.where(own, jnp.concatenate([part] * COUNT, axis=0), 0.0)
        sh, sl = halves(spread)
        ch, cl = halves(map_ref[...].reshape(SLOTS, WIDTH))
        two = jnp.dot(jnp.concatenate([sh, sl], axis=0), ch, preferred_element_type=F32)
        full = two[:64] + two[64:] + jnp.dot(sh, cl, preferred_element_type=F32)
        for p in range(COUNT):
            for c in range(CHUNKS):
                t = e * TILES + p * CHUNKS + c
                pool[t] = pool[t] + full[p * 8 : (p + 1) * 8, c * 128 : (c + 1) * 128]


def coarse_into_pool(got_ref, copies, weights, maps, pool, gathered, then=()):
    sums = unpack(got_ref, gathered)
    out = None
    for c in range(PARTS):
        copies[c].wait()
        if then:
            then[c].start()
        term = partial_solve(weights, gathered, c)
        out = term if out is None else out + term
    into_pool(out, maps, pool)
    return sums


def totals(sums, count):
    lane, sub = lanes(), sublanes()
    row = jnp.broadcast_to(sums, (8, 128))
    return [
        jnp.broadcast_to(jnp.sum(jnp.where(lane == i * 8 + sub, row, 0.0), axis=1, keepdims=True), (8, 128))
        for i in range(count)
    ]


def solve_first_kernel(
    core, table, ia_ref, ix_ref, ib_ref, own_ref, other_ref, am_ref, m_ref, bm_ref, a_ref, x_ref, b_ref, inverse_ref,
    z_ref, u_ref, weights_ref, pool, gathered, weights, held, sems, rows, names, index, ids,
):
    mine = core[0]
    small = [
        pltpu.make_async_copy(ref.at[TILES], ids.at[e], sems.at[COUNT + PARTS + e])
        for e, ref in enumerate((ia_ref, ix_ref, ib_ref))
    ]
    for copy in small:
        copy.start()
    copies = fetch(inverse_ref, held, sems)
    for copy in small:
        copy.wait()
    gather_rows(mine, ids, own_ref, other_ref, rows, names)
    fill_pool(pool, a_ref, x_ref, b_ref)
    chips = PARTS * PART // 128
    own = own_ref[pl.ds(32, chips, stride=CARD), :]
    other = other_ref[pl.ds(32, chips, stride=CARD), :]
    first = jnp.where(mine == 0, own, other)
    second = jnp.where(mine == 0, other, own)
    index[...] = jnp.where(lanes((chips, 128)) < 64, first, pltpu.roll(second, 64, 1)).astype(jnp.int32)
    for q in range(chips):
        at = q * CARD + 33
        own, other = own_ref[at : at + 4, :], other_ref[at : at + 4, :]
        first = jnp.where(mine == 0, own, other)
        second = jnp.where(mine == 0, other, own)
        place(jnp.concatenate([first, second], axis=0), q, gathered)
    upper = (names[...] & 63) >= 32
    kept = jnp.where(upper == (lanes((3 * SLOTS, 128)) >= 64), rows[...], 0.0)
    high, low = halves(kept)
    both = jnp.concatenate([high, low], axis=0)
    names[...] = names[...] >> 6
    spot = sublanes((128, 256)) & 63

    def spread(q, carry):
        row = jnp.concatenate([index[pl.ds(2 * q, 1), :], index[pl.ds(2 * q + 1, 1), :]], axis=1)
        onehot = (spot == (row & 63)).astype(F32).astype(BF16)
        full = jnp.dot(both, onehot, preferred_element_type=F32)
        block = row >> 6
        named = names[...]
        hit = jnp.concatenate([named, named], axis=1) == block
        at = pl.ds(pl.multiple_of((q & 3) * 256, 256), 256)
        weights[q >> 2, 0 : 3 * SLOTS, at] = jnp.where(hit, full[: 3 * SLOTS], 0.0).astype(BF16)
        weights[q >> 2, 3 * SLOTS :, at] = jnp.where(hit, full[3 * SLOTS :], 0.0).astype(BF16)
        return carry

    stores = []
    out = None
    for part in range(PARTS):
        lax.fori_loop(part * 4, part * 4 + 4, spread, 0, unroll=4)
        store = pltpu.make_async_copy(weights.at[part], weights_ref.at[part], sems.at[COUNT + part])
        store.start()
        stores.append(store)
        term = partial_solve(weights, gathered, part)
        out = term if out is None else out + term
    into_pool(out, (am_ref, m_ref, bm_ref), pool)
    z = [0.5 * t for t in jump(pool, table)]
    for t in range(TILES):
        z_ref[t] = z[t]
    multiply(z, copies, held, u_ref)
    for store in stores:
        store.wait()


def solve_second_kernel(
    table, got_ref, weights_ref, am_ref, m_ref, bm_ref, a_ref, x_ref, b_ref, inverse_ref, r0_ref, z0_ref, w0_ref,
    y_ref, r_ref, z_ref, scale_ref, u_ref, pool, gathered, weights, held, sems,
):
    parts = fetch(weights_ref, weights, sems, COUNT)
    copies = copies_of(inverse_ref, held, sems)
    fill_pool(pool, a_ref, x_ref, b_ref)
    sums = coarse_into_pool(got_ref, parts, weights, (am_ref, m_ref, bm_ref), pool, gathered, copies)
    energy, curve = totals(sums, 2)
    step = energy / curve
    scale_ref[0] = energy
    scale_ref[1] = curve
    scale_ref[2] = step
    y = jump(pool, table)
    z = []
    for t in range(TILES):
        half = 0.5 * y[t]
        y_ref[t] = half
        r_ref[t] = r0_ref[t] - step * w0_ref[t]
        z.append(z0_ref[t] - step * half)
        z_ref[t] = z[t]
    multiply(z, copies, held, u_ref)


def solve_third_kernel(
    table, got_ref, weights_ref, am_ref, m_ref, bm_ref, a_ref, x_ref, b_ref,
    scale_ref, z0_ref, w0_ref, y0_ref, r1_ref, z1_ref, v1_ref, multipliers_ref, residual_ref, preconditioned_ref,
    pool, gathered, weights, sems,
):
    parts = fetch(weights_ref, weights, sems)
    fill_pool(pool, a_ref, x_ref, b_ref)
    sums = coarse_into_pool(got_ref, parts, weights, (am_ref, m_ref, bm_ref), pool, gathered)
    energy, zv, pv, zw = totals(sums, 4)
    first = scale_ref[2]
    grow = energy / scale_ref[0]
    second = energy / (zv + grow * (pv + zw) + grow * grow * scale_ref[1])
    y = jump(pool, table)
    for p in range(COUNT):
        for c in range(CHUNKS):
            t = p * CHUNKS + c
            at = slice(c * 128, (c + 1) * 128)
            multipliers_ref[p, :, at] = first * z0_ref[t] + second * (z1_ref[t] + grow * z0_ref[t])
            residual_ref[p, :, at] = r1_ref[t] - second * (v1_ref[t] + grow * w0_ref[t])
            preconditioned_ref[p, :, at] = z1_ref[t] - second * (0.5 * y[t] + grow * y0_ref[t])


def shards(loads, local_inverse, schur, corner_map, corner_index, partner, coarse_inverse):
    tiles = lax.axis_size("tile")
    devices = lax.axis_size(GT)
    inner_swap = [(i, i ^ 1) for i in range(tiles)]
    outer_swap = [(i, (i - 1) % tiles if i % 2 == 0 else (i + 1) % tiles) for i in range(tiles)]
    same_core = [[2 * i + c for i in range(devices // 2)] for c in range(2)]
    core = lax.axis_index("tile") % 2

    def both(x):
        return lax.ppermute(x, "tile", inner_swap), lax.ppermute(x, "tile", outer_swap)

    field = shape(TILES, 8, 128)
    pool = pltpu.VMEM((3 * TILES, 8, 128), F32)
    gathered = pltpu.VMEM((16, devices * SLOTS), BF16)
    pay = shape(devices * 5, 128)
    sems = pltpu.SemaphoreType.DMA((COUNT,))

    core = core.astype(jnp.int32).reshape(1)
    held = pltpu.VMEM((COUNT, WIDTH, WIDTH), F32)
    solver = pltpu.VMEM((PARTS, 6 * SLOTS, PART), BF16)
    inverse, stiff = in_hbm(local_inverse), in_hbm(schur)
    u, table = call(
        start_kernel,
        [shape(TILES + 1, 8, 128), jax.ShapeDtypeStruct((16, 128), jnp.int32)],
        [SMEM] + [ANY] * 4,
        [
            pltpu.VMEM((COUNT, CASES, WIDTH), F32),
            pltpu.VMEM((COUNT, CORNERS), jnp.int32),
            pltpu.VMEM((COUNT, FACES), jnp.int32),
            held,
            pltpu.SemaphoreType.DMA((COUNT + 3,)),
        ],
        us=4,
    )(core, in_hbm(loads), in_hbm(corner_index), in_hbm(partner), inverse)
    ua, ub = both(u)
    indices = (ua, u, ub)

    def spread(x):
        return lax.all_to_all(x.reshape(devices, -1), GT, 0, 0, tiled=True).reshape(-1, 128)

    def through(x):
        (q,) = call(product_kernel, [field], [VMEM, ANY], [held, sems], us=3)(x, stiff)
        qa, qb = both(q)
        return qa, q, qb

    r0, card = call(send_first_kernel, [field, shape(devices // 2 * CARD, 128)], [SMEM] + [VMEM] * 5, [pool])(
        table, ua, u, ub, corner_map, coarse_inverse
    )
    own_cards = lax.all_to_all(
        card.reshape(devices // 2, -1), GT, 0, 0, tiled=True, axis_index_groups=same_core
    ).reshape(-1, 128)
    pooled = through(r0)
    ma, mb = both(corner_map)
    maps = (ma, corner_map, mb)
    own_cards, pooled, maps = lax.optimization_barrier((own_cards, pooled, maps))
    other_cards = lax.ppermute(own_cards, "tile", inner_swap)
    z0, u, weights = pl.pallas_call(
        solve_first_kernel,
        in_specs=[SMEM] * 2 + [ANY] * 3 + [VMEM] * 8 + [ANY],
        out_specs=[VMEM, VMEM, ANY],
        out_shape=[field, field, pltpu.HBM((PARTS, 6 * SLOTS, PART), BF16)],
        scratch_shapes=[
            pool,
            gathered,
            solver,
            held,
            pltpu.SemaphoreType.DMA((COUNT + PARTS + 3,)),
            pltpu.VMEM((3 * SLOTS, 128), F32),
            pltpu.VMEM((3 * SLOTS, 128), jnp.int32),
            pltpu.VMEM((devices // 2, 128), jnp.int32),
            pltpu.SMEM((3, 8, 128), F32),
        ],
        compiler_params=PARAMS,
        cost_estimate=pl.CostEstimate(flops=4_000_000_000, bytes_accessed=20_000_000, transcendentals=0),
    )(core, table, *indices, own_cards, other_cards, *maps, *pooled, inverse)
    weights = in_hbm(weights)
    solve_scratch = [pool, gathered, solver, held, pltpu.SemaphoreType.DMA((COUNT + PARTS,))]
    ua, ub = both(u)
    w0, parts = call(send_second_kernel, [field, pay], [SMEM] + [VMEM] * 6, [pool])(
        table, ua, u, ub, corner_map, r0, z0
    )
    got = spread(parts)
    pooled = through(w0)
    y0, r1, z1, scale, u = call(
        solve_second_kernel,
        [field, field, field, shape(3, 8, 128), field],
        [SMEM, VMEM, ANY] + [VMEM] * 6 + [ANY] + [VMEM] * 3,
        solve_scratch,
        us=6,
    )(table, got, weights, *maps, *pooled, inverse, r0, z0, w0)
    ua, ub = both(u)
    v1, parts = call(send_third_kernel, [field, pay], [SMEM] + [VMEM] * 8, [pool])(
        table, ua, u, ub, corner_map, r1, z1, z0, w0
    )
    got = spread(parts)
    pooled = through(v1)
    return tuple(
        call(
            solve_third_kernel,
            [shape(COUNT, CASES, WIDTH)] * 3,
            [SMEM, VMEM, ANY] + [VMEM] * 13,
            [pool, gathered, solver, pltpu.SemaphoreType.DMA((PARTS,))],
            us=5,
        )(table, got, weights, *maps, *pooled, scale, z0, w0, y0, r1, z1, v1)
    )


def solution(mesh):
    three = P(GT, None, None)
    two = P(GT, None)
    return jax.shard_map(
        shards,
        mesh=mesh,
        in_specs=(three, three, three, three, two, two, two),
        out_specs=(three, three, three),
        check_vma=False,
    )
```

```python
import jax
import jax.numpy as jnp
from jax import lax
from jax.experimental import pallas as pl
from jax.experimental.pallas import tpu as pltpu
from jax.sharding import PartitionSpec as P

GT = ("group", "tile")
F32 = jnp.float32
BF16 = jnp.bfloat16
NT = (((1,), (1,)), ((), ()))
VMEM = pl.BlockSpec(memory_space=pltpu.VMEM)
SMEM = pl.BlockSpec(memory_space=pltpu.SMEM)
ANY = pl.BlockSpec(memory_space=pl.ANY)
PARAMS = pltpu.CompilerParams(vmem_limit_bytes=24 << 20)

COUNT, CASES, WIDTH, CORNERS, ROWS, FACES = 8, 8, 384, 8, 64, 12
CHUNKS = WIDTH // 128
TILES = COUNT * CHUNKS
SLOTS = COUNT * CORNERS
CARD = 37
PARTS, PART = 8, 1024


def call(kernel, outs, specs, scratch=(), us=2):
    return pl.pallas_call(
        kernel,
        in_specs=specs,
        out_specs=[VMEM] * len(outs),
        out_shape=outs,
        scratch_shapes=list(scratch),
        compiler_params=PARAMS,
        cost_estimate=pl.CostEstimate(flops=us * 500_000_000, bytes_accessed=us * 3_000_000, transcendentals=0),
    )


def in_hbm(x):
    return pltpu.with_memory_space_constraint(x, pltpu.HBM)


def shape(*dims):
    return jax.ShapeDtypeStruct(dims, F32)


def halves(x):
    high = x.astype(BF16)
    return high, (x - high.astype(F32)).astype(BF16)


def product(vector, matrix):
    vh, vl = halves(vector)
    mh, ml = halves(matrix)
    first = jnp.dot(jnp.concatenate([vh, vl], 0), mh, preferred_element_type=F32)
    return first[:8] + first[8:] + jnp.dot(vh, ml, preferred_element_type=F32)


def lanes(shape_=(8, 128)):
    return lax.broadcasted_iota(jnp.int32, shape_, 1)


def sublanes(shape_=(8, 128)):
    return lax.broadcasted_iota(jnp.int32, shape_, 0)


def put_tiles(ref, p, row):
    for c in range(CHUNKS):
        ref[p * CHUNKS + c] = row[:, c * 128 : (c + 1) * 128]


def get_row(tiles, p):
    return jnp.concatenate([tiles[p * CHUNKS + c] for c in range(CHUNKS)], axis=1)


def jump(pool, table):
    quarter = lanes() // 32
    out = []
    for t in range(TILES):
        p, c = divmod(t, CHUNKS)
        other = None
        for q in range(4):
            f = c * 4 + q
            face = pltpu.roll(pool[table[p, f]], table[8 + p, f], 1)
            other = face if other is None else jnp.where(quarter == q, face, other)
        out.append(pool[TILES + t] - other)
    return out


def fill_pool(pool, a_ref, x_ref, b_ref):
    for e, ref in enumerate((a_ref, x_ref, b_ref)):
        for t in range(TILES):
            pool[e * TILES + t] = ref[t]


def mate_places(core, partner, table_ref):
    region = (partner >= COUNT * FACES).astype(jnp.int32) + (partner >= 2 * COUNT * FACES).astype(jnp.int32)
    within = partner - region * (COUNT * FACES)
    particle = jnp.zeros_like(within)
    for p in range(1, COUNT):
        particle = particle + (within >= p * FACES).astype(jnp.int32)
    face = within - particle * FACES
    region = jnp.where(core[0] == 1, region, 2 - region)
    table_ref[0:8, 0:FACES] = region * TILES + particle * CHUNKS + (face >> 2)
    table_ref[8:16, 0:FACES] = ((lanes((COUNT, FACES)) - face) & 3) * 32


def index_row(index):
    wide = jnp.concatenate([index.astype(F32)] * 16, axis=1)
    keep = lanes() // 8 == sublanes()
    return jnp.broadcast_to(jnp.sum(jnp.where(keep, wide, 0.0), axis=0, keepdims=True), (8, 128))


def copies_of(source, held, sems, first=0):
    return [pltpu.make_async_copy(source.at[i], held.at[i], sems.at[first + i]) for i in range(source.shape[0])]


def fetch(source, held, sems, first=0):
    copies = copies_of(source, held, sems, first)
    for copy in copies:
        copy.start()
    return copies


def multiply(x, copies, held, out_ref):
    for p in range(COUNT):
        copies[p].wait()
        put_tiles(out_ref, p, product(get_row(x, p), held[p]))


def start_kernel(
    core, loads_ref, index_ref, partner_ref, inverse_ref, out_ref, table_ref, loads, index, partner, held, sems
):
    small = [
        pltpu.make_async_copy(source, to, sems.at[COUNT + i])
        for i, (source, to) in enumerate(((loads_ref, loads), (index_ref, index), (partner_ref, partner)))
    ]
    for copy in small:
        copy.start()
    copies = fetch(inverse_ref, held, sems)
    for copy in small:
        copy.wait()
    out_ref[TILES] = index_row(index[...])
    mate_places(core, partner[...], table_ref)
    for p in range(COUNT):
        copies[p].wait()
        put_tiles(out_ref, p, product(loads[p], held[p]))


def product_kernel(x_ref, matrix_ref, out_ref, held, sems):
    copies = fetch(matrix_ref, held, sems)
    multiply(x_ref, copies, held, out_ref)


def column_to_row(columns):
    lane, sub = lanes(), sublanes()
    row = jnp.zeros((8, 128), F32)
    for i, column in enumerate(columns):
        row = jnp.where(lane == i * 8 + sub, jnp.broadcast_to(column, (8, 128)), row)
    return jnp.sum(row, axis=0, keepdims=True)


def case_sum(first, second):
    total = first[0] * second[0]
    for t in range(1, TILES):
        total = total + first[t] * second[t]
    return jnp.sum(total, axis=1, keepdims=True)


def contributions(r, map_ref):
    lane = lanes()
    contrib = jnp.zeros((8, 128), F32)
    for p in range(COUNT):
        for j in range(CORNERS):
            part = r[p * CHUNKS] * map_ref[p, j : j + 1, 0:128]
            for c in range(1, CHUNKS):
                part = part + r[p * CHUNKS + c] * map_ref[p, j : j + 1, c * 128 : (c + 1) * 128]
            total = jnp.sum(part, axis=1, keepdims=True)
            contrib = jnp.where(lane == p * CORNERS + j, jnp.broadcast_to(total, (8, 128)), contrib)
    turned = pltpu.roll(pltpu.roll(contrib, 64, 1), 4, 0)
    return jnp.where(lane < 64, contrib, turned)


def send(r, map_ref, columns, pay_ref):
    pay = contributions(r, map_ref)
    pay = jnp.where(sublanes() < 4, pay, jnp.broadcast_to(column_to_row(columns), (8, 128)))[0:5]
    for at in range(0, pay_ref.shape[0], 5):
        pay_ref[at : at + 5, :] = pay


def send_first_kernel(table, a_ref, x_ref, b_ref, map_ref, inverse_ref, r_ref, card_ref, pool):
    fill_pool(pool, a_ref, x_ref, b_ref)
    r = jump(pool, table)
    for t in range(TILES):
        r_ref[t] = r[t]
    inverse = inverse_ref[...]
    pay = contributions(r, map_ref)
    card = jnp.concatenate([inverse[:32], inverse[32:]], axis=1)
    tail = jnp.where(sublanes() < 1, x_ref[TILES], pltpu.roll(pay, 1, 0))[0:5]
    for at in range(0, card_ref.shape[0], CARD):
        card_ref[at : at + 32, :] = card
        card_ref[at + 32 : at + CARD, :] = tail


def send_second_kernel(table, a_ref, x_ref, b_ref, map_ref, r0_ref, z0_ref, w_ref, pay_ref, pool):
    fill_pool(pool, a_ref, x_ref, b_ref)
    w = jump(pool, table)
    for t in range(TILES):
        w_ref[t] = w[t]
    send(w, map_ref, [case_sum(r0_ref, z0_ref), case_sum(z0_ref, w)], pay_ref)


def send_third_kernel(
    table, a_ref, x_ref, b_ref, map_ref, r1_ref, z1_ref, z0_ref, w0_ref, v_ref, pay_ref, pool
):
    fill_pool(pool, a_ref, x_ref, b_ref)
    v = jump(pool, table)
    for t in range(TILES):
        v_ref[t] = v[t]
    columns = [case_sum(r1_ref, z1_ref), case_sum(z1_ref, v), case_sum(z0_ref, v), case_sum(z1_ref, w0_ref)]
    send(v, map_ref, columns, pay_ref)


def gather_rows(mine, ids, own_ref, other_ref, rows, names):
    def pick(j, carry):
        row = ids[j >> 6, 0, j & 63].astype(jnp.int32)
        owner = row >> 6
        at = (owner >> 1) * CARD + (row & 31)
        same = (owner & 1) == mine
        here = own_ref[pl.ds(at, 1), :]
        there = other_ref[pl.ds(at, 1), :]
        rows[pl.ds(j, 1), :] = jnp.where(same, here, there)
        names[pl.ds(j, 1), :] = jnp.full((1, 128), row, jnp.int32)
        return carry

    lax.fori_loop(0, 3 * SLOTS, pick, 0, unroll=16)


def place(pair, q, gathered):
    straight = (sublanes() < 4) == (lanes() < 64)
    tile = jnp.where(straight, pair, pltpu.roll(pltpu.roll(pair, 64, 1), 4, 0))
    high, low = halves(tile)
    gathered[:, q * 128 : (q + 1) * 128] = jnp.concatenate([high, low], axis=0)


def unpack(got_ref, gathered):
    for q in range(PARTS * PART // 128):
        at = 10 * q
        place(jnp.concatenate([got_ref[at : at + 4, :], got_ref[at + 5 : at + 9, :]], axis=0), q, gathered)
    return jnp.sum(got_ref[pl.ds(4, PARTS * PART // SLOTS, stride=5), :], axis=0, keepdims=True)


def partial_solve(weights, gathered, c):
    return lax.dot_general(weights[c], gathered[:, c * PART : (c + 1) * PART], NT, preferred_element_type=F32)


def into_pool(out, maps, pool):
    count = 3 * SLOTS
    sol = out[:count] + out[count:]
    sol = sol.T
    sol = sol[:8] + sol[8:]
    own = sublanes((64, 64)) // 8 == lanes((64, 64)) // 8
    for e, map_ref in enumerate(maps):
        part = sol[:, e * SLOTS : (e + 1) * SLOTS]
        spread = jnp.where(own, jnp.concatenate([part] * COUNT, axis=0), 0.0)
        sh, sl = halves(spread)
        ch, cl = halves(map_ref[...].reshape(SLOTS, WIDTH))
        two = jnp.dot(jnp.concatenate([sh, sl], axis=0), ch, preferred_element_type=F32)
        full = two[:64] + two[64:] + jnp.dot(sh, cl, preferred_element_type=F32)
        for p in range(COUNT):
            for c in range(CHUNKS):
                t = e * TILES + p * CHUNKS + c
                pool[t] = pool[t] + full[p * 8 : (p + 1) * 8, c * 128 : (c + 1) * 128]


def coarse_into_pool(got_ref, copies, weights, maps, pool, gathered, then=()):
    sums = unpack(got_ref, gathered)
    out = None
    for c in range(PARTS):
        copies[c].wait()
        if then:
            then[c].start()
        term = partial_solve(weights, gathered, c)
        out = term if out is None else out + term
    into_pool(out, maps, pool)
    return sums


def totals(sums, count):
    lane, sub = lanes(), sublanes()
    row = jnp.broadcast_to(sums, (8, 128))
    return [
        jnp.broadcast_to(jnp.sum(jnp.where(lane == i * 8 + sub, row, 0.0), axis=1, keepdims=True), (8, 128))
        for i in range(count)
    ]


def solve_first_kernel(
    core, table, ia_ref, ix_ref, ib_ref, own_ref, other_ref, am_ref, m_ref, bm_ref, a_ref, x_ref, b_ref, inverse_ref,
    z_ref, u_ref, weights_ref, pool, gathered, weights, held, sems, rows, names, index, ids,
):
    mine = core[0]
    small = [
        pltpu.make_async_copy(ref.at[TILES], ids.at[e], sems.at[COUNT + PARTS + e])
        for e, ref in enumerate((ia_ref, ix_ref, ib_ref))
    ]
    for copy in small:
        copy.start()
    copies = fetch(inverse_ref, held, sems)
    for copy in small:
        copy.wait()
    gather_rows(mine, ids, own_ref, other_ref, rows, names)
    fill_pool(pool, a_ref, x_ref, b_ref)
    chips = PARTS * PART // 128
    own = own_ref[pl.ds(32, chips, stride=CARD), :]
    other = other_ref[pl.ds(32, chips, stride=CARD), :]
    first = jnp.where(mine == 0, own, other)
    second = jnp.where(mine == 0, other, own)
    index[...] = jnp.where(lanes((chips, 128)) < 64, first, pltpu.roll(second, 64, 1)).astype(jnp.int32)
    for q in range(chips):
        at = q * CARD + 33
        own, other = own_ref[at : at + 4, :], other_ref[at : at + 4, :]
        first = jnp.where(mine == 0, own, other)
        second = jnp.where(mine == 0, other, own)
        place(jnp.concatenate([first, second], axis=0), q, gathered)
    upper = (names[...] & 63) >= 32
    kept = jnp.where(upper == (lanes((3 * SLOTS, 128)) >= 64), rows[...], 0.0)
    high, low = halves(kept)
    both = jnp.concatenate([high, low], axis=0)
    names[...] = names[...] >> 6
    spot = sublanes((128, 256)) & 63

    def spread(q, carry):
        row = jnp.concatenate([index[pl.ds(2 * q, 1), :], index[pl.ds(2 * q + 1, 1), :]], axis=1)
        onehot = (spot == (row & 63)).astype(F32).astype(BF16)
        full = jnp.dot(both, onehot, preferred_element_type=F32)
        block = row >> 6
        named = names[...]
        hit = jnp.concatenate([named, named], axis=1) == block
        at = pl.ds(pl.multiple_of((q & 3) * 256, 256), 256)
        weights[q >> 2, 0 : 3 * SLOTS, at] = jnp.where(hit, full[: 3 * SLOTS], 0.0).astype(BF16)
        weights[q >> 2, 3 * SLOTS :, at] = jnp.where(hit, full[3 * SLOTS :], 0.0).astype(BF16)
        return carry

    stores = []
    out = None
    for part in range(PARTS):
        lax.fori_loop(part * 4, part * 4 + 4, spread, 0, unroll=4)
        store = pltpu.make_async_copy(weights.at[part], weights_ref.at[part], sems.at[COUNT + part])
        store.start()
        stores.append(store)
        term = partial_solve(weights, gathered, part)
        out = term if out is None else out + term
    into_pool(out, (am_ref, m_ref, bm_ref), pool)
    z = [0.5 * t for t in jump(pool, table)]
    for t in range(TILES):
        z_ref[t] = z[t]
    multiply(z, copies, held, u_ref)
    for store in stores:
        store.wait()


def solve_second_kernel(
    table, got_ref, weights_ref, am_ref, m_ref, bm_ref, a_ref, x_ref, b_ref, inverse_ref, r0_ref, z0_ref, w0_ref,
    y_ref, r_ref, z_ref, scale_ref, u_ref, pool, gathered, weights, held, sems,
):
    parts = fetch(weights_ref, weights, sems, COUNT)
    copies = copies_of(inverse_ref, held, sems)
    fill_pool(pool, a_ref, x_ref, b_ref)
    sums = coarse_into_pool(got_ref, parts, weights, (am_ref, m_ref, bm_ref), pool, gathered, copies)
    energy, curve = totals(sums, 2)
    step = energy / curve
    scale_ref[0] = energy
    scale_ref[1] = curve
    scale_ref[2] = step
    y = jump(pool, table)
    z = []
    for t in range(TILES):
        half = 0.5 * y[t]
        y_ref[t] = half
        r_ref[t] = r0_ref[t] - step * w0_ref[t]
        z.append(z0_ref[t] - step * half)
        z_ref[t] = z[t]
    multiply(z, copies, held, u_ref)


def solve_third_kernel(
    table, got_ref, weights_ref, am_ref, m_ref, bm_ref, a_ref, x_ref, b_ref,
    scale_ref, z0_ref, w0_ref, y0_ref, r1_ref, z1_ref, v1_ref, multipliers_ref, residual_ref, preconditioned_ref,
    pool, gathered, weights, sems,
):
    parts = fetch(weights_ref, weights, sems)
    fill_pool(pool, a_ref, x_ref, b_ref)
    sums = coarse_into_pool(got_ref, parts, weights, (am_ref, m_ref, bm_ref), pool, gathered)
    energy, zv, pv, zw = totals(sums, 4)
    first = scale_ref[2]
    grow = energy / scale_ref[0]
    second = energy / (zv + grow * (pv + zw) + grow * grow * scale_ref[1])
    y = jump(pool, table)
    for p in range(COUNT):
        for c in range(CHUNKS):
            t = p * CHUNKS + c
            at = slice(c * 128, (c + 1) * 128)
            multipliers_ref[p, :, at] = first * z0_ref[t] + second * (z1_ref[t] + grow * z0_ref[t])
            residual_ref[p, :, at] = r1_ref[t] - second * (v1_ref[t] + grow * w0_ref[t])
            preconditioned_ref[p, :, at] = z1_ref[t] - second * (0.5 * y[t] + grow * y0_ref[t])


def shards(loads, local_inverse, schur, corner_map, corner_index, partner, coarse_inverse):
    tiles = lax.axis_size("tile")
    devices = lax.axis_size(GT)
    inner_swap = [(i, i ^ 1) for i in range(tiles)]
    outer_swap = [(i, (i - 1) % tiles if i % 2 == 0 else (i + 1) % tiles) for i in range(tiles)]
    same_core = [[2 * i + c for i in range(devices // 2)] for c in range(2)]
    core = lax.axis_index("tile") % 2

    def both(x):
        return lax.ppermute(x, "tile", inner_swap), lax.ppermute(x, "tile", outer_swap)

    field = shape(TILES, 8, 128)
    pool = pltpu.VMEM((3 * TILES, 8, 128), F32)
    gathered = pltpu.VMEM((16, devices * SLOTS), BF16)
    pay = shape(devices * 5, 128)
    sems = pltpu.SemaphoreType.DMA((COUNT,))

    core = core.astype(jnp.int32).reshape(1)
    held = pltpu.VMEM((COUNT, WIDTH, WIDTH), F32)
    solver = pltpu.VMEM((PARTS, 6 * SLOTS, PART), BF16)
    inverse, stiff = in_hbm(local_inverse), in_hbm(schur)
    u, table = call(
        start_kernel,
        [shape(TILES + 1, 8, 128), jax.ShapeDtypeStruct((16, 128), jnp.int32)],
        [SMEM] + [ANY] * 4,
        [
            pltpu.VMEM((COUNT, CASES, WIDTH), F32),
            pltpu.VMEM((COUNT, CORNERS), jnp.int32),
            pltpu.VMEM((COUNT, FACES), jnp.int32),
            held,
            pltpu.SemaphoreType.DMA((COUNT + 3,)),
        ],
        us=4,
    )(core, in_hbm(loads), in_hbm(corner_index), in_hbm(partner), inverse)
    ma, mb = both(corner_map)
    maps = (ma, corner_map, mb)
    ua, ub = both(u)
    maps, ua, ub = lax.optimization_barrier((maps, ua, ub))
    indices = (ua, u, ub)

    def spread(x):
        return lax.all_to_all(x.reshape(devices, -1), GT, 0, 0, tiled=True).reshape(-1, 128)

    def through(x):
        (q,) = call(product_kernel, [field], [VMEM, ANY], [held, sems], us=3)(x, stiff)
        qa, qb = both(q)
        return qa, q, qb

    r0, card = call(send_first_kernel, [field, shape(devices // 2 * CARD, 128)], [SMEM] + [VMEM] * 5, [pool])(
        table, ua, u, ub, corner_map, coarse_inverse
    )
    own_cards = lax.all_to_all(
        card.reshape(devices // 2, -1), GT, 0, 0, tiled=True, axis_index_groups=same_core
    ).reshape(-1, 128)
    pooled = through(r0)
    own_cards, pooled = lax.optimization_barrier((own_cards, pooled))
    other_cards = lax.ppermute(own_cards, "tile", inner_swap)
    z0, u, weights = pl.pallas_call(
        solve_first_kernel,
        in_specs=[SMEM] * 2 + [ANY] * 3 + [VMEM] * 8 + [ANY],
        out_specs=[VMEM, VMEM, ANY],
        out_shape=[field, field, pltpu.HBM((PARTS, 6 * SLOTS, PART), BF16)],
        scratch_shapes=[
            pool,
            gathered,
            solver,
            held,
            pltpu.SemaphoreType.DMA((COUNT + PARTS + 3,)),
            pltpu.VMEM((3 * SLOTS, 128), F32),
            pltpu.VMEM((3 * SLOTS, 128), jnp.int32),
            pltpu.VMEM((devices // 2, 128), jnp.int32),
            pltpu.SMEM((3, 8, 128), F32),
        ],
        compiler_params=PARAMS,
        cost_estimate=pl.CostEstimate(flops=4_000_000_000, bytes_accessed=20_000_000, transcendentals=0),
    )(core, table, *indices, own_cards, other_cards, *maps, *pooled, inverse)
    weights = in_hbm(weights)
    solve_scratch = [pool, gathered, solver, held, pltpu.SemaphoreType.DMA((COUNT + PARTS,))]
    ua, ub = both(u)
    w0, parts = call(send_second_kernel, [field, pay], [SMEM] + [VMEM] * 6, [pool])(
        table, ua, u, ub, corner_map, r0, z0
    )
    got = spread(parts)
    pooled = through(w0)
    y0, r1, z1, scale, u = call(
        solve_second_kernel,
        [field, field, field, shape(3, 8, 128), field],
        [SMEM, VMEM, ANY] + [VMEM] * 6 + [ANY] + [VMEM] * 3,
        solve_scratch,
        us=6,
    )(table, got, weights, *maps, *pooled, inverse, r0, z0, w0)
    ua, ub = both(u)
    v1, parts = call(send_third_kernel, [field, pay], [SMEM] + [VMEM] * 8, [pool])(
        table, ua, u, ub, corner_map, r1, z1, z0, w0
    )
    got = spread(parts)
    pooled = through(v1)
    return tuple(
        call(
            solve_third_kernel,
            [shape(COUNT, CASES, WIDTH)] * 3,
            [SMEM, VMEM, ANY] + [VMEM] * 13,
            [pool, gathered, solver, pltpu.SemaphoreType.DMA((PARTS,))],
            us=5,
        )(table, got, weights, *maps, *pooled, scale, z0, w0, y0, r1, z1, v1)
    )


def solution(mesh):
    three = P(GT, None, None)
    two = P(GT, None)
    return jax.shard_map(
        shards,
        mesh=mesh,
        in_specs=(three, three, three, three, two, two, two),
        out_specs=(three, three, three),
        check_vma=False,
    )
```

```python
import jax
import jax.numpy as jnp
from jax import lax
from jax.experimental import pallas as pl
from jax.experimental.pallas import tpu as pltpu
from jax.sharding import PartitionSpec as P

GT = ("group", "tile")
F32 = jnp.float32
BF16 = jnp.bfloat16
NT = (((1,), (1,)), ((), ()))
VMEM = pl.BlockSpec(memory_space=pltpu.VMEM)
SMEM = pl.BlockSpec(memory_space=pltpu.SMEM)
ANY = pl.BlockSpec(memory_space=pl.ANY)
PARAMS = pltpu.CompilerParams(vmem_limit_bytes=24 << 20)

COUNT, CASES, WIDTH, CORNERS, ROWS, FACES = 8, 8, 384, 8, 64, 12
CHUNKS = WIDTH // 128
TILES = COUNT * CHUNKS
SLOTS = COUNT * CORNERS
CARD = 37
PARTS, PART = 8, 1024


def call(kernel, outs, specs, scratch=(), us=2):
    return pl.pallas_call(
        kernel,
        in_specs=specs,
        out_specs=[VMEM] * len(outs),
        out_shape=outs,
        scratch_shapes=list(scratch),
        compiler_params=PARAMS,
        cost_estimate=pl.CostEstimate(flops=us * 500_000_000, bytes_accessed=us * 3_000_000, transcendentals=0),
    )


def in_hbm(x):
    return pltpu.with_memory_space_constraint(x, pltpu.HBM)


def shape(*dims):
    return jax.ShapeDtypeStruct(dims, F32)


def halves(x):
    high = x.astype(BF16)
    return high, (x - high.astype(F32)).astype(BF16)


def product(vector, matrix):
    vh, vl = halves(vector)
    mh, ml = halves(matrix)
    first = jnp.dot(jnp.concatenate([vh, vl], 0), mh, preferred_element_type=F32)
    return first[:8] + first[8:] + jnp.dot(vh, ml, preferred_element_type=F32)


def lanes(shape_=(8, 128)):
    return lax.broadcasted_iota(jnp.int32, shape_, 1)


def sublanes(shape_=(8, 128)):
    return lax.broadcasted_iota(jnp.int32, shape_, 0)


def put_tiles(ref, p, row):
    for c in range(CHUNKS):
        ref[p * CHUNKS + c] = row[:, c * 128 : (c + 1) * 128]


def get_row(tiles, p):
    return jnp.concatenate([tiles[p * CHUNKS + c] for c in range(CHUNKS)], axis=1)


def jump(pool, table):
    quarter = lanes() // 32
    out = []
    for t in range(TILES):
        p, c = divmod(t, CHUNKS)
        other = None
        for q in range(4):
            f = c * 4 + q
            face = pltpu.roll(pool[table[p, f]], table[8 + p, f], 1)
            other = face if other is None else jnp.where(quarter == q, face, other)
        out.append(pool[TILES + t] - other)
    return out


def fill_pool(pool, a_ref, x_ref, b_ref):
    for e, ref in enumerate((a_ref, x_ref, b_ref)):
        for t in range(TILES):
            pool[e * TILES + t] = ref[t]


def mate_places(core, partner, table_ref):
    region = (partner >= COUNT * FACES).astype(jnp.int32) + (partner >= 2 * COUNT * FACES).astype(jnp.int32)
    within = partner - region * (COUNT * FACES)
    particle = jnp.zeros_like(within)
    for p in range(1, COUNT):
        particle = particle + (within >= p * FACES).astype(jnp.int32)
    face = within - particle * FACES
    region = jnp.where(core[0] == 1, region, 2 - region)
    table_ref[0:8, 0:FACES] = region * TILES + particle * CHUNKS + (face >> 2)
    table_ref[8:16, 0:FACES] = ((lanes((COUNT, FACES)) - face) & 3) * 32


def index_row(index):
    wide = jnp.concatenate([index.astype(F32)] * 16, axis=1)
    keep = lanes() // 8 == sublanes()
    return jnp.broadcast_to(jnp.sum(jnp.where(keep, wide, 0.0), axis=0, keepdims=True), (8, 128))


def copies_of(source, held, sems, first=0):
    return [pltpu.make_async_copy(source.at[i], held.at[i], sems.at[first + i]) for i in range(source.shape[0])]


def fetch(source, held, sems, first=0):
    copies = copies_of(source, held, sems, first)
    for copy in copies:
        copy.start()
    return copies


def multiply(x, copies, held, out_ref):
    for p in range(COUNT):
        copies[p].wait()
        put_tiles(out_ref, p, product(get_row(x, p), held[p]))


def start_kernel(
    core, loads_ref, index_ref, partner_ref, inverse_ref, out_ref, table_ref, loads, index, partner, held, sems
):
    small = [
        pltpu.make_async_copy(source, to, sems.at[COUNT + i])
        for i, (source, to) in enumerate(((loads_ref, loads), (index_ref, index), (partner_ref, partner)))
    ]
    for copy in small:
        copy.start()
    copies = fetch(inverse_ref, held, sems)
    for copy in small:
        copy.wait()
    out_ref[TILES] = index_row(index[...])
    mate_places(core, partner[...], table_ref)
    for p in range(COUNT):
        copies[p].wait()
        put_tiles(out_ref, p, product(loads[p], held[p]))


def product_kernel(x_ref, matrix_ref, out_ref, held, sems):
    copies = fetch(matrix_ref, held, sems)
    multiply(x_ref, copies, held, out_ref)


def column_to_row(columns):
    lane, sub = lanes(), sublanes()
    row = jnp.zeros((8, 128), F32)
    for i, column in enumerate(columns):
        row = jnp.where(lane == i * 8 + sub, jnp.broadcast_to(column, (8, 128)), row)
    return jnp.sum(row, axis=0, keepdims=True)


def case_sum(first, second):
    total = first[0] * second[0]
    for t in range(1, TILES):
        total = total + first[t] * second[t]
    return jnp.sum(total, axis=1, keepdims=True)


def contributions(r, map_ref):
    lane = lanes()
    contrib = jnp.zeros((8, 128), F32)
    for p in range(COUNT):
        for j in range(CORNERS):
            part = r[p * CHUNKS] * map_ref[p, j : j + 1, 0:128]
            for c in range(1, CHUNKS):
                part = part + r[p * CHUNKS + c] * map_ref[p, j : j + 1, c * 128 : (c + 1) * 128]
            total = jnp.sum(part, axis=1, keepdims=True)
            contrib = jnp.where(lane == p * CORNERS + j, jnp.broadcast_to(total, (8, 128)), contrib)
    turned = pltpu.roll(pltpu.roll(contrib, 64, 1), 4, 0)
    return jnp.where(lane < 64, contrib, turned)


def send(r, map_ref, columns, pay_ref):
    pay = contributions(r, map_ref)
    pay = jnp.where(sublanes() < 4, pay, jnp.broadcast_to(column_to_row(columns), (8, 128)))[0:5]
    for at in range(0, pay_ref.shape[0], 5):
        pay_ref[at : at + 5, :] = pay


def send_first_kernel(table, a_ref, x_ref, b_ref, map_ref, inverse_ref, r_ref, card_ref, pool):
    fill_pool(pool, a_ref, x_ref, b_ref)
    r = jump(pool, table)
    for t in range(TILES):
        r_ref[t] = r[t]
    inverse = inverse_ref[...]
    pay = contributions(r, map_ref)
    card = jnp.concatenate([inverse[:32], inverse[32:]], axis=1)
    tail = jnp.where(sublanes() < 1, x_ref[TILES], pltpu.roll(pay, 1, 0))[0:5]
    for at in range(0, card_ref.shape[0], CARD):
        card_ref[at : at + 32, :] = card
        card_ref[at + 32 : at + CARD, :] = tail


def multiply_held(x, matrix_ref, out_ref):
    for p in range(COUNT):
        put_tiles(out_ref, p, product(get_row(x, p), matrix_ref[p]))


def send_second_kernel(table, a_ref, x_ref, b_ref, map_ref, schur_ref, r0_ref, z0_ref, w_ref, pay_ref, q_ref, pool):
    fill_pool(pool, a_ref, x_ref, b_ref)
    w = jump(pool, table)
    for t in range(TILES):
        w_ref[t] = w[t]
    send(w, map_ref, [case_sum(r0_ref, z0_ref), case_sum(z0_ref, w)], pay_ref)
    multiply_held(w, schur_ref, q_ref)


def send_third_kernel(
    table, a_ref, x_ref, b_ref, map_ref, schur_ref, r1_ref, z1_ref, z0_ref, w0_ref, v_ref, pay_ref, q_ref, pool
):
    fill_pool(pool, a_ref, x_ref, b_ref)
    v = jump(pool, table)
    for t in range(TILES):
        v_ref[t] = v[t]
    columns = [case_sum(r1_ref, z1_ref), case_sum(z1_ref, v), case_sum(z0_ref, v), case_sum(z1_ref, w0_ref)]
    send(v, map_ref, columns, pay_ref)
    multiply_held(v, schur_ref, q_ref)


def gather_rows(mine, ids, own_ref, other_ref, rows, names):
    def pick(j, carry):
        row = ids[j >> 6, 0, j & 63].astype(jnp.int32)
        owner = row >> 6
        at = (owner >> 1) * CARD + (row & 31)
        same = (owner & 1) == mine
        here = own_ref[pl.ds(at, 1), :]
        there = other_ref[pl.ds(at, 1), :]
        rows[pl.ds(j, 1), :] = jnp.where(same, here, there)
        names[pl.ds(j, 1), :] = jnp.full((1, 128), row, jnp.int32)
        return carry

    lax.fori_loop(0, 3 * SLOTS, pick, 0, unroll=16)


def place(pair, q, gathered):
    straight = (sublanes() < 4) == (lanes() < 64)
    tile = jnp.where(straight, pair, pltpu.roll(pltpu.roll(pair, 64, 1), 4, 0))
    high, low = halves(tile)
    gathered[:, q * 128 : (q + 1) * 128] = jnp.concatenate([high, low], axis=0)


def unpack(got_ref, gathered):
    for q in range(PARTS * PART // 128):
        at = 10 * q
        place(jnp.concatenate([got_ref[at : at + 4, :], got_ref[at + 5 : at + 9, :]], axis=0), q, gathered)
    return jnp.sum(got_ref[pl.ds(4, PARTS * PART // SLOTS, stride=5), :], axis=0, keepdims=True)


def partial_solve(weights, gathered, c):
    return lax.dot_general(weights[c], gathered[:, c * PART : (c + 1) * PART], NT, preferred_element_type=F32)


def into_pool(out, maps, pool):
    count = 3 * SLOTS
    sol = out[:count] + out[count:]
    sol = sol.T
    sol = sol[:8] + sol[8:]
    own = sublanes((64, 64)) // 8 == lanes((64, 64)) // 8
    for e, map_ref in enumerate(maps):
        part = sol[:, e * SLOTS : (e + 1) * SLOTS]
        spread = jnp.where(own, jnp.concatenate([part] * COUNT, axis=0), 0.0)
        sh, sl = halves(spread)
        ch, cl = halves(map_ref[...].reshape(SLOTS, WIDTH))
        two = jnp.dot(jnp.concatenate([sh, sl], axis=0), ch, preferred_element_type=F32)
        full = two[:64] + two[64:] + jnp.dot(sh, cl, preferred_element_type=F32)
        for p in range(COUNT):
            for c in range(CHUNKS):
                t = e * TILES + p * CHUNKS + c
                pool[t] = pool[t] + full[p * 8 : (p + 1) * 8, c * 128 : (c + 1) * 128]


def coarse_kernel(got_ref, weights_ref, out_ref, sums_ref, gathered, weights, sems):
    copies = fetch(weights_ref, weights, sems)
    sums_ref[...] = jnp.broadcast_to(unpack(got_ref, gathered), (8, 128))
    out = None
    for c in range(PARTS):
        copies[c].wait()
        term = partial_solve(weights, gathered, c)
        out = term if out is None else out + term
    out_ref[...] = out


def totals(sums, count):
    lane, sub = lanes(), sublanes()
    row = jnp.broadcast_to(sums, (8, 128))
    return [
        jnp.broadcast_to(jnp.sum(jnp.where(lane == i * 8 + sub, row, 0.0), axis=1, keepdims=True), (8, 128))
        for i in range(count)
    ]


def solve_first_kernel(
    core, table, ia_ref, ix_ref, ib_ref, own_ref, other_ref, am_ref, m_ref, bm_ref, a_ref, x_ref, b_ref, inverse_ref,
    z_ref, u_ref, weights_ref, pool, gathered, weights, held, sems, rows, names, index, ids,
):
    mine = core[0]
    small = [
        pltpu.make_async_copy(ref.at[TILES], ids.at[e], sems.at[COUNT + PARTS + e])
        for e, ref in enumerate((ia_ref, ix_ref, ib_ref))
    ]
    for copy in small:
        copy.start()
    copies = fetch(inverse_ref, held, sems)
    for copy in small:
        copy.wait()
    gather_rows(mine, ids, own_ref, other_ref, rows, names)
    fill_pool(pool, a_ref, x_ref, b_ref)
    chips = PARTS * PART // 128
    own = own_ref[pl.ds(32, chips, stride=CARD), :]
    other = other_ref[pl.ds(32, chips, stride=CARD), :]
    first = jnp.where(mine == 0, own, other)
    second = jnp.where(mine == 0, other, own)
    index[...] = jnp.where(lanes((chips, 128)) < 64, first, pltpu.roll(second, 64, 1)).astype(jnp.int32)
    for q in range(chips):
        at = q * CARD + 33
        own, other = own_ref[at : at + 4, :], other_ref[at : at + 4, :]
        first = jnp.where(mine == 0, own, other)
        second = jnp.where(mine == 0, other, own)
        place(jnp.concatenate([first, second], axis=0), q, gathered)
    upper = (names[...] & 63) >= 32
    kept = jnp.where(upper == (lanes((3 * SLOTS, 128)) >= 64), rows[...], 0.0)
    high, low = halves(kept)
    both = jnp.concatenate([high, low], axis=0)
    names[...] = names[...] >> 6
    spot = sublanes((128, 256)) & 63

    def spread(q, carry):
        row = jnp.concatenate([index[pl.ds(2 * q, 1), :], index[pl.ds(2 * q + 1, 1), :]], axis=1)
        onehot = (spot == (row & 63)).astype(F32).astype(BF16)
        full = jnp.dot(both, onehot, preferred_element_type=F32)
        block = row >> 6
        named = names[...]
        hit = jnp.concatenate([named, named], axis=1) == block
        at = pl.ds(pl.multiple_of((q & 3) * 256, 256), 256)
        weights[q >> 2, 0 : 3 * SLOTS, at] = jnp.where(hit, full[: 3 * SLOTS], 0.0).astype(BF16)
        weights[q >> 2, 3 * SLOTS :, at] = jnp.where(hit, full[3 * SLOTS :], 0.0).astype(BF16)
        return carry

    stores = []
    out = None
    for part in range(PARTS):
        lax.fori_loop(part * 4, part * 4 + 4, spread, 0, unroll=4)
        store = pltpu.make_async_copy(weights.at[part], weights_ref.at[part], sems.at[COUNT + part])
        store.start()
        stores.append(store)
        term = partial_solve(weights, gathered, part)
        out = term if out is None else out + term
    into_pool(out, (am_ref, m_ref, bm_ref), pool)
    z = [0.5 * t for t in jump(pool, table)]
    for t in range(TILES):
        z_ref[t] = z[t]
    multiply(z, copies, held, u_ref)
    for store in stores:
        store.wait()


def solve_second_kernel(
    table, out_ref, sums_ref, am_ref, m_ref, bm_ref, a_ref, x_ref, b_ref, inverse_ref, r0_ref, z0_ref, w0_ref,
    y_ref, r_ref, z_ref, scale_ref, u_ref, pool,
):
    fill_pool(pool, a_ref, x_ref, b_ref)
    into_pool(out_ref[...], (am_ref, m_ref, bm_ref), pool)
    energy, curve = totals(sums_ref[0:1, :], 2)
    step = energy / curve
    scale_ref[0] = energy
    scale_ref[1] = curve
    scale_ref[2] = step
    y = jump(pool, table)
    z = []
    for t in range(TILES):
        half = 0.5 * y[t]
        y_ref[t] = half
        r_ref[t] = r0_ref[t] - step * w0_ref[t]
        z.append(z0_ref[t] - step * half)
        z_ref[t] = z[t]
    multiply_held(z, inverse_ref, u_ref)


def solve_third_kernel(
    table, out_ref, sums_ref, am_ref, m_ref, bm_ref, a_ref, x_ref, b_ref,
    scale_ref, z0_ref, w0_ref, y0_ref, r1_ref, z1_ref, v1_ref, multipliers_ref, residual_ref, preconditioned_ref,
    pool,
):
    fill_pool(pool, a_ref, x_ref, b_ref)
    into_pool(out_ref[...], (am_ref, m_ref, bm_ref), pool)
    energy, zv, pv, zw = totals(sums_ref[0:1, :], 4)
    first = scale_ref[2]
    grow = energy / scale_ref[0]
    second = energy / (zv + grow * (pv + zw) + grow * grow * scale_ref[1])
    y = jump(pool, table)
    for p in range(COUNT):
        for c in range(CHUNKS):
            t = p * CHUNKS + c
            at = slice(c * 128, (c + 1) * 128)
            multipliers_ref[p, :, at] = first * z0_ref[t] + second * (z1_ref[t] + grow * z0_ref[t])
            residual_ref[p, :, at] = r1_ref[t] - second * (v1_ref[t] + grow * w0_ref[t])
            preconditioned_ref[p, :, at] = z1_ref[t] - second * (0.5 * y[t] + grow * y0_ref[t])


def shards(loads, local_inverse, schur, corner_map, corner_index, partner, coarse_inverse):
    tiles = lax.axis_size("tile")
    devices = lax.axis_size(GT)
    inner_swap = [(i, i ^ 1) for i in range(tiles)]
    outer_swap = [(i, (i - 1) % tiles if i % 2 == 0 else (i + 1) % tiles) for i in range(tiles)]
    same_core = [[2 * i + c for i in range(devices // 2)] for c in range(2)]
    core = lax.axis_index("tile") % 2

    def both(x):
        return lax.ppermute(x, "tile", inner_swap), lax.ppermute(x, "tile", outer_swap)

    field = shape(TILES, 8, 128)
    pool = pltpu.VMEM((3 * TILES, 8, 128), F32)
    gathered = pltpu.VMEM((16, devices * SLOTS), BF16)
    pay = shape(devices * 5, 128)
    sems = pltpu.SemaphoreType.DMA((COUNT,))

    core = core.astype(jnp.int32).reshape(1)
    held = pltpu.VMEM((COUNT, WIDTH, WIDTH), F32)
    solver = pltpu.VMEM((PARTS, 6 * SLOTS, PART), BF16)
    inverse, stiff = in_hbm(local_inverse), in_hbm(schur)
    u, table = call(
        start_kernel,
        [shape(TILES + 1, 8, 128), jax.ShapeDtypeStruct((16, 128), jnp.int32)],
        [SMEM] + [ANY] * 4,
        [
            pltpu.VMEM((COUNT, CASES, WIDTH), F32),
            pltpu.VMEM((COUNT, CORNERS), jnp.int32),
            pltpu.VMEM((COUNT, FACES), jnp.int32),
            held,
            pltpu.SemaphoreType.DMA((COUNT + 3,)),
        ],
        us=4,
    )(core, in_hbm(loads), in_hbm(corner_index), in_hbm(partner), inverse)
    ua, ub = both(u)
    indices = (ua, u, ub)

    def spread(x):
        return lax.all_to_all(x.reshape(devices, -1), GT, 0, 0, tiled=True).reshape(-1, 128)

    def through(x):
        (q,) = call(product_kernel, [field], [VMEM, ANY], [held, sems], us=3)(x, stiff)
        qa, qb = both(q)
        return qa, q, qb

    r0, card = call(send_first_kernel, [field, shape(devices // 2 * CARD, 128)], [SMEM] + [VMEM] * 5, [pool])(
        table, ua, u, ub, corner_map, coarse_inverse
    )
    own_cards = lax.all_to_all(
        card.reshape(devices // 2, -1), GT, 0, 0, tiled=True, axis_index_groups=same_core
    ).reshape(-1, 128)
    pooled = through(r0)
    ma, mb = both(corner_map)
    maps = (ma, corner_map, mb)
    own_cards, pooled, maps = lax.optimization_barrier((own_cards, pooled, maps))
    other_cards = lax.ppermute(own_cards, "tile", inner_swap)
    z0, u, weights = pl.pallas_call(
        solve_first_kernel,
        in_specs=[SMEM] * 2 + [ANY] * 3 + [VMEM] * 8 + [ANY],
        out_specs=[VMEM, VMEM, ANY],
        out_shape=[field, field, pltpu.HBM((PARTS, 6 * SLOTS, PART), BF16)],
        scratch_shapes=[
            pool,
            gathered,
            solver,
            held,
            pltpu.SemaphoreType.DMA((COUNT + PARTS + 3,)),
            pltpu.VMEM((3 * SLOTS, 128), F32),
            pltpu.VMEM((3 * SLOTS, 128), jnp.int32),
            pltpu.VMEM((devices // 2, 128), jnp.int32),
            pltpu.SMEM((3, 8, 128), F32),
        ],
        compiler_params=PARAMS,
        cost_estimate=pl.CostEstimate(flops=4_000_000_000, bytes_accessed=20_000_000, transcendentals=0),
    )(core, table, *indices, own_cards, other_cards, *maps, *pooled, inverse)
    weights = in_hbm(weights)
    coarse_scratch = [gathered, solver, pltpu.SemaphoreType.DMA((PARTS,))]
    coarse_out = [shape(6 * SLOTS, 16), shape(8, 128)]
    ua, ub = both(u)
    w0, parts, q = call(send_second_kernel, [field, pay, field], [SMEM] + [VMEM] * 7, [pool], us=3)(
        table, ua, u, ub, corner_map, schur, r0, z0
    )
    qa, qb = both(q)
    out, sums = call(coarse_kernel, coarse_out, [VMEM, ANY], coarse_scratch, us=20)(spread(parts), weights)
    y0, r1, z1, scale, u = call(
        solve_second_kernel, [field, field, field, shape(3, 8, 128), field], [SMEM] + [VMEM] * 12, [pool], us=3
    )(table, out, sums, *maps, qa, q, qb, local_inverse, r0, z0, w0)
    ua, ub = both(u)
    v1, parts, q = call(send_third_kernel, [field, pay, field], [SMEM] + [VMEM] * 9, [pool], us=3)(
        table, ua, u, ub, corner_map, schur, r1, z1, z0, w0
    )
    qa, qb = both(q)
    out, sums = call(coarse_kernel, coarse_out, [VMEM, ANY], coarse_scratch, us=20)(spread(parts), weights)
    return tuple(
        call(solve_third_kernel, [shape(COUNT, CASES, WIDTH)] * 3, [SMEM] + [VMEM] * 15, [pool], us=2)(
            table, out, sums, *maps, qa, q, qb, scale, z0, w0, y0, r1, z1, v1
        )
    )


def solution(mesh):
    three = P(GT, None, None)
    two = P(GT, None)
    return jax.shard_map(
        shards,
        mesh=mesh,
        in_specs=(three, three, three, three, two, two, two),
        out_specs=(three, three, three),
        check_vma=False,
    )
```

```python
import jax
import jax.numpy as jnp
from jax import lax
from jax.experimental import pallas as pl
from jax.experimental.pallas import tpu as pltpu
from jax.sharding import PartitionSpec as P

GT = ("group", "tile")
F32 = jnp.float32
BF16 = jnp.bfloat16
NT = (((1,), (1,)), ((), ()))
VMEM = pl.BlockSpec(memory_space=pltpu.VMEM)
SMEM = pl.BlockSpec(memory_space=pltpu.SMEM)
ANY = pl.BlockSpec(memory_space=pl.ANY)
PARAMS = pltpu.CompilerParams(vmem_limit_bytes=24 << 20)

COUNT, CASES, WIDTH, CORNERS, ROWS, FACES = 8, 8, 384, 8, 64, 12
CHUNKS = WIDTH // 128
TILES = COUNT * CHUNKS
SLOTS = COUNT * CORNERS
CARD = 37
PARTS, PART, KEEP = 8, 1024, 2


def call(kernel, outs, specs, scratch=(), us=2):
    return pl.pallas_call(
        kernel,
        in_specs=specs,
        out_specs=[VMEM] * len(outs),
        out_shape=outs,
        scratch_shapes=list(scratch),
        compiler_params=PARAMS,
        cost_estimate=pl.CostEstimate(flops=us * 500_000_000, bytes_accessed=us * 3_000_000, transcendentals=0),
    )


def in_hbm(x):
    return pltpu.with_memory_space_constraint(x, pltpu.HBM)


def shape(*dims):
    return jax.ShapeDtypeStruct(dims, F32)


def halves(x):
    high = x.astype(BF16)
    return high, (x - high.astype(F32)).astype(BF16)


def product(vector, matrix):
    vh, vl = halves(vector)
    mh, ml = halves(matrix)
    first = jnp.dot(jnp.concatenate([vh, vl], 0), mh, preferred_element_type=F32)
    return first[:8] + first[8:] + jnp.dot(vh, ml, preferred_element_type=F32)


def lanes(shape_=(8, 128)):
    return lax.broadcasted_iota(jnp.int32, shape_, 1)


def sublanes(shape_=(8, 128)):
    return lax.broadcasted_iota(jnp.int32, shape_, 0)


def put_tiles(ref, p, row):
    for c in range(CHUNKS):
        ref[p * CHUNKS + c] = row[:, c * 128 : (c + 1) * 128]


def get_row(tiles, p):
    return jnp.concatenate([tiles[p * CHUNKS + c] for c in range(CHUNKS)], axis=1)


def jump(pool, table):
    quarter = lanes() // 32
    out = []
    for t in range(TILES):
        p, c = divmod(t, CHUNKS)
        other = None
        for q in range(4):
            f = c * 4 + q
            face = pltpu.roll(pool[table[p, f]], table[8 + p, f], 1)
            other = face if other is None else jnp.where(quarter == q, face, other)
        out.append(pool[TILES + t] - other)
    return out


def fill_pool(pool, a_ref, x_ref, b_ref):
    for e, ref in enumerate((a_ref, x_ref, b_ref)):
        for t in range(TILES):
            pool[e * TILES + t] = ref[t]


def mate_places(core, partner, table_ref):
    region = (partner >= COUNT * FACES).astype(jnp.int32) + (partner >= 2 * COUNT * FACES).astype(jnp.int32)
    within = partner - region * (COUNT * FACES)
    particle = jnp.zeros_like(within)
    for p in range(1, COUNT):
        particle = particle + (within >= p * FACES).astype(jnp.int32)
    face = within - particle * FACES
    region = jnp.where(core[0] == 1, region, 2 - region)
    table_ref[0:8, 0:FACES] = region * TILES + particle * CHUNKS + (face >> 2)
    table_ref[8:16, 0:FACES] = ((lanes((COUNT, FACES)) - face) & 3) * 32


def index_row(index):
    wide = jnp.concatenate([index.astype(F32)] * 16, axis=1)
    keep = lanes() // 8 == sublanes()
    return jnp.broadcast_to(jnp.sum(jnp.where(keep, wide, 0.0), axis=0, keepdims=True), (8, 128))


def copies_of(source, held, sems, first=0):
    return [pltpu.make_async_copy(source.at[i], held.at[i], sems.at[first + i]) for i in range(source.shape[0])]


def fetch(source, held, sems, first=0):
    copies = copies_of(source, held, sems, first)
    for copy in copies:
        copy.start()
    return copies


def multiply(x, copies, held, out_ref):
    for p in range(COUNT):
        copies[p].wait()
        put_tiles(out_ref, p, product(get_row(x, p), held[p]))


def start_kernel(
    core, loads_ref, index_ref, partner_ref, inverse_ref, out_ref, table_ref, loads, index, partner, held, sems
):
    small = [
        pltpu.make_async_copy(source, to, sems.at[COUNT + i])
        for i, (source, to) in enumerate(((loads_ref, loads), (index_ref, index), (partner_ref, partner)))
    ]
    for copy in small:
        copy.start()
    copies = fetch(inverse_ref, held, sems)
    for copy in small:
        copy.wait()
    out_ref[TILES] = index_row(index[...])
    mate_places(core, partner[...], table_ref)
    for p in range(COUNT):
        copies[p].wait()
        put_tiles(out_ref, p, product(loads[p], held[p]))


def product_kernel(x_ref, matrix_ref, out_ref, held, sems):
    copies = fetch(matrix_ref, held, sems)
    multiply(x_ref, copies, held, out_ref)


def column_to_row(columns):
    lane, sub = lanes(), sublanes()
    row = jnp.zeros((8, 128), F32)
    for i, column in enumerate(columns):
        row = jnp.where(lane == i * 8 + sub, jnp.broadcast_to(column, (8, 128)), row)
    return jnp.sum(row, axis=0, keepdims=True)


def case_sum(first, second):
    total = first[0] * second[0]
    for t in range(1, TILES):
        total = total + first[t] * second[t]
    return jnp.sum(total, axis=1, keepdims=True)


def contributions(r, map_ref):
    lane = lanes()
    contrib = jnp.zeros((8, 128), F32)
    for p in range(COUNT):
        for j in range(CORNERS):
            part = r[p * CHUNKS] * map_ref[p, j : j + 1, 0:128]
            for c in range(1, CHUNKS):
                part = part + r[p * CHUNKS + c] * map_ref[p, j : j + 1, c * 128 : (c + 1) * 128]
            total = jnp.sum(part, axis=1, keepdims=True)
            contrib = jnp.where(lane == p * CORNERS + j, jnp.broadcast_to(total, (8, 128)), contrib)
    turned = pltpu.roll(pltpu.roll(contrib, 64, 1), 4, 0)
    return jnp.where(lane < 64, contrib, turned)


def send(r, map_ref, columns, pay_ref):
    pay = contributions(r, map_ref)
    pay = jnp.where(sublanes() < 4, pay, jnp.broadcast_to(column_to_row(columns), (8, 128)))[0:5]
    for at in range(0, pay_ref.shape[0], 5):
        pay_ref[at : at + 5, :] = pay


def send_first_kernel(table, a_ref, x_ref, b_ref, map_ref, inverse_ref, r_ref, card_ref, pool):
    fill_pool(pool, a_ref, x_ref, b_ref)
    r = jump(pool, table)
    for t in range(TILES):
        r_ref[t] = r[t]
    inverse = inverse_ref[...]
    pay = contributions(r, map_ref)
    card = jnp.concatenate([inverse[:32], inverse[32:]], axis=1)
    tail = jnp.where(sublanes() < 1, x_ref[TILES], pltpu.roll(pay, 1, 0))[0:5]
    for at in range(0, card_ref.shape[0], CARD):
        card_ref[at : at + 32, :] = card
        card_ref[at + 32 : at + CARD, :] = tail


def multiply_held(x, matrix_ref, out_ref):
    for p in range(COUNT):
        put_tiles(out_ref, p, product(get_row(x, p), matrix_ref[p]))


def send_second_kernel(
    table, a_ref, x_ref, b_ref, map_ref, schur_ref, r0_ref, z0_ref, weights_ref, w_ref, pay_ref, q_ref, kept_ref,
    pool, sems,
):
    keeps = [pltpu.make_async_copy(weights_ref.at[c], kept_ref.at[c], sems.at[c]) for c in range(KEEP)]
    for keep in keeps:
        keep.start()
    fill_pool(pool, a_ref, x_ref, b_ref)
    w = jump(pool, table)
    for t in range(TILES):
        w_ref[t] = w[t]
    send(w, map_ref, [case_sum(r0_ref, z0_ref), case_sum(z0_ref, w)], pay_ref)
    multiply_held(w, schur_ref, q_ref)
    for keep in keeps:
        keep.wait()


def send_third_kernel(
    table, a_ref, x_ref, b_ref, map_ref, schur_ref, r1_ref, z1_ref, z0_ref, w0_ref, weights_ref,
    v_ref, pay_ref, q_ref, kept_ref, pool, sems,
):
    keeps = [pltpu.make_async_copy(weights_ref.at[c], kept_ref.at[c], sems.at[c]) for c in range(KEEP)]
    for keep in keeps:
        keep.start()
    fill_pool(pool, a_ref, x_ref, b_ref)
    v = jump(pool, table)
    for t in range(TILES):
        v_ref[t] = v[t]
    columns = [case_sum(r1_ref, z1_ref), case_sum(z1_ref, v), case_sum(z0_ref, v), case_sum(z1_ref, w0_ref)]
    send(v, map_ref, columns, pay_ref)
    multiply_held(v, schur_ref, q_ref)
    for keep in keeps:
        keep.wait()


def gather_rows(mine, ids, own_ref, other_ref, rows, names):
    def pick(j, carry):
        row = ids[j >> 6, 0, j & 63].astype(jnp.int32)
        owner = row >> 6
        at = (owner >> 1) * CARD + (row & 31)
        same = (owner & 1) == mine
        here = own_ref[pl.ds(at, 1), :]
        there = other_ref[pl.ds(at, 1), :]
        rows[pl.ds(j, 1), :] = jnp.where(same, here, there)
        names[pl.ds(j, 1), :] = jnp.full((1, 128), row, jnp.int32)
        return carry

    lax.fori_loop(0, 3 * SLOTS, pick, 0, unroll=16)


def place(pair, q, gathered):
    straight = (sublanes() < 4) == (lanes() < 64)
    tile = jnp.where(straight, pair, pltpu.roll(pltpu.roll(pair, 64, 1), 4, 0))
    high, low = halves(tile)
    gathered[:, q * 128 : (q + 1) * 128] = jnp.concatenate([high, low], axis=0)


def unpack(got_ref, gathered):
    for q in range(PARTS * PART // 128):
        at = 10 * q
        place(jnp.concatenate([got_ref[at : at + 4, :], got_ref[at + 5 : at + 9, :]], axis=0), q, gathered)
    return jnp.sum(got_ref[pl.ds(4, PARTS * PART // SLOTS, stride=5), :], axis=0, keepdims=True)


def partial_solve(weights, gathered, c):
    return lax.dot_general(weights[...], gathered[:, c * PART : (c + 1) * PART], NT, preferred_element_type=F32)


def into_pool(out, maps, pool):
    count = 3 * SLOTS
    sol = out[:count] + out[count:]
    sol = sol.T
    sol = sol[:8] + sol[8:]
    own = sublanes((64, 64)) // 8 == lanes((64, 64)) // 8
    for e, map_ref in enumerate(maps):
        part = sol[:, e * SLOTS : (e + 1) * SLOTS]
        spread = jnp.where(own, jnp.concatenate([part] * COUNT, axis=0), 0.0)
        sh, sl = halves(spread)
        ch, cl = halves(map_ref[...].reshape(SLOTS, WIDTH))
        two = jnp.dot(jnp.concatenate([sh, sl], axis=0), ch, preferred_element_type=F32)
        full = two[:64] + two[64:] + jnp.dot(sh, cl, preferred_element_type=F32)
        for p in range(COUNT):
            for c in range(CHUNKS):
                t = e * TILES + p * CHUNKS + c
                pool[t] = pool[t] + full[p * 8 : (p + 1) * 8, c * 128 : (c + 1) * 128]


def coarse_kernel(got_ref, kept_ref, weights_ref, out_ref, sums_ref, gathered, weights, sems):
    copies = [
        pltpu.make_async_copy(weights_ref.at[c], weights.at[c - KEEP], sems.at[c - KEEP]) for c in range(KEEP, PARTS)
    ]
    for copy in copies:
        copy.start()
    sums_ref[...] = jnp.broadcast_to(unpack(got_ref, gathered), (8, 128))
    out = partial_solve(kept_ref.at[0], gathered, 0)
    for c in range(1, PARTS):
        if c >= KEEP:
            copies[c - KEEP].wait()
        out = out + partial_solve(kept_ref.at[c] if c < KEEP else weights.at[c - KEEP], gathered, c)
    out_ref[...] = out


def totals(sums, count):
    lane, sub = lanes(), sublanes()
    row = jnp.broadcast_to(sums, (8, 128))
    return [
        jnp.broadcast_to(jnp.sum(jnp.where(lane == i * 8 + sub, row, 0.0), axis=1, keepdims=True), (8, 128))
        for i in range(count)
    ]


def solve_first_kernel(
    core, table, ia_ref, ix_ref, ib_ref, own_ref, other_ref, am_ref, m_ref, bm_ref, a_ref, x_ref, b_ref, inverse_ref,
    z_ref, u_ref, weights_ref, pool, gathered, weights, held, sems, rows, names, index, ids,
):
    mine = core[0]
    small = [
        pltpu.make_async_copy(ref.at[TILES], ids.at[e], sems.at[COUNT + PARTS + e])
        for e, ref in enumerate((ia_ref, ix_ref, ib_ref))
    ]
    for copy in small:
        copy.start()
    copies = fetch(inverse_ref, held, sems)
    for copy in small:
        copy.wait()
    gather_rows(mine, ids, own_ref, other_ref, rows, names)
    fill_pool(pool, a_ref, x_ref, b_ref)
    chips = PARTS * PART // 128
    own = own_ref[pl.ds(32, chips, stride=CARD), :]
    other = other_ref[pl.ds(32, chips, stride=CARD), :]
    first = jnp.where(mine == 0, own, other)
    second = jnp.where(mine == 0, other, own)
    index[...] = jnp.where(lanes((chips, 128)) < 64, first, pltpu.roll(second, 64, 1)).astype(jnp.int32)
    for q in range(chips):
        at = q * CARD + 33
        own, other = own_ref[at : at + 4, :], other_ref[at : at + 4, :]
        first = jnp.where(mine == 0, own, other)
        second = jnp.where(mine == 0, other, own)
        place(jnp.concatenate([first, second], axis=0), q, gathered)
    upper = (names[...] & 63) >= 32
    kept = jnp.where(upper == (lanes((3 * SLOTS, 128)) >= 64), rows[...], 0.0)
    high, low = halves(kept)
    both = jnp.concatenate([high, low], axis=0)
    names[...] = names[...] >> 6
    spot = sublanes((128, 256)) & 63

    def spread(q, carry):
        row = jnp.concatenate([index[pl.ds(2 * q, 1), :], index[pl.ds(2 * q + 1, 1), :]], axis=1)
        onehot = (spot == (row & 63)).astype(F32).astype(BF16)
        full = jnp.dot(both, onehot, preferred_element_type=F32)
        block = row >> 6
        named = names[...]
        hit = jnp.concatenate([named, named], axis=1) == block
        at = pl.ds(pl.multiple_of((q & 3) * 256, 256), 256)
        weights[q >> 2, 0 : 3 * SLOTS, at] = jnp.where(hit, full[: 3 * SLOTS], 0.0).astype(BF16)
        weights[q >> 2, 3 * SLOTS :, at] = jnp.where(hit, full[3 * SLOTS :], 0.0).astype(BF16)
        return carry

    stores = []
    out = None
    for part in range(PARTS):
        lax.fori_loop(part * 4, part * 4 + 4, spread, 0, unroll=4)
        store = pltpu.make_async_copy(weights.at[part], weights_ref.at[part], sems.at[COUNT + part])
        store.start()
        stores.append(store)
        term = partial_solve(weights.at[part], gathered, part)
        out = term if out is None else out + term
    into_pool(out, (am_ref, m_ref, bm_ref), pool)
    z = [0.5 * t for t in jump(pool, table)]
    for t in range(TILES):
        z_ref[t] = z[t]
    multiply(z, copies, held, u_ref)
    for store in stores:
        store.wait()


def solve_second_kernel(
    table, out_ref, sums_ref, am_ref, m_ref, bm_ref, a_ref, x_ref, b_ref, inverse_ref, r0_ref, z0_ref, w0_ref,
    y_ref, r_ref, z_ref, scale_ref, u_ref, pool,
):
    fill_pool(pool, a_ref, x_ref, b_ref)
    into_pool(out_ref[...], (am_ref, m_ref, bm_ref), pool)
    energy, curve = totals(sums_ref[0:1, :], 2)
    step = energy / curve
    scale_ref[0] = energy
    scale_ref[1] = curve
    scale_ref[2] = step
    y = jump(pool, table)
    z = []
    for t in range(TILES):
        half = 0.5 * y[t]
        y_ref[t] = half
        r_ref[t] = r0_ref[t] - step * w0_ref[t]
        z.append(z0_ref[t] - step * half)
        z_ref[t] = z[t]
    multiply_held(z, inverse_ref, u_ref)


def solve_third_kernel(
    table, out_ref, sums_ref, am_ref, m_ref, bm_ref, a_ref, x_ref, b_ref,
    scale_ref, z0_ref, w0_ref, y0_ref, r1_ref, z1_ref, v1_ref, multipliers_ref, residual_ref, preconditioned_ref,
    pool,
):
    fill_pool(pool, a_ref, x_ref, b_ref)
    into_pool(out_ref[...], (am_ref, m_ref, bm_ref), pool)
    energy, zv, pv, zw = totals(sums_ref[0:1, :], 4)
    first = scale_ref[2]
    grow = energy / scale_ref[0]
    second = energy / (zv + grow * (pv + zw) + grow * grow * scale_ref[1])
    y = jump(pool, table)
    for p in range(COUNT):
        for c in range(CHUNKS):
            t = p * CHUNKS + c
            at = slice(c * 128, (c + 1) * 128)
            multipliers_ref[p, :, at] = first * z0_ref[t] + second * (z1_ref[t] + grow * z0_ref[t])
            residual_ref[p, :, at] = r1_ref[t] - second * (v1_ref[t] + grow * w0_ref[t])
            preconditioned_ref[p, :, at] = z1_ref[t] - second * (0.5 * y[t] + grow * y0_ref[t])


def shards(loads, local_inverse, schur, corner_map, corner_index, partner, coarse_inverse):
    tiles = lax.axis_size("tile")
    devices = lax.axis_size(GT)
    inner_swap = [(i, i ^ 1) for i in range(tiles)]
    outer_swap = [(i, (i - 1) % tiles if i % 2 == 0 else (i + 1) % tiles) for i in range(tiles)]
    same_core = [[2 * i + c for i in range(devices // 2)] for c in range(2)]
    core = lax.axis_index("tile") % 2

    def both(x):
        return lax.ppermute(x, "tile", inner_swap), lax.ppermute(x, "tile", outer_swap)

    field = shape(TILES, 8, 128)
    pool = pltpu.VMEM((3 * TILES, 8, 128), F32)
    gathered = pltpu.VMEM((16, devices * SLOTS), BF16)
    pay = shape(devices * 5, 128)
    sems = pltpu.SemaphoreType.DMA((COUNT,))

    core = core.astype(jnp.int32).reshape(1)
    held = pltpu.VMEM((COUNT, WIDTH, WIDTH), F32)
    solver = pltpu.VMEM((PARTS, 6 * SLOTS, PART), BF16)
    inverse, stiff = in_hbm(local_inverse), in_hbm(schur)
    u, table = call(
        start_kernel,
        [shape(TILES + 1, 8, 128), jax.ShapeDtypeStruct((16, 128), jnp.int32)],
        [SMEM] + [ANY] * 4,
        [
            pltpu.VMEM((COUNT, CASES, WIDTH), F32),
            pltpu.VMEM((COUNT, CORNERS), jnp.int32),
            pltpu.VMEM((COUNT, FACES), jnp.int32),
            held,
            pltpu.SemaphoreType.DMA((COUNT + 3,)),
        ],
        us=4,
    )(core, in_hbm(loads), in_hbm(corner_index), in_hbm(partner), inverse)
    ua, ub = both(u)
    indices = (ua, u, ub)

    def spread(x):
        return lax.all_to_all(x.reshape(devices, -1), GT, 0, 0, tiled=True).reshape(-1, 128)

    def through(x):
        (q,) = call(product_kernel, [field], [VMEM, ANY], [held, sems], us=3)(x, stiff)
        qa, qb = both(q)
        return qa, q, qb

    r0, card = call(send_first_kernel, [field, shape(devices // 2 * CARD, 128)], [SMEM] + [VMEM] * 5, [pool])(
        table, ua, u, ub, corner_map, coarse_inverse
    )
    own_cards = lax.all_to_all(
        card.reshape(devices // 2, -1), GT, 0, 0, tiled=True, axis_index_groups=same_core
    ).reshape(-1, 128)
    pooled = through(r0)
    ma, mb = both(corner_map)
    maps = (ma, corner_map, mb)
    own_cards, pooled, maps = lax.optimization_barrier((own_cards, pooled, maps))
    other_cards = lax.ppermute(own_cards, "tile", inner_swap)
    z0, u, weights = pl.pallas_call(
        solve_first_kernel,
        in_specs=[SMEM] * 2 + [ANY] * 3 + [VMEM] * 8 + [ANY],
        out_specs=[VMEM, VMEM, ANY],
        out_shape=[field, field, pltpu.HBM((PARTS, 6 * SLOTS, PART), BF16)],
        scratch_shapes=[
            pool,
            gathered,
            solver,
            held,
            pltpu.SemaphoreType.DMA((COUNT + PARTS + 3,)),
            pltpu.VMEM((3 * SLOTS, 128), F32),
            pltpu.VMEM((3 * SLOTS, 128), jnp.int32),
            pltpu.VMEM((devices // 2, 128), jnp.int32),
            pltpu.SMEM((3, 8, 128), F32),
        ],
        compiler_params=PARAMS,
        cost_estimate=pl.CostEstimate(flops=4_000_000_000, bytes_accessed=20_000_000, transcendentals=0),
    )(core, table, *indices, own_cards, other_cards, *maps, *pooled, inverse)
    weights = in_hbm(weights)
    rest = pltpu.VMEM((PARTS - KEEP, 6 * SLOTS, PART), BF16)
    kept_shape = jax.ShapeDtypeStruct((KEEP, 6 * SLOTS, PART), BF16)
    keep_scratch = [pool, pltpu.SemaphoreType.DMA((KEEP,))]
    coarse_scratch = [gathered, rest, pltpu.SemaphoreType.DMA((PARTS - KEEP,))]
    coarse_out = [shape(6 * SLOTS, 16), shape(8, 128)]
    ua, ub = both(u)
    w0, parts, q, kept = call(
        send_second_kernel, [field, pay, field, kept_shape], [SMEM] + [VMEM] * 7 + [ANY], keep_scratch, us=3
    )(
        table, ua, u, ub, corner_map, schur, r0, z0, weights
    )
    qa, qb = both(q)
    out, sums = call(coarse_kernel, coarse_out, [VMEM, VMEM, ANY], coarse_scratch, us=20)(spread(parts), kept, weights)
    y0, r1, z1, scale, u = call(
        solve_second_kernel, [field, field, field, shape(3, 8, 128), field], [SMEM] + [VMEM] * 12, [pool], us=3
    )(table, out, sums, *maps, qa, q, qb, local_inverse, r0, z0, w0)
    ua, ub = both(u)
    v1, parts, q, kept = call(
        send_third_kernel, [field, pay, field, kept_shape], [SMEM] + [VMEM] * 9 + [ANY], keep_scratch, us=3
    )(
        table, ua, u, ub, corner_map, schur, r1, z1, z0, w0, weights
    )
    qa, qb = both(q)
    out, sums = call(coarse_kernel, coarse_out, [VMEM, VMEM, ANY], coarse_scratch, us=20)(spread(parts), kept, weights)
    return tuple(
        call(solve_third_kernel, [shape(COUNT, CASES, WIDTH)] * 3, [SMEM] + [VMEM] * 15, [pool], us=2)(
            table, out, sums, *maps, qa, q, qb, scale, z0, w0, y0, r1, z1, v1
        )
    )


def solution(mesh):
    three = P(GT, None, None)
    two = P(GT, None)
    return jax.shard_map(
        shards,
        mesh=mesh,
        in_specs=(three, three, three, three, two, two, two),
        out_specs=(three, three, three),
        check_vma=False,
    )
```

```python
import jax
import jax.numpy as jnp
from jax import lax
from jax.experimental import pallas as pl
from jax.experimental.pallas import tpu as pltpu
from jax.sharding import PartitionSpec as P

GT = ("group", "tile")
F32 = jnp.float32
BF16 = jnp.bfloat16
NT = (((1,), (1,)), ((), ()))
VMEM = pl.BlockSpec(memory_space=pltpu.VMEM)
SMEM = pl.BlockSpec(memory_space=pltpu.SMEM)
ANY = pl.BlockSpec(memory_space=pl.ANY)
PARAMS = pltpu.CompilerParams(vmem_limit_bytes=24 << 20)

COUNT, CASES, WIDTH, CORNERS, ROWS, FACES = 8, 8, 384, 8, 64, 12
CHUNKS = WIDTH // 128
TILES = COUNT * CHUNKS
SLOTS = COUNT * CORNERS
CARD = 37
PARTS, PART, KEEP = 8, 1024, 2


def call(kernel, outs, specs, scratch=(), us=2):
    return pl.pallas_call(
        kernel,
        in_specs=specs,
        out_specs=[VMEM] * len(outs),
        out_shape=outs,
        scratch_shapes=list(scratch),
        compiler_params=PARAMS,
        cost_estimate=pl.CostEstimate(flops=us * 500_000_000, bytes_accessed=us * 3_000_000, transcendentals=0),
    )


def in_hbm(x):
    return pltpu.with_memory_space_constraint(x, pltpu.HBM)


def shape(*dims):
    return jax.ShapeDtypeStruct(dims, F32)


def halves(x):
    high = x.astype(BF16)
    return high, (x - high.astype(F32)).astype(BF16)


def product(vector, matrix):
    vh, vl = halves(vector)
    mh, ml = halves(matrix)
    first = jnp.dot(jnp.concatenate([vh, vl], 0), mh, preferred_element_type=F32)
    return first[:8] + first[8:] + jnp.dot(vh, ml, preferred_element_type=F32)


def lanes(shape_=(8, 128)):
    return lax.broadcasted_iota(jnp.int32, shape_, 1)


def sublanes(shape_=(8, 128)):
    return lax.broadcasted_iota(jnp.int32, shape_, 0)


def put_tiles(ref, p, row):
    for c in range(CHUNKS):
        ref[p * CHUNKS + c] = row[:, c * 128 : (c + 1) * 128]


def get_row(tiles, p):
    return jnp.concatenate([tiles[p * CHUNKS + c] for c in range(CHUNKS)], axis=1)


def jump(pool, table):
    quarter = lanes() // 32
    out = []
    for t in range(TILES):
        p, c = divmod(t, CHUNKS)
        other = None
        for q in range(4):
            f = c * 4 + q
            face = pltpu.roll(pool[table[p, f]], table[8 + p, f], 1)
            other = face if other is None else jnp.where(quarter == q, face, other)
        out.append(pool[TILES + t] - other)
    return out


def fill_pool(pool, a_ref, x_ref, b_ref):
    for e, ref in enumerate((a_ref, x_ref, b_ref)):
        for t in range(TILES):
            pool[e * TILES + t] = ref[t]


def mate_places(core, partner, table_ref):
    region = (partner >= COUNT * FACES).astype(jnp.int32) + (partner >= 2 * COUNT * FACES).astype(jnp.int32)
    within = partner - region * (COUNT * FACES)
    particle = jnp.zeros_like(within)
    for p in range(1, COUNT):
        particle = particle + (within >= p * FACES).astype(jnp.int32)
    face = within - particle * FACES
    region = jnp.where(core[0] == 1, region, 2 - region)
    table_ref[0:8, 0:FACES] = region * TILES + particle * CHUNKS + (face >> 2)
    table_ref[8:16, 0:FACES] = ((lanes((COUNT, FACES)) - face) & 3) * 32


def index_row(index):
    wide = jnp.concatenate([index.astype(F32)] * 16, axis=1)
    keep = lanes() // 8 == sublanes()
    return jnp.broadcast_to(jnp.sum(jnp.where(keep, wide, 0.0), axis=0, keepdims=True), (8, 128))


def copies_of(source, held, sems, first=0):
    return [pltpu.make_async_copy(source.at[i], held.at[i], sems.at[first + i]) for i in range(source.shape[0])]


def fetch(source, held, sems, first=0):
    copies = copies_of(source, held, sems, first)
    for copy in copies:
        copy.start()
    return copies


def multiply(x, copies, held, out_ref):
    for p in range(COUNT):
        copies[p].wait()
        put_tiles(out_ref, p, product(get_row(x, p), held[p]))


def start_kernel(
    core, loads_ref, index_ref, partner_ref, inverse_ref, out_ref, table_ref, loads, index, partner, held, sems
):
    small = [
        pltpu.make_async_copy(source, to, sems.at[COUNT + i])
        for i, (source, to) in enumerate(((loads_ref, loads), (index_ref, index), (partner_ref, partner)))
    ]
    for copy in small:
        copy.start()
    copies = fetch(inverse_ref, held, sems)
    for copy in small:
        copy.wait()
    out_ref[TILES] = index_row(index[...])
    mate_places(core, partner[...], table_ref)
    for p in range(COUNT):
        copies[p].wait()
        put_tiles(out_ref, p, product(loads[p], held[p]))


def product_kernel(x_ref, matrix_ref, out_ref, held, sems):
    copies = fetch(matrix_ref, held, sems)
    multiply(x_ref, copies, held, out_ref)


def column_to_row(columns):
    lane, sub = lanes(), sublanes()
    row = jnp.zeros((8, 128), F32)
    for i, column in enumerate(columns):
        row = jnp.where(lane == i * 8 + sub, jnp.broadcast_to(column, (8, 128)), row)
    return jnp.sum(row, axis=0, keepdims=True)


def case_sum(first, second):
    total = first[0] * second[0]
    for t in range(1, TILES):
        total = total + first[t] * second[t]
    return jnp.sum(total, axis=1, keepdims=True)


def contributions(r, map_ref):
    lane = lanes()
    contrib = jnp.zeros((8, 128), F32)
    for p in range(COUNT):
        for j in range(CORNERS):
            part = r[p * CHUNKS] * map_ref[p, j : j + 1, 0:128]
            for c in range(1, CHUNKS):
                part = part + r[p * CHUNKS + c] * map_ref[p, j : j + 1, c * 128 : (c + 1) * 128]
            total = jnp.sum(part, axis=1, keepdims=True)
            contrib = jnp.where(lane == p * CORNERS + j, jnp.broadcast_to(total, (8, 128)), contrib)
    turned = pltpu.roll(pltpu.roll(contrib, 64, 1), 4, 0)
    return jnp.where(lane < 64, contrib, turned)


def send(r, map_ref, columns, pay_ref):
    pay = contributions(r, map_ref)
    pay = jnp.where(sublanes() < 4, pay, jnp.broadcast_to(column_to_row(columns), (8, 128)))[0:5]
    for at in range(0, pay_ref.shape[0], 5):
        pay_ref[at : at + 5, :] = pay


def send_first_kernel(table, a_ref, x_ref, b_ref, map_ref, inverse_ref, r_ref, card_ref, pool):
    fill_pool(pool, a_ref, x_ref, b_ref)
    r = jump(pool, table)
    for t in range(TILES):
        r_ref[t] = r[t]
    inverse = inverse_ref[...]
    pay = contributions(r, map_ref)
    card = jnp.concatenate([inverse[:32], inverse[32:]], axis=1)
    tail = jnp.where(sublanes() < 1, x_ref[TILES], pltpu.roll(pay, 1, 0))[0:5]
    for at in range(0, card_ref.shape[0], CARD):
        card_ref[at : at + 32, :] = card
        card_ref[at + 32 : at + CARD, :] = tail


def multiply_held(x, matrix_ref, out_ref):
    for p in range(COUNT):
        put_tiles(out_ref, p, product(get_row(x, p), matrix_ref[p]))


def send_second_kernel(table, a_ref, x_ref, b_ref, map_ref, schur_ref, r0_ref, z0_ref, w_ref, pay_ref, q_ref, pool):
    fill_pool(pool, a_ref, x_ref, b_ref)
    w = jump(pool, table)
    for t in range(TILES):
        w_ref[t] = w[t]
    send(w, map_ref, [case_sum(r0_ref, z0_ref), case_sum(z0_ref, w)], pay_ref)
    multiply_held(w, schur_ref, q_ref)


def send_third_kernel(
    table, a_ref, x_ref, b_ref, map_ref, schur_ref, r1_ref, z1_ref, z0_ref, w0_ref, v_ref, pay_ref, q_ref, pool
):
    fill_pool(pool, a_ref, x_ref, b_ref)
    v = jump(pool, table)
    for t in range(TILES):
        v_ref[t] = v[t]
    columns = [case_sum(r1_ref, z1_ref), case_sum(z1_ref, v), case_sum(z0_ref, v), case_sum(z1_ref, w0_ref)]
    send(v, map_ref, columns, pay_ref)
    multiply_held(v, schur_ref, q_ref)


def gather_rows(mine, ids, own_ref, other_ref, rows, names):
    def pick(j, carry):
        row = ids[j >> 6, 0, j & 63].astype(jnp.int32)
        owner = row >> 6
        at = (owner >> 1) * CARD + (row & 31)
        same = (owner & 1) == mine
        here = own_ref[pl.ds(at, 1), :]
        there = other_ref[pl.ds(at, 1), :]
        rows[pl.ds(j, 1), :] = jnp.where(same, here, there)
        names[pl.ds(j, 1), :] = jnp.full((1, 128), row, jnp.int32)
        return carry

    lax.fori_loop(0, 3 * SLOTS, pick, 0, unroll=16)


def place(pair, q, gathered):
    straight = (sublanes() < 4) == (lanes() < 64)
    tile = jnp.where(straight, pair, pltpu.roll(pltpu.roll(pair, 64, 1), 4, 0))
    high, low = halves(tile)
    gathered[:, q * 128 : (q + 1) * 128] = jnp.concatenate([high, low], axis=0)


def unpack(got_ref, gathered):
    for q in range(PARTS * PART // 128):
        at = 10 * q
        place(jnp.concatenate([got_ref[at : at + 4, :], got_ref[at + 5 : at + 9, :]], axis=0), q, gathered)
    return jnp.sum(got_ref[pl.ds(4, PARTS * PART // SLOTS, stride=5), :], axis=0, keepdims=True)


def partial_solve(weights, gathered, c):
    return lax.dot_general(weights[...], gathered[:, c * PART : (c + 1) * PART], NT, preferred_element_type=F32)


def into_pool(out, maps, pool):
    count = 3 * SLOTS
    sol = out[:count] + out[count:]
    sol = sol.T
    sol = sol[:8] + sol[8:]
    own = sublanes((64, 64)) // 8 == lanes((64, 64)) // 8
    for e, map_ref in enumerate(maps):
        part = sol[:, e * SLOTS : (e + 1) * SLOTS]
        spread = jnp.where(own, jnp.concatenate([part] * COUNT, axis=0), 0.0)
        sh, sl = halves(spread)
        ch, cl = halves(map_ref[...].reshape(SLOTS, WIDTH))
        two = jnp.dot(jnp.concatenate([sh, sl], axis=0), ch, preferred_element_type=F32)
        full = two[:64] + two[64:] + jnp.dot(sh, cl, preferred_element_type=F32)
        for p in range(COUNT):
            for c in range(CHUNKS):
                t = e * TILES + p * CHUNKS + c
                pool[t] = pool[t] + full[p * 8 : (p + 1) * 8, c * 128 : (c + 1) * 128]


def hold_kernel(after_ref, source_ref, held_ref, sems):
    del after_ref
    for copy in fetch(source_ref, held_ref, sems):
        copy.wait()


def keep_kernel(after_ref, weights_ref, kept_ref, sems):
    del after_ref
    copies = [pltpu.make_async_copy(weights_ref.at[c], kept_ref.at[c], sems.at[c]) for c in range(KEEP)]
    for copy in copies:
        copy.start()
    for copy in copies:
        copy.wait()


def coarse_kernel(got_ref, kept_ref, weights_ref, out_ref, sums_ref, gathered, weights, sems):
    copies = [
        pltpu.make_async_copy(weights_ref.at[c], weights.at[c - KEEP], sems.at[c - KEEP]) for c in range(KEEP, PARTS)
    ]
    for copy in copies:
        copy.start()
    sums_ref[...] = jnp.broadcast_to(unpack(got_ref, gathered), (8, 128))
    out = partial_solve(kept_ref.at[0], gathered, 0)
    for c in range(1, PARTS):
        if c >= KEEP:
            copies[c - KEEP].wait()
        out = out + partial_solve(kept_ref.at[c] if c < KEEP else weights.at[c - KEEP], gathered, c)
    out_ref[...] = out


def totals(sums, count):
    lane, sub = lanes(), sublanes()
    row = jnp.broadcast_to(sums, (8, 128))
    return [
        jnp.broadcast_to(jnp.sum(jnp.where(lane == i * 8 + sub, row, 0.0), axis=1, keepdims=True), (8, 128))
        for i in range(count)
    ]


def solve_first_kernel(
    core, table, ia_ref, ix_ref, ib_ref, own_ref, other_ref, am_ref, m_ref, bm_ref, a_ref, x_ref, b_ref, inverse_ref,
    z_ref, u_ref, weights_ref, pool, gathered, weights, held, sems, rows, names, index, ids,
):
    mine = core[0]
    small = [
        pltpu.make_async_copy(ref.at[TILES], ids.at[e], sems.at[COUNT + PARTS + e])
        for e, ref in enumerate((ia_ref, ix_ref, ib_ref))
    ]
    for copy in small:
        copy.start()
    copies = fetch(inverse_ref, held, sems)
    for copy in small:
        copy.wait()
    gather_rows(mine, ids, own_ref, other_ref, rows, names)
    fill_pool(pool, a_ref, x_ref, b_ref)
    chips = PARTS * PART // 128
    own = own_ref[pl.ds(32, chips, stride=CARD), :]
    other = other_ref[pl.ds(32, chips, stride=CARD), :]
    first = jnp.where(mine == 0, own, other)
    second = jnp.where(mine == 0, other, own)
    index[...] = jnp.where(lanes((chips, 128)) < 64, first, pltpu.roll(second, 64, 1)).astype(jnp.int32)
    for q in range(chips):
        at = q * CARD + 33
        own, other = own_ref[at : at + 4, :], other_ref[at : at + 4, :]
        first = jnp.where(mine == 0, own, other)
        second = jnp.where(mine == 0, other, own)
        place(jnp.concatenate([first, second], axis=0), q, gathered)
    upper = (names[...] & 63) >= 32
    kept = jnp.where(upper == (lanes((3 * SLOTS, 128)) >= 64), rows[...], 0.0)
    high, low = halves(kept)
    both = jnp.concatenate([high, low], axis=0)
    names[...] = names[...] >> 6
    spot = sublanes((128, 256)) & 63

    def spread(q, carry):
        row = jnp.concatenate([index[pl.ds(2 * q, 1), :], index[pl.ds(2 * q + 1, 1), :]], axis=1)
        onehot = (spot == (row & 63)).astype(F32).astype(BF16)
        full = jnp.dot(both, onehot, preferred_element_type=F32)
        block = row >> 6
        named = names[...]
        hit = jnp.concatenate([named, named], axis=1) == block
        at = pl.ds(pl.multiple_of((q & 3) * 256, 256), 256)
        weights[q >> 2, 0 : 3 * SLOTS, at] = jnp.where(hit, full[: 3 * SLOTS], 0.0).astype(BF16)
        weights[q >> 2, 3 * SLOTS :, at] = jnp.where(hit, full[3 * SLOTS :], 0.0).astype(BF16)
        return carry

    stores = []
    out = None
    for part in range(PARTS):
        lax.fori_loop(part * 4, part * 4 + 4, spread, 0, unroll=4)
        store = pltpu.make_async_copy(weights.at[part], weights_ref.at[part], sems.at[COUNT + part])
        store.start()
        stores.append(store)
        term = partial_solve(weights.at[part], gathered, part)
        out = term if out is None else out + term
    into_pool(out, (am_ref, m_ref, bm_ref), pool)
    z = [0.5 * t for t in jump(pool, table)]
    for t in range(TILES):
        z_ref[t] = z[t]
    multiply(z, copies, held, u_ref)
    for store in stores:
        store.wait()


def solve_second_kernel(
    table, out_ref, sums_ref, am_ref, m_ref, bm_ref, a_ref, x_ref, b_ref, inverse_ref, r0_ref, z0_ref, w0_ref,
    y_ref, r_ref, z_ref, scale_ref, u_ref, pool,
):
    fill_pool(pool, a_ref, x_ref, b_ref)
    into_pool(out_ref[...], (am_ref, m_ref, bm_ref), pool)
    energy, curve = totals(sums_ref[0:1, :], 2)
    step = energy / curve
    scale_ref[0] = energy
    scale_ref[1] = curve
    scale_ref[2] = step
    y = jump(pool, table)
    z = []
    for t in range(TILES):
        half = 0.5 * y[t]
        y_ref[t] = half
        r_ref[t] = r0_ref[t] - step * w0_ref[t]
        z.append(z0_ref[t] - step * half)
        z_ref[t] = z[t]
    multiply_held(z, inverse_ref, u_ref)


def solve_third_kernel(
    table, out_ref, sums_ref, am_ref, m_ref, bm_ref, a_ref, x_ref, b_ref,
    scale_ref, z0_ref, w0_ref, y0_ref, r1_ref, z1_ref, v1_ref, multipliers_ref, residual_ref, preconditioned_ref,
    pool,
):
    fill_pool(pool, a_ref, x_ref, b_ref)
    into_pool(out_ref[...], (am_ref, m_ref, bm_ref), pool)
    energy, zv, pv, zw = totals(sums_ref[0:1, :], 4)
    first = scale_ref[2]
    grow = energy / scale_ref[0]
    second = energy / (zv + grow * (pv + zw) + grow * grow * scale_ref[1])
    y = jump(pool, table)
    for p in range(COUNT):
        for c in range(CHUNKS):
            t = p * CHUNKS + c
            at = slice(c * 128, (c + 1) * 128)
            multipliers_ref[p, :, at] = first * z0_ref[t] + second * (z1_ref[t] + grow * z0_ref[t])
            residual_ref[p, :, at] = r1_ref[t] - second * (v1_ref[t] + grow * w0_ref[t])
            preconditioned_ref[p, :, at] = z1_ref[t] - second * (0.5 * y[t] + grow * y0_ref[t])


def shards(loads, local_inverse, schur, corner_map, corner_index, partner, coarse_inverse):
    tiles = lax.axis_size("tile")
    devices = lax.axis_size(GT)
    inner_swap = [(i, i ^ 1) for i in range(tiles)]
    outer_swap = [(i, (i - 1) % tiles if i % 2 == 0 else (i + 1) % tiles) for i in range(tiles)]
    same_core = [[2 * i + c for i in range(devices // 2)] for c in range(2)]
    core = lax.axis_index("tile") % 2

    def both(x):
        return lax.ppermute(x, "tile", inner_swap), lax.ppermute(x, "tile", outer_swap)

    field = shape(TILES, 8, 128)
    pool = pltpu.VMEM((3 * TILES, 8, 128), F32)
    gathered = pltpu.VMEM((16, devices * SLOTS), BF16)
    pay = shape(devices * 5, 128)
    sems = pltpu.SemaphoreType.DMA((COUNT,))

    core = core.astype(jnp.int32).reshape(1)
    held = pltpu.VMEM((COUNT, WIDTH, WIDTH), F32)
    solver = pltpu.VMEM((PARTS, 6 * SLOTS, PART), BF16)
    inverse, stiff = in_hbm(local_inverse), in_hbm(schur)
    u, table = call(
        start_kernel,
        [shape(TILES + 1, 8, 128), jax.ShapeDtypeStruct((16, 128), jnp.int32)],
        [SMEM] + [ANY] * 4,
        [
            pltpu.VMEM((COUNT, CASES, WIDTH), F32),
            pltpu.VMEM((COUNT, CORNERS), jnp.int32),
            pltpu.VMEM((COUNT, FACES), jnp.int32),
            held,
            pltpu.SemaphoreType.DMA((COUNT + 3,)),
        ],
        us=4,
    )(core, in_hbm(loads), in_hbm(corner_index), in_hbm(partner), inverse)
    ua, ub = both(u)
    indices = (ua, u, ub)

    def spread(x):
        return lax.all_to_all(x.reshape(devices, -1), GT, 0, 0, tiled=True).reshape(-1, 128)

    def through(x):
        (q,) = call(product_kernel, [field], [VMEM, ANY], [held, sems], us=3)(x, stiff)
        qa, qb = both(q)
        return qa, q, qb

    r0, card = call(send_first_kernel, [field, shape(devices // 2 * CARD, 128)], [SMEM] + [VMEM] * 5, [pool])(
        table, ua, u, ub, corner_map, coarse_inverse
    )
    own_cards = lax.all_to_all(
        card.reshape(devices // 2, -1), GT, 0, 0, tiled=True, axis_index_groups=same_core
    ).reshape(-1, 128)
    pooled = through(r0)
    ma, mb = both(corner_map)
    maps = (ma, corner_map, mb)
    own_cards, pooled, maps = lax.optimization_barrier((own_cards, pooled, maps))
    other_cards = lax.ppermute(own_cards, "tile", inner_swap)
    z0, u, weights = pl.pallas_call(
        solve_first_kernel,
        in_specs=[SMEM] * 2 + [ANY] * 3 + [VMEM] * 8 + [ANY],
        out_specs=[VMEM, VMEM, ANY],
        out_shape=[field, field, pltpu.HBM((PARTS, 6 * SLOTS, PART), BF16)],
        scratch_shapes=[
            pool,
            gathered,
            solver,
            held,
            pltpu.SemaphoreType.DMA((COUNT + PARTS + 3,)),
            pltpu.VMEM((3 * SLOTS, 128), F32),
            pltpu.VMEM((3 * SLOTS, 128), jnp.int32),
            pltpu.VMEM((devices // 2, 128), jnp.int32),
            pltpu.SMEM((3, 8, 128), F32),
        ],
        compiler_params=PARAMS,
        cost_estimate=pl.CostEstimate(flops=4_000_000_000, bytes_accessed=20_000_000, transcendentals=0),
    )(core, table, *indices, own_cards, other_cards, *maps, *pooled, inverse)
    weights = in_hbm(weights)
    rest = pltpu.VMEM((PARTS - KEEP, 6 * SLOTS, PART), BF16)
    kept_shape = jax.ShapeDtypeStruct((KEEP, 6 * SLOTS, PART), BF16)
    coarse_scratch = [gathered, rest, pltpu.SemaphoreType.DMA((PARTS - KEEP,))]

    def hold(after):
        return call(hold_kernel, [shape(COUNT, WIDTH, WIDTH)], [ANY] * 2, [sems], us=2)(after, stiff)[0]

    def keep(after):
        return call(keep_kernel, [kept_shape], [ANY] * 2, [pltpu.SemaphoreType.DMA((KEEP,))], us=2)(after, weights)[0]

    coarse_out = [shape(6 * SLOTS, 16), shape(8, 128)]
    ua, ub = both(u)
    w0, parts, q = call(send_second_kernel, [field, pay, field], [SMEM] + [VMEM] * 7, [pool], us=3)(
        table, ua, u, ub, corner_map, hold(u), r0, z0
    )
    qa, qb = both(q)
    out, sums = call(coarse_kernel, coarse_out, [VMEM, VMEM, ANY], coarse_scratch, us=20)(spread(parts), keep(qb), weights)
    y0, r1, z1, scale, u = call(
        solve_second_kernel, [field, field, field, shape(3, 8, 128), field], [SMEM] + [VMEM] * 12, [pool], us=3
    )(table, out, sums, *maps, qa, q, qb, local_inverse, r0, z0, w0)
    ua, ub = both(u)
    v1, parts, q = call(send_third_kernel, [field, pay, field], [SMEM] + [VMEM] * 9, [pool], us=3)(
        table, ua, u, ub, corner_map, hold(u), r1, z1, z0, w0
    )
    qa, qb = both(q)
    out, sums = call(coarse_kernel, coarse_out, [VMEM, VMEM, ANY], coarse_scratch, us=20)(spread(parts), keep(qb), weights)
    return tuple(
        call(solve_third_kernel, [shape(COUNT, CASES, WIDTH)] * 3, [SMEM] + [VMEM] * 15, [pool], us=2)(
            table, out, sums, *maps, qa, q, qb, scale, z0, w0, y0, r1, z1, v1
        )
    )


def solution(mesh):
    three = P(GT, None, None)
    two = P(GT, None)
    return jax.shard_map(
        shards,
        mesh=mesh,
        in_specs=(three, three, three, three, two, two, two),
        out_specs=(three, three, three),
        check_vma=False,
    )
```

```python
import jax
import jax.numpy as jnp
from jax import lax
from jax.experimental import pallas as pl
from jax.experimental.pallas import tpu as pltpu
from jax.sharding import PartitionSpec as P

GT = ("group", "tile")
F32 = jnp.float32
BF16 = jnp.bfloat16
NT = (((1,), (1,)), ((), ()))
VMEM = pl.BlockSpec(memory_space=pltpu.VMEM)
SMEM = pl.BlockSpec(memory_space=pltpu.SMEM)
ANY = pl.BlockSpec(memory_space=pl.ANY)
PARAMS = pltpu.CompilerParams(vmem_limit_bytes=24 << 20)

COUNT, CASES, WIDTH, CORNERS, ROWS, FACES = 8, 8, 384, 8, 64, 12
CHUNKS = WIDTH // 128
TILES = COUNT * CHUNKS
SLOTS = COUNT * CORNERS
CARD = 37
PARTS, PART, KEEP = 8, 1024, 2


def call(kernel, outs, specs, scratch=(), us=2):
    return pl.pallas_call(
        kernel,
        in_specs=specs,
        out_specs=[VMEM] * len(outs),
        out_shape=outs,
        scratch_shapes=list(scratch),
        compiler_params=PARAMS,
        cost_estimate=pl.CostEstimate(flops=us * 500_000_000, bytes_accessed=us * 3_000_000, transcendentals=0),
    )


def in_hbm(x):
    return pltpu.with_memory_space_constraint(x, pltpu.HBM)


def shape(*dims):
    return jax.ShapeDtypeStruct(dims, F32)


def halves(x):
    high = x.astype(BF16)
    return high, (x - high.astype(F32)).astype(BF16)


def product(vector, matrix):
    vh, vl = halves(vector)
    mh, ml = halves(matrix)
    first = jnp.dot(jnp.concatenate([vh, vl], 0), mh, preferred_element_type=F32)
    return first[:8] + first[8:] + jnp.dot(vh, ml, preferred_element_type=F32)


def lanes(shape_=(8, 128)):
    return lax.broadcasted_iota(jnp.int32, shape_, 1)


def sublanes(shape_=(8, 128)):
    return lax.broadcasted_iota(jnp.int32, shape_, 0)


def put_tiles(ref, p, row):
    for c in range(CHUNKS):
        ref[p * CHUNKS + c] = row[:, c * 128 : (c + 1) * 128]


def get_row(tiles, p):
    return jnp.concatenate([tiles[p * CHUNKS + c] for c in range(CHUNKS)], axis=1)


def jump(pool, table):
    quarter = lanes() // 32
    out = []
    for t in range(TILES):
        p, c = divmod(t, CHUNKS)
        other = None
        for q in range(4):
            f = c * 4 + q
            face = pltpu.roll(pool[table[p, f]], table[8 + p, f], 1)
            other = face if other is None else jnp.where(quarter == q, face, other)
        out.append(pool[TILES + t] - other)
    return out


def fill_pool(pool, a_ref, x_ref, b_ref):
    for e, ref in enumerate((a_ref, x_ref, b_ref)):
        for t in range(TILES):
            pool[e * TILES + t] = ref[t]


def mate_places(core, partner, table_ref):
    region = (partner >= COUNT * FACES).astype(jnp.int32) + (partner >= 2 * COUNT * FACES).astype(jnp.int32)
    within = partner - region * (COUNT * FACES)
    particle = jnp.zeros_like(within)
    for p in range(1, COUNT):
        particle = particle + (within >= p * FACES).astype(jnp.int32)
    face = within - particle * FACES
    region = jnp.where(core[0] == 1, region, 2 - region)
    table_ref[0:8, 0:FACES] = region * TILES + particle * CHUNKS + (face >> 2)
    table_ref[8:16, 0:FACES] = ((lanes((COUNT, FACES)) - face) & 3) * 32


def index_row(index):
    wide = jnp.concatenate([index.astype(F32)] * 16, axis=1)
    keep = lanes() // 8 == sublanes()
    return jnp.broadcast_to(jnp.sum(jnp.where(keep, wide, 0.0), axis=0, keepdims=True), (8, 128))


def copies_of(source, held, sems, first=0):
    return [pltpu.make_async_copy(source.at[i], held.at[i], sems.at[first + i]) for i in range(source.shape[0])]


def fetch(source, held, sems, first=0):
    copies = copies_of(source, held, sems, first)
    for copy in copies:
        copy.start()
    return copies


def multiply(x, copies, held, out_ref):
    for p in range(COUNT):
        copies[p].wait()
        put_tiles(out_ref, p, product(get_row(x, p), held[p]))


def start_kernel(
    core, loads_ref, index_ref, partner_ref, inverse_ref, out_ref, table_ref, loads, index, partner, held, sems
):
    small = [
        pltpu.make_async_copy(source, to, sems.at[COUNT + i])
        for i, (source, to) in enumerate(((loads_ref, loads), (index_ref, index), (partner_ref, partner)))
    ]
    for copy in small:
        copy.start()
    copies = fetch(inverse_ref, held, sems)
    for copy in small:
        copy.wait()
    out_ref[TILES] = index_row(index[...])
    mate_places(core, partner[...], table_ref)
    for p in range(COUNT):
        copies[p].wait()
        put_tiles(out_ref, p, product(loads[p], held[p]))


def product_kernel(x_ref, matrix_ref, out_ref, held, sems):
    copies = fetch(matrix_ref, held, sems)
    multiply(x_ref, copies, held, out_ref)


def column_to_row(columns):
    lane, sub = lanes(), sublanes()
    row = jnp.zeros((8, 128), F32)
    for i, column in enumerate(columns):
        row = jnp.where(lane == i * 8 + sub, jnp.broadcast_to(column, (8, 128)), row)
    return jnp.sum(row, axis=0, keepdims=True)


def case_sum(first, second):
    total = first[0] * second[0]
    for t in range(1, TILES):
        total = total + first[t] * second[t]
    return jnp.sum(total, axis=1, keepdims=True)


def contributions(r, map_ref):
    lane = lanes()
    contrib = jnp.zeros((8, 128), F32)
    for p in range(COUNT):
        for j in range(CORNERS):
            part = r[p * CHUNKS] * map_ref[p, j : j + 1, 0:128]
            for c in range(1, CHUNKS):
                part = part + r[p * CHUNKS + c] * map_ref[p, j : j + 1, c * 128 : (c + 1) * 128]
            total = jnp.sum(part, axis=1, keepdims=True)
            contrib = jnp.where(lane == p * CORNERS + j, jnp.broadcast_to(total, (8, 128)), contrib)
    turned = pltpu.roll(pltpu.roll(contrib, 64, 1), 4, 0)
    return jnp.where(lane < 64, contrib, turned)


def send(r, map_ref, columns, pay_ref):
    pay = contributions(r, map_ref)
    pay = jnp.where(sublanes() < 4, pay, jnp.broadcast_to(column_to_row(columns), (8, 128)))[0:5]
    for at in range(0, pay_ref.shape[0], 5):
        pay_ref[at : at + 5, :] = pay


def send_first_kernel(table, a_ref, x_ref, b_ref, map_ref, inverse_ref, r_ref, card_ref, pool):
    fill_pool(pool, a_ref, x_ref, b_ref)
    r = jump(pool, table)
    for t in range(TILES):
        r_ref[t] = r[t]
    inverse = inverse_ref[...]
    pay = contributions(r, map_ref)
    card = jnp.concatenate([inverse[:32], inverse[32:]], axis=1)
    tail = jnp.where(sublanes() < 1, x_ref[TILES], pltpu.roll(pay, 1, 0))[0:5]
    for at in range(0, card_ref.shape[0], CARD):
        card_ref[at : at + 32, :] = card
        card_ref[at + 32 : at + CARD, :] = tail


def multiply_held(x, matrix_ref, out_ref):
    for p in range(COUNT):
        put_tiles(out_ref, p, product(get_row(x, p), matrix_ref[p]))


def send_second_kernel(table, a_ref, x_ref, b_ref, map_ref, schur_ref, r0_ref, z0_ref, w_ref, pay_ref, q_ref, pool):
    fill_pool(pool, a_ref, x_ref, b_ref)
    w = jump(pool, table)
    for t in range(TILES):
        w_ref[t] = w[t]
    send(w, map_ref, [case_sum(r0_ref, z0_ref), case_sum(z0_ref, w)], pay_ref)
    multiply_held(w, schur_ref, q_ref)


def send_third_kernel(
    table, a_ref, x_ref, b_ref, map_ref, schur_ref, r1_ref, z1_ref, z0_ref, w0_ref, v_ref, pay_ref, q_ref, pool
):
    fill_pool(pool, a_ref, x_ref, b_ref)
    v = jump(pool, table)
    for t in range(TILES):
        v_ref[t] = v[t]
    columns = [case_sum(r1_ref, z1_ref), case_sum(z1_ref, v), case_sum(z0_ref, v), case_sum(z1_ref, w0_ref)]
    send(v, map_ref, columns, pay_ref)
    multiply_held(v, schur_ref, q_ref)


def gather_rows(mine, ids, own_ref, other_ref, rows, names):
    def pick(j, carry):
        row = ids[j >> 6, 0, j & 63].astype(jnp.int32)
        owner = row >> 6
        at = (owner >> 1) * CARD + (row & 31)
        same = (owner & 1) == mine
        here = own_ref[pl.ds(at, 1), :]
        there = other_ref[pl.ds(at, 1), :]
        rows[pl.ds(j, 1), :] = jnp.where(same, here, there)
        names[pl.ds(j, 1), :] = jnp.full((1, 128), row, jnp.int32)
        return carry

    lax.fori_loop(0, 3 * SLOTS, pick, 0, unroll=16)


def place(pair, q, gathered):
    straight = (sublanes() < 4) == (lanes() < 64)
    tile = jnp.where(straight, pair, pltpu.roll(pltpu.roll(pair, 64, 1), 4, 0))
    high, low = halves(tile)
    gathered[:, q * 128 : (q + 1) * 128] = jnp.concatenate([high, low], axis=0)


def unpack(got_ref, gathered):
    for q in range(PARTS * PART // 128):
        at = 10 * q
        place(jnp.concatenate([got_ref[at : at + 4, :], got_ref[at + 5 : at + 9, :]], axis=0), q, gathered)
    return jnp.sum(got_ref[pl.ds(4, PARTS * PART // SLOTS, stride=5), :], axis=0, keepdims=True)


def partial_solve(weights, gathered, c):
    return lax.dot_general(weights[...], gathered[:, c * PART : (c + 1) * PART], NT, preferred_element_type=F32)


def into_pool(out, maps, pool):
    count = 3 * SLOTS
    sol = out[:count] + out[count:]
    sol = sol.T
    sol = sol[:8] + sol[8:]
    own = sublanes((64, 64)) // 8 == lanes((64, 64)) // 8
    for e, map_ref in enumerate(maps):
        part = sol[:, e * SLOTS : (e + 1) * SLOTS]
        spread = jnp.where(own, jnp.concatenate([part] * COUNT, axis=0), 0.0)
        sh, sl = halves(spread)
        ch, cl = halves(map_ref[...].reshape(SLOTS, WIDTH))
        two = jnp.dot(jnp.concatenate([sh, sl], axis=0), ch, preferred_element_type=F32)
        full = two[:64] + two[64:] + jnp.dot(sh, cl, preferred_element_type=F32)
        for p in range(COUNT):
            for c in range(CHUNKS):
                t = e * TILES + p * CHUNKS + c
                pool[t] = pool[t] + full[p * 8 : (p + 1) * 8, c * 128 : (c + 1) * 128]


def hold_kernel(after_ref, source_ref, held_ref, sems):
    del after_ref
    for copy in fetch(source_ref, held_ref, sems):
        copy.wait()


def keep_kernel(after_ref, weights_ref, kept_ref, sems):
    del after_ref
    copies = [pltpu.make_async_copy(weights_ref.at[c], kept_ref.at[c], sems.at[c]) for c in range(KEEP)]
    for copy in copies:
        copy.start()
    for copy in copies:
        copy.wait()


def coarse_kernel(got_ref, kept_ref, weights_ref, out_ref, sums_ref, gathered, weights, sems):
    copies = [
        pltpu.make_async_copy(weights_ref.at[c], weights.at[c - KEEP], sems.at[c - KEEP]) for c in range(KEEP, PARTS)
    ]
    for copy in copies:
        copy.start()
    sums_ref[...] = jnp.broadcast_to(unpack(got_ref, gathered), (8, 128))
    out = partial_solve(kept_ref.at[0], gathered, 0)
    for c in range(1, PARTS):
        if c >= KEEP:
            copies[c - KEEP].wait()
        out = out + partial_solve(kept_ref.at[c] if c < KEEP else weights.at[c - KEEP], gathered, c)
    out_ref[...] = out


def totals(sums, count):
    lane, sub = lanes(), sublanes()
    row = jnp.broadcast_to(sums, (8, 128))
    return [
        jnp.broadcast_to(jnp.sum(jnp.where(lane == i * 8 + sub, row, 0.0), axis=1, keepdims=True), (8, 128))
        for i in range(count)
    ]


def solve_first_kernel(
    core, table, ia_ref, ix_ref, ib_ref, own_ref, other_ref, am_ref, m_ref, bm_ref, a_ref, x_ref, b_ref, inverse_ref,
    z_ref, u_ref, weights_ref, pool, gathered, weights, held, sems, rows, names, index, ids,
):
    mine = core[0]
    small = [
        pltpu.make_async_copy(ref.at[TILES], ids.at[e], sems.at[COUNT + PARTS + e])
        for e, ref in enumerate((ia_ref, ix_ref, ib_ref))
    ]
    for copy in small:
        copy.start()
    copies = fetch(inverse_ref, held, sems)
    for copy in small:
        copy.wait()
    gather_rows(mine, ids, own_ref, other_ref, rows, names)
    fill_pool(pool, a_ref, x_ref, b_ref)
    chips = PARTS * PART // 128
    own = own_ref[pl.ds(32, chips, stride=CARD), :]
    other = other_ref[pl.ds(32, chips, stride=CARD), :]
    first = jnp.where(mine == 0, own, other)
    second = jnp.where(mine == 0, other, own)
    index[...] = jnp.where(lanes((chips, 128)) < 64, first, pltpu.roll(second, 64, 1)).astype(jnp.int32)
    for q in range(chips):
        at = q * CARD + 33
        own, other = own_ref[at : at + 4, :], other_ref[at : at + 4, :]
        first = jnp.where(mine == 0, own, other)
        second = jnp.where(mine == 0, other, own)
        place(jnp.concatenate([first, second], axis=0), q, gathered)
    upper = (names[...] & 63) >= 32
    kept = jnp.where(upper == (lanes((3 * SLOTS, 128)) >= 64), rows[...], 0.0)
    high, low = halves(kept)
    both = jnp.concatenate([high, low], axis=0)
    names[...] = names[...] >> 6
    spot = sublanes((128, 256)) & 63

    def spread(q, carry):
        row = jnp.concatenate([index[pl.ds(2 * q, 1), :], index[pl.ds(2 * q + 1, 1), :]], axis=1)
        onehot = (spot == (row & 63)).astype(F32).astype(BF16)
        full = jnp.dot(both, onehot, preferred_element_type=F32)
        block = row >> 6
        named = names[...]
        hit = jnp.concatenate([named, named], axis=1) == block
        at = pl.ds(pl.multiple_of((q & 3) * 256, 256), 256)
        weights[q >> 2, 0 : 3 * SLOTS, at] = jnp.where(hit, full[: 3 * SLOTS], 0.0).astype(BF16)
        weights[q >> 2, 3 * SLOTS :, at] = jnp.where(hit, full[3 * SLOTS :], 0.0).astype(BF16)
        return carry

    stores = []
    out = None
    for part in range(PARTS):
        lax.fori_loop(part * 4, part * 4 + 4, spread, 0, unroll=4)
        store = pltpu.make_async_copy(weights.at[part], weights_ref.at[part], sems.at[COUNT + part])
        store.start()
        stores.append(store)
        term = partial_solve(weights.at[part], gathered, part)
        out = term if out is None else out + term
    into_pool(out, (am_ref, m_ref, bm_ref), pool)
    z = [0.5 * t for t in jump(pool, table)]
    for t in range(TILES):
        z_ref[t] = z[t]
    multiply(z, copies, held, u_ref)
    for store in stores:
        store.wait()


def solve_second_kernel(
    table, out_ref, sums_ref, am_ref, m_ref, bm_ref, a_ref, x_ref, b_ref, inverse_ref, r0_ref, z0_ref, w0_ref,
    y_ref, r_ref, z_ref, scale_ref, u_ref, pool,
):
    fill_pool(pool, a_ref, x_ref, b_ref)
    into_pool(out_ref[...], (am_ref, m_ref, bm_ref), pool)
    energy, curve = totals(sums_ref[0:1, :], 2)
    step = energy / curve
    scale_ref[0] = energy
    scale_ref[1] = curve
    scale_ref[2] = step
    y = jump(pool, table)
    z = []
    for t in range(TILES):
        half = 0.5 * y[t]
        y_ref[t] = half
        r_ref[t] = r0_ref[t] - step * w0_ref[t]
        z.append(z0_ref[t] - step * half)
        z_ref[t] = z[t]
    multiply_held(z, inverse_ref, u_ref)


def solve_third_kernel(
    table, out_ref, sums_ref, am_ref, m_ref, bm_ref, a_ref, x_ref, b_ref,
    scale_ref, z0_ref, w0_ref, y0_ref, r1_ref, z1_ref, v1_ref, multipliers_ref, residual_ref, preconditioned_ref,
    pool,
):
    fill_pool(pool, a_ref, x_ref, b_ref)
    into_pool(out_ref[...], (am_ref, m_ref, bm_ref), pool)
    energy, zv, pv, zw = totals(sums_ref[0:1, :], 4)
    first = scale_ref[2]
    grow = energy / scale_ref[0]
    second = energy / (zv + grow * (pv + zw) + grow * grow * scale_ref[1])
    y = jump(pool, table)
    for p in range(COUNT):
        for c in range(CHUNKS):
            t = p * CHUNKS + c
            at = slice(c * 128, (c + 1) * 128)
            multipliers_ref[p, :, at] = first * z0_ref[t] + second * (z1_ref[t] + grow * z0_ref[t])
            residual_ref[p, :, at] = r1_ref[t] - second * (v1_ref[t] + grow * w0_ref[t])
            preconditioned_ref[p, :, at] = z1_ref[t] - second * (0.5 * y[t] + grow * y0_ref[t])


def shards(loads, local_inverse, schur, corner_map, corner_index, partner, coarse_inverse):
    tiles = lax.axis_size("tile")
    devices = lax.axis_size(GT)
    inner_swap = [(i, i ^ 1) for i in range(tiles)]
    outer_swap = [(i, (i - 1) % tiles if i % 2 == 0 else (i + 1) % tiles) for i in range(tiles)]
    same_core = [[2 * i + c for i in range(devices // 2)] for c in range(2)]
    core = lax.axis_index("tile") % 2

    def both(x):
        return lax.ppermute(x, "tile", inner_swap), lax.ppermute(x, "tile", outer_swap)

    field = shape(TILES, 8, 128)
    pool = pltpu.VMEM((3 * TILES, 8, 128), F32)
    gathered = pltpu.VMEM((16, devices * SLOTS), BF16)
    pay = shape(devices * 5, 128)
    sems = pltpu.SemaphoreType.DMA((COUNT,))

    core = core.astype(jnp.int32).reshape(1)
    held = pltpu.VMEM((COUNT, WIDTH, WIDTH), F32)
    solver = pltpu.VMEM((PARTS, 6 * SLOTS, PART), BF16)
    inverse, stiff = in_hbm(local_inverse), in_hbm(schur)
    u, table = call(
        start_kernel,
        [shape(TILES + 1, 8, 128), jax.ShapeDtypeStruct((16, 128), jnp.int32)],
        [SMEM] + [ANY] * 4,
        [
            pltpu.VMEM((COUNT, CASES, WIDTH), F32),
            pltpu.VMEM((COUNT, CORNERS), jnp.int32),
            pltpu.VMEM((COUNT, FACES), jnp.int32),
            held,
            pltpu.SemaphoreType.DMA((COUNT + 3,)),
        ],
        us=4,
    )(core, in_hbm(loads), in_hbm(corner_index), in_hbm(partner), inverse)
    ua, ub = both(u)
    indices = (ua, u, ub)

    def spread(x):
        return lax.all_to_all(x.reshape(devices, -1), GT, 0, 0, tiled=True).reshape(-1, 128)

    def through(x):
        (q,) = call(product_kernel, [field], [VMEM, ANY], [held, sems], us=3)(x, stiff)
        qa, qb = both(q)
        return qa, q, qb

    r0, card = call(send_first_kernel, [field, shape(devices // 2 * CARD, 128)], [SMEM] + [VMEM] * 5, [pool])(
        table, ua, u, ub, corner_map, coarse_inverse
    )
    own_cards = lax.all_to_all(
        card.reshape(devices // 2, -1), GT, 0, 0, tiled=True, axis_index_groups=same_core
    ).reshape(-1, 128)
    pooled = through(r0)
    ma, mb = both(corner_map)
    maps = (ma, corner_map, mb)
    qa, q, qb = pooled
    own_cards, q = lax.optimization_barrier((own_cards, q))
    pooled = (qa, q, qb)
    other_cards = lax.ppermute(own_cards, "tile", inner_swap)
    z0, u, weights = pl.pallas_call(
        solve_first_kernel,
        in_specs=[SMEM] * 2 + [ANY] * 3 + [VMEM] * 8 + [ANY],
        out_specs=[VMEM, VMEM, ANY],
        out_shape=[field, field, pltpu.HBM((PARTS, 6 * SLOTS, PART), BF16)],
        scratch_shapes=[
            pool,
            gathered,
            solver,
            held,
            pltpu.SemaphoreType.DMA((COUNT + PARTS + 3,)),
            pltpu.VMEM((3 * SLOTS, 128), F32),
            pltpu.VMEM((3 * SLOTS, 128), jnp.int32),
            pltpu.VMEM((devices // 2, 128), jnp.int32),
            pltpu.SMEM((3, 8, 128), F32),
        ],
        compiler_params=PARAMS,
        cost_estimate=pl.CostEstimate(flops=4_000_000_000, bytes_accessed=20_000_000, transcendentals=0),
    )(core, table, *indices, own_cards, other_cards, *maps, *pooled, inverse)
    weights = in_hbm(weights)
    rest = pltpu.VMEM((PARTS - KEEP, 6 * SLOTS, PART), BF16)
    kept_shape = jax.ShapeDtypeStruct((KEEP, 6 * SLOTS, PART), BF16)
    coarse_scratch = [gathered, rest, pltpu.SemaphoreType.DMA((PARTS - KEEP,))]

    def hold(after):
        return call(hold_kernel, [shape(COUNT, WIDTH, WIDTH)], [ANY] * 2, [sems], us=2)(after, stiff)[0]

    def keep(after):
        return call(keep_kernel, [kept_shape], [ANY] * 2, [pltpu.SemaphoreType.DMA((KEEP,))], us=2)(after, weights)[0]

    coarse_out = [shape(6 * SLOTS, 16), shape(8, 128)]
    ua, ub = both(u)
    w0, parts, q = call(send_second_kernel, [field, pay, field], [SMEM] + [VMEM] * 7, [pool], us=3)(
        table, ua, u, ub, corner_map, hold(u), r0, z0
    )
    qa, qb = both(q)
    out, sums = call(coarse_kernel, coarse_out, [VMEM, VMEM, ANY], coarse_scratch, us=20)(spread(parts), keep(q), weights)
    y0, r1, z1, scale, u = call(
        solve_second_kernel, [field, field, field, shape(3, 8, 128), field], [SMEM] + [VMEM] * 12, [pool], us=3
    )(table, out, sums, *maps, qa, q, qb, local_inverse, r0, z0, w0)
    ua, ub = both(u)
    v1, parts, q = call(send_third_kernel, [field, pay, field], [SMEM] + [VMEM] * 9, [pool], us=3)(
        table, ua, u, ub, corner_map, hold(u), r1, z1, z0, w0
    )
    qa, qb = both(q)
    out, sums = call(coarse_kernel, coarse_out, [VMEM, VMEM, ANY], coarse_scratch, us=20)(spread(parts), keep(q), weights)
    return tuple(
        call(solve_third_kernel, [shape(COUNT, CASES, WIDTH)] * 3, [SMEM] + [VMEM] * 15, [pool], us=2)(
            table, out, sums, *maps, qa, q, qb, scale, z0, w0, y0, r1, z1, v1
        )
    )


def solution(mesh):
    three = P(GT, None, None)
    two = P(GT, None)
    return jax.shard_map(
        shards,
        mesh=mesh,
        in_specs=(three, three, three, three, two, two, two),
        out_specs=(three, three, three),
        check_vma=False,
    )
```

```python
import jax
import jax.numpy as jnp
from jax import lax
from jax.experimental import pallas as pl
from jax.experimental.pallas import tpu as pltpu
from jax.sharding import PartitionSpec as P

GT = ("group", "tile")
F32 = jnp.float32
BF16 = jnp.bfloat16
NT = (((1,), (1,)), ((), ()))
VMEM = pl.BlockSpec(memory_space=pltpu.VMEM)
SMEM = pl.BlockSpec(memory_space=pltpu.SMEM)
ANY = pl.BlockSpec(memory_space=pl.ANY)
PARAMS = pltpu.CompilerParams(vmem_limit_bytes=24 << 20)

COUNT, CASES, WIDTH, CORNERS, ROWS, FACES = 8, 8, 384, 8, 64, 12
CHUNKS = WIDTH // 128
TILES = COUNT * CHUNKS
SLOTS = COUNT * CORNERS
CARD = 37
PARTS, PART, KEEP = 8, 1024, 2


def call(kernel, outs, specs, scratch=(), us=2):
    return pl.pallas_call(
        kernel,
        in_specs=specs,
        out_specs=[VMEM] * len(outs),
        out_shape=outs,
        scratch_shapes=list(scratch),
        compiler_params=PARAMS,
        cost_estimate=pl.CostEstimate(flops=us * 500_000_000, bytes_accessed=us * 3_000_000, transcendentals=0),
    )


def in_hbm(x):
    return pltpu.with_memory_space_constraint(x, pltpu.HBM)


def shape(*dims):
    return jax.ShapeDtypeStruct(dims, F32)


def halves(x):
    high = x.astype(BF16)
    return high, (x - high.astype(F32)).astype(BF16)


def product(vector, matrix):
    vh, vl = halves(vector)
    mh, ml = halves(matrix)
    first = jnp.dot(jnp.concatenate([vh, vl], 0), mh, preferred_element_type=F32)
    return first[:8] + first[8:] + jnp.dot(vh, ml, preferred_element_type=F32)


def lanes(shape_=(8, 128)):
    return lax.broadcasted_iota(jnp.int32, shape_, 1)


def sublanes(shape_=(8, 128)):
    return lax.broadcasted_iota(jnp.int32, shape_, 0)


def put_tiles(ref, p, row):
    for c in range(CHUNKS):
        ref[p * CHUNKS + c] = row[:, c * 128 : (c + 1) * 128]


def get_row(tiles, p):
    return jnp.concatenate([tiles[p * CHUNKS + c] for c in range(CHUNKS)], axis=1)


def jump(pool, table):
    quarter = lanes() // 32
    out = []
    for t in range(TILES):
        p, c = divmod(t, CHUNKS)
        other = None
        for q in range(4):
            f = c * 4 + q
            face = pltpu.roll(pool[table[p, f]], table[8 + p, f], 1)
            other = face if other is None else jnp.where(quarter == q, face, other)
        out.append(pool[TILES + t] - other)
    return out


def fill_pool(pool, a_ref, x_ref, b_ref):
    for e, ref in enumerate((a_ref, x_ref, b_ref)):
        for t in range(TILES):
            pool[e * TILES + t] = ref[t]


def mate_places(core, partner, table_ref):
    region = (partner >= COUNT * FACES).astype(jnp.int32) + (partner >= 2 * COUNT * FACES).astype(jnp.int32)
    within = partner - region * (COUNT * FACES)
    particle = jnp.zeros_like(within)
    for p in range(1, COUNT):
        particle = particle + (within >= p * FACES).astype(jnp.int32)
    face = within - particle * FACES
    region = jnp.where(core[0] == 1, region, 2 - region)
    table_ref[0:8, 0:FACES] = region * TILES + particle * CHUNKS + (face >> 2)
    table_ref[8:16, 0:FACES] = ((lanes((COUNT, FACES)) - face) & 3) * 32


def index_row(index):
    wide = jnp.concatenate([index.astype(F32)] * 16, axis=1)
    keep = lanes() // 8 == sublanes()
    return jnp.broadcast_to(jnp.sum(jnp.where(keep, wide, 0.0), axis=0, keepdims=True), (8, 128))


def copies_of(source, held, sems, first=0):
    return [pltpu.make_async_copy(source.at[i], held.at[i], sems.at[first + i]) for i in range(source.shape[0])]


def fetch(source, held, sems, first=0):
    copies = copies_of(source, held, sems, first)
    for copy in copies:
        copy.start()
    return copies


def multiply(x, copies, held, out_ref):
    for p in range(COUNT):
        copies[p].wait()
        put_tiles(out_ref, p, product(get_row(x, p), held[p]))


def start_kernel(
    core, loads_ref, index_ref, partner_ref, inverse_ref, out_ref, table_ref, loads, index, partner, held, sems
):
    small = [
        pltpu.make_async_copy(source, to, sems.at[COUNT + i])
        for i, (source, to) in enumerate(((loads_ref, loads), (index_ref, index), (partner_ref, partner)))
    ]
    for copy in small:
        copy.start()
    copies = fetch(inverse_ref, held, sems)
    for copy in small:
        copy.wait()
    out_ref[TILES] = index_row(index[...])
    mate_places(core, partner[...], table_ref)
    for p in range(COUNT):
        copies[p].wait()
        put_tiles(out_ref, p, product(loads[p], held[p]))


def product_kernel(x_ref, matrix_ref, out_ref, held, sems):
    copies = fetch(matrix_ref, held, sems)
    multiply(x_ref, copies, held, out_ref)


def column_to_row(columns):
    lane, sub = lanes(), sublanes()
    row = jnp.zeros((8, 128), F32)
    for i, column in enumerate(columns):
        row = jnp.where(lane == i * 8 + sub, jnp.broadcast_to(column, (8, 128)), row)
    return jnp.sum(row, axis=0, keepdims=True)


def case_sum(first, second):
    total = first[0] * second[0]
    for t in range(1, TILES):
        total = total + first[t] * second[t]
    return jnp.sum(total, axis=1, keepdims=True)


def contributions(r, map_ref):
    lane = lanes()
    contrib = jnp.zeros((8, 128), F32)
    for p in range(COUNT):
        for j in range(CORNERS):
            part = r[p * CHUNKS] * map_ref[p, j : j + 1, 0:128]
            for c in range(1, CHUNKS):
                part = part + r[p * CHUNKS + c] * map_ref[p, j : j + 1, c * 128 : (c + 1) * 128]
            total = jnp.sum(part, axis=1, keepdims=True)
            contrib = jnp.where(lane == p * CORNERS + j, jnp.broadcast_to(total, (8, 128)), contrib)
    turned = pltpu.roll(pltpu.roll(contrib, 64, 1), 4, 0)
    return jnp.where(lane < 64, contrib, turned)


def send(r, map_ref, columns, pay_ref):
    pay = contributions(r, map_ref)
    pay = jnp.where(sublanes() < 4, pay, jnp.broadcast_to(column_to_row(columns), (8, 128)))[0:5]
    for at in range(0, pay_ref.shape[0], 5):
        pay_ref[at : at + 5, :] = pay


def send_first_kernel(table, a_ref, x_ref, b_ref, map_ref, inverse_ref, r_ref, card_ref, pool):
    fill_pool(pool, a_ref, x_ref, b_ref)
    r = jump(pool, table)
    for t in range(TILES):
        r_ref[t] = r[t]
    inverse = inverse_ref[...]
    pay = contributions(r, map_ref)
    card = jnp.concatenate([inverse[:32], inverse[32:]], axis=1)
    tail = jnp.where(sublanes() < 1, x_ref[TILES], pltpu.roll(pay, 1, 0))[0:5]
    for at in range(0, card_ref.shape[0], CARD):
        card_ref[at : at + 32, :] = card
        card_ref[at + 32 : at + CARD, :] = tail


def multiply_held(x, matrix_ref, out_ref):
    for p in range(COUNT):
        put_tiles(out_ref, p, product(get_row(x, p), matrix_ref[p]))


def send_second_kernel(table, a_ref, x_ref, b_ref, map_ref, schur_ref, r0_ref, z0_ref, w_ref, pay_ref, q_ref, pool):
    fill_pool(pool, a_ref, x_ref, b_ref)
    w = jump(pool, table)
    for t in range(TILES):
        w_ref[t] = w[t]
    send(w, map_ref, [case_sum(r0_ref, z0_ref), case_sum(z0_ref, w)], pay_ref)
    multiply_held(w, schur_ref, q_ref)


def send_third_kernel(
    table, a_ref, x_ref, b_ref, map_ref, schur_ref, r1_ref, z1_ref, z0_ref, w0_ref, v_ref, pay_ref, q_ref, pool
):
    fill_pool(pool, a_ref, x_ref, b_ref)
    v = jump(pool, table)
    for t in range(TILES):
        v_ref[t] = v[t]
    columns = [case_sum(r1_ref, z1_ref), case_sum(z1_ref, v), case_sum(z0_ref, v), case_sum(z1_ref, w0_ref)]
    send(v, map_ref, columns, pay_ref)
    multiply_held(v, schur_ref, q_ref)


def gather_rows(mine, ids, own_ref, other_ref, rows, names):
    def pick(j, carry):
        row = ids[j >> 6, 0, j & 63].astype(jnp.int32)
        owner = row >> 6
        at = (owner >> 1) * CARD + (row & 31)
        same = (owner & 1) == mine
        here = own_ref[pl.ds(at, 1), :]
        there = other_ref[pl.ds(at, 1), :]
        rows[pl.ds(j, 1), :] = jnp.where(same, here, there)
        names[pl.ds(j, 1), :] = jnp.full((1, 128), row, jnp.int32)
        return carry

    lax.fori_loop(0, 3 * SLOTS, pick, 0, unroll=16)


def place(pair, q, gathered):
    straight = (sublanes() < 4) == (lanes() < 64)
    tile = jnp.where(straight, pair, pltpu.roll(pltpu.roll(pair, 64, 1), 4, 0))
    high, low = halves(tile)
    gathered[:, q * 128 : (q + 1) * 128] = jnp.concatenate([high, low], axis=0)


def unpack(got_ref, gathered):
    for q in range(PARTS * PART // 128):
        at = 10 * q
        place(jnp.concatenate([got_ref[at : at + 4, :], got_ref[at + 5 : at + 9, :]], axis=0), q, gathered)
    return jnp.sum(got_ref[pl.ds(4, PARTS * PART // SLOTS, stride=5), :], axis=0, keepdims=True)


def partial_solve(weights, gathered, c):
    return lax.dot_general(weights[...], gathered[:, c * PART : (c + 1) * PART], NT, preferred_element_type=F32)


def into_pool(out, maps, pool):
    count = 3 * SLOTS
    sol = out[:count] + out[count:]
    sol = sol.T
    sol = sol[:8] + sol[8:]
    own = sublanes((64, 64)) // 8 == lanes((64, 64)) // 8
    for e, map_ref in enumerate(maps):
        part = sol[:, e * SLOTS : (e + 1) * SLOTS]
        spread = jnp.where(own, jnp.concatenate([part] * COUNT, axis=0), 0.0)
        sh, sl = halves(spread)
        ch, cl = halves(map_ref[...].reshape(SLOTS, WIDTH))
        two = jnp.dot(jnp.concatenate([sh, sl], axis=0), ch, preferred_element_type=F32)
        full = two[:64] + two[64:] + jnp.dot(sh, cl, preferred_element_type=F32)
        for p in range(COUNT):
            for c in range(CHUNKS):
                t = e * TILES + p * CHUNKS + c
                pool[t] = pool[t] + full[p * 8 : (p + 1) * 8, c * 128 : (c + 1) * 128]


def hold_kernel(after_ref, source_ref, held_ref, sems):
    del after_ref
    for copy in fetch(source_ref, held_ref, sems):
        copy.wait()


def keep_kernel(after_ref, weights_ref, kept_ref, sems):
    del after_ref
    copies = [pltpu.make_async_copy(weights_ref.at[c], kept_ref.at[c], sems.at[c]) for c in range(KEEP)]
    for copy in copies:
        copy.start()
    for copy in copies:
        copy.wait()


def coarse_kernel(got_ref, kept_ref, weights_ref, out_ref, sums_ref, gathered, weights, sems):
    copies = [
        pltpu.make_async_copy(weights_ref.at[c], weights.at[c - KEEP], sems.at[c - KEEP]) for c in range(KEEP, PARTS)
    ]
    for copy in copies:
        copy.start()
    sums_ref[...] = jnp.broadcast_to(unpack(got_ref, gathered), (8, 128))
    out = partial_solve(kept_ref.at[0], gathered, 0)
    for c in range(1, PARTS):
        if c >= KEEP:
            copies[c - KEEP].wait()
        out = out + partial_solve(kept_ref.at[c] if c < KEEP else weights.at[c - KEEP], gathered, c)
    out_ref[...] = out


def totals(sums, count):
    lane, sub = lanes(), sublanes()
    row = jnp.broadcast_to(sums, (8, 128))
    return [
        jnp.broadcast_to(jnp.sum(jnp.where(lane == i * 8 + sub, row, 0.0), axis=1, keepdims=True), (8, 128))
        for i in range(count)
    ]


def solve_first_kernel(
    core, table, ia_ref, ix_ref, ib_ref, own_ref, other_ref, am_ref, m_ref, bm_ref, a_ref, x_ref, b_ref, inverse_ref,
    z_ref, u_ref, weights_ref, pool, gathered, weights, held, sems, rows, names, index, ids,
):
    mine = core[0]
    small = [
        pltpu.make_async_copy(ref.at[TILES], ids.at[e], sems.at[COUNT + PARTS + e])
        for e, ref in enumerate((ia_ref, ix_ref, ib_ref))
    ]
    for copy in small:
        copy.start()
    copies = fetch(inverse_ref, held, sems)
    for copy in small:
        copy.wait()
    gather_rows(mine, ids, own_ref, other_ref, rows, names)
    fill_pool(pool, a_ref, x_ref, b_ref)
    chips = PARTS * PART // 128
    own = own_ref[pl.ds(32, chips, stride=CARD), :]
    other = other_ref[pl.ds(32, chips, stride=CARD), :]
    first = jnp.where(mine == 0, own, other)
    second = jnp.where(mine == 0, other, own)
    index[...] = jnp.where(lanes((chips, 128)) < 64, first, pltpu.roll(second, 64, 1)).astype(jnp.int32)
    for q in range(chips):
        at = q * CARD + 33
        own, other = own_ref[at : at + 4, :], other_ref[at : at + 4, :]
        first = jnp.where(mine == 0, own, other)
        second = jnp.where(mine == 0, other, own)
        place(jnp.concatenate([first, second], axis=0), q, gathered)
    upper = (names[...] & 63) >= 32
    kept = jnp.where(upper == (lanes((3 * SLOTS, 128)) >= 64), rows[...], 0.0)
    high, low = halves(kept)
    both = jnp.concatenate([high, low], axis=0)
    names[...] = names[...] >> 6
    spot = sublanes((128, 256)) & 63

    def spread(q, carry):
        row = jnp.concatenate([index[pl.ds(2 * q, 1), :], index[pl.ds(2 * q + 1, 1), :]], axis=1)
        onehot = (spot == (row & 63)).astype(F32).astype(BF16)
        full = jnp.dot(both, onehot, preferred_element_type=F32)
        block = row >> 6
        named = names[...]
        hit = jnp.concatenate([named, named], axis=1) == block
        at = pl.ds(pl.multiple_of((q & 3) * 256, 256), 256)
        weights[q >> 2, 0 : 3 * SLOTS, at] = jnp.where(hit, full[: 3 * SLOTS], 0.0).astype(BF16)
        weights[q >> 2, 3 * SLOTS :, at] = jnp.where(hit, full[3 * SLOTS :], 0.0).astype(BF16)
        return carry

    stores = []
    out = None
    for part in range(PARTS):
        lax.fori_loop(part * 4, part * 4 + 4, spread, 0, unroll=4)
        store = pltpu.make_async_copy(weights.at[part], weights_ref.at[part], sems.at[COUNT + part])
        store.start()
        stores.append(store)
        term = partial_solve(weights.at[part], gathered, part)
        out = term if out is None else out + term
    into_pool(out, (am_ref, m_ref, bm_ref), pool)
    z = [0.5 * t for t in jump(pool, table)]
    for t in range(TILES):
        z_ref[t] = z[t]
    multiply(z, copies, held, u_ref)
    for store in stores:
        store.wait()


def solve_second_kernel(
    table, out_ref, sums_ref, am_ref, m_ref, bm_ref, a_ref, x_ref, b_ref, inverse_ref, r0_ref, z0_ref, w0_ref,
    y_ref, r_ref, z_ref, scale_ref, u_ref, pool,
):
    fill_pool(pool, a_ref, x_ref, b_ref)
    into_pool(out_ref[...], (am_ref, m_ref, bm_ref), pool)
    energy, curve = totals(sums_ref[0:1, :], 2)
    step = energy / curve
    scale_ref[0] = energy
    scale_ref[1] = curve
    scale_ref[2] = step
    y = jump(pool, table)
    z = []
    for t in range(TILES):
        half = 0.5 * y[t]
        y_ref[t] = half
        r_ref[t] = r0_ref[t] - step * w0_ref[t]
        z.append(z0_ref[t] - step * half)
        z_ref[t] = z[t]
    multiply_held(z, inverse_ref, u_ref)


def solve_third_kernel(
    table, out_ref, sums_ref, am_ref, m_ref, bm_ref, a_ref, x_ref, b_ref,
    scale_ref, z0_ref, w0_ref, y0_ref, r1_ref, z1_ref, v1_ref, multipliers_ref, residual_ref, preconditioned_ref,
    pool,
):
    fill_pool(pool, a_ref, x_ref, b_ref)
    into_pool(out_ref[...], (am_ref, m_ref, bm_ref), pool)
    energy, zv, pv, zw = totals(sums_ref[0:1, :], 4)
    first = scale_ref[2]
    grow = energy / scale_ref[0]
    second = energy / (zv + grow * (pv + zw) + grow * grow * scale_ref[1])
    y = jump(pool, table)
    for p in range(COUNT):
        for c in range(CHUNKS):
            t = p * CHUNKS + c
            at = slice(c * 128, (c + 1) * 128)
            multipliers_ref[p, :, at] = first * z0_ref[t] + second * (z1_ref[t] + grow * z0_ref[t])
            residual_ref[p, :, at] = r1_ref[t] - second * (v1_ref[t] + grow * w0_ref[t])
            preconditioned_ref[p, :, at] = z1_ref[t] - second * (0.5 * y[t] + grow * y0_ref[t])


def shards(loads, local_inverse, schur, corner_map, corner_index, partner, coarse_inverse):
    tiles = lax.axis_size("tile")
    devices = lax.axis_size(GT)
    inner_swap = [(i, i ^ 1) for i in range(tiles)]
    outer_swap = [(i, (i - 1) % tiles if i % 2 == 0 else (i + 1) % tiles) for i in range(tiles)]
    same_core = [[2 * i + c for i in range(devices // 2)] for c in range(2)]
    core = lax.axis_index("tile") % 2

    def both(x):
        return lax.ppermute(x, "tile", inner_swap), lax.ppermute(x, "tile", outer_swap)

    field = shape(TILES, 8, 128)
    pool = pltpu.VMEM((3 * TILES, 8, 128), F32)
    gathered = pltpu.VMEM((16, devices * SLOTS), BF16)
    pay = shape(devices * 5, 128)
    sems = pltpu.SemaphoreType.DMA((COUNT,))

    core = core.astype(jnp.int32).reshape(1)
    held = pltpu.VMEM((COUNT, WIDTH, WIDTH), F32)
    solver = pltpu.VMEM((PARTS, 6 * SLOTS, PART), BF16)
    inverse, stiff = in_hbm(local_inverse), in_hbm(schur)
    u, table = call(
        start_kernel,
        [shape(TILES + 1, 8, 128), jax.ShapeDtypeStruct((16, 128), jnp.int32)],
        [SMEM] + [ANY] * 4,
        [
            pltpu.VMEM((COUNT, CASES, WIDTH), F32),
            pltpu.VMEM((COUNT, CORNERS), jnp.int32),
            pltpu.VMEM((COUNT, FACES), jnp.int32),
            held,
            pltpu.SemaphoreType.DMA((COUNT + 3,)),
        ],
        us=4,
    )(core, in_hbm(loads), in_hbm(corner_index), in_hbm(partner), inverse)
    ua, ub = both(u)
    indices = (ua, u, ub)

    def spread(x):
        return lax.all_to_all(x.reshape(devices, -1), GT, 0, 0, tiled=True).reshape(-1, 128)

    def through(x):
        (q,) = call(product_kernel, [field], [VMEM, ANY], [held, sems], us=3)(x, stiff)
        qa, qb = both(q)
        return qa, q, qb

    r0, card = call(send_first_kernel, [field, shape(devices // 2 * CARD, 128)], [SMEM] + [VMEM] * 5, [pool])(
        table, ua, u, ub, corner_map, coarse_inverse
    )
    own_cards = lax.all_to_all(
        card.reshape(devices // 2, -1), GT, 0, 0, tiled=True, axis_index_groups=same_core
    ).reshape(-1, 128)
    pooled = through(r0)
    ma, mb = both(corner_map)
    maps = (ma, corner_map, mb)
    own_cards, pooled, maps = lax.optimization_barrier((own_cards, pooled, maps))
    other_cards = lax.ppermute(own_cards, "tile", inner_swap)
    z0, u, weights = pl.pallas_call(
        solve_first_kernel,
        in_specs=[SMEM] * 2 + [ANY] * 3 + [VMEM] * 8 + [ANY],
        out_specs=[VMEM, VMEM, ANY],
        out_shape=[field, field, pltpu.HBM((PARTS, 6 * SLOTS, PART), BF16)],
        scratch_shapes=[
            pool,
            gathered,
            solver,
            held,
            pltpu.SemaphoreType.DMA((COUNT + PARTS + 3,)),
            pltpu.VMEM((3 * SLOTS, 128), F32),
            pltpu.VMEM((3 * SLOTS, 128), jnp.int32),
            pltpu.VMEM((devices // 2, 128), jnp.int32),
            pltpu.SMEM((3, 8, 128), F32),
        ],
        compiler_params=PARAMS,
        cost_estimate=pl.CostEstimate(flops=4_000_000_000, bytes_accessed=20_000_000, transcendentals=0),
    )(core, table, *indices, own_cards, other_cards, *maps, *pooled, inverse)
    weights = in_hbm(weights)
    rest = pltpu.VMEM((PARTS - KEEP, 6 * SLOTS, PART), BF16)
    kept_shape = jax.ShapeDtypeStruct((KEEP, 6 * SLOTS, PART), BF16)
    coarse_scratch = [gathered, rest, pltpu.SemaphoreType.DMA((PARTS - KEEP,))]

    def hold(after):
        return call(hold_kernel, [shape(COUNT, WIDTH, WIDTH)], [ANY] * 2, [sems], us=2)(after, stiff)[0]

    def keep(after):
        return call(keep_kernel, [kept_shape], [ANY] * 2, [pltpu.SemaphoreType.DMA((KEEP,))], us=2)(after, weights)[0]

    coarse_out = [shape(6 * SLOTS, 16), shape(8, 128)]
    ua, ub = both(u)
    w0, parts, q = call(send_second_kernel, [field, pay, field], [SMEM] + [VMEM] * 7, [pool], us=3)(
        table, ua, u, ub, corner_map, hold(u), r0, z0
    )
    qa, qb = both(q)
    out, sums = call(coarse_kernel, coarse_out, [VMEM, VMEM, ANY], coarse_scratch, us=20)(spread(parts), keep(q), weights)
    y0, r1, z1, scale, u = call(
        solve_second_kernel, [field, field, field, shape(3, 8, 128), field], [SMEM] + [VMEM] * 12, [pool], us=3
    )(table, out, sums, *maps, qa, q, qb, local_inverse, r0, z0, w0)
    ua, ub = both(u)
    v1, parts, q = call(send_third_kernel, [field, pay, field], [SMEM] + [VMEM] * 9, [pool], us=3)(
        table, ua, u, ub, corner_map, hold(u), r1, z1, z0, w0
    )
    qa, qb = both(q)
    out, sums = call(coarse_kernel, coarse_out, [VMEM, VMEM, ANY], coarse_scratch, us=20)(spread(parts), keep(q), weights)
    return tuple(
        call(solve_third_kernel, [shape(COUNT, CASES, WIDTH)] * 3, [SMEM] + [VMEM] * 15, [pool], us=2)(
            table, out, sums, *maps, qa, q, qb, scale, z0, w0, y0, r1, z1, v1
        )
    )


def solution(mesh):
    three = P(GT, None, None)
    two = P(GT, None)
    return jax.shard_map(
        shards,
        mesh=mesh,
        in_specs=(three, three, three, three, two, two, two),
        out_specs=(three, three, three),
        check_vma=False,
    )
```

```python
import jax
import jax.numpy as jnp
from jax import lax
from jax.experimental import pallas as pl
from jax.experimental.pallas import tpu as pltpu
from jax.sharding import PartitionSpec as P

GT = ("group", "tile")
F32 = jnp.float32
BF16 = jnp.bfloat16
NT = (((1,), (1,)), ((), ()))
VMEM = pl.BlockSpec(memory_space=pltpu.VMEM)
SMEM = pl.BlockSpec(memory_space=pltpu.SMEM)
ANY = pl.BlockSpec(memory_space=pl.ANY)
PARAMS = pltpu.CompilerParams(vmem_limit_bytes=24 << 20)

COUNT, CASES, WIDTH, CORNERS, ROWS, FACES = 8, 8, 384, 8, 64, 12
CHUNKS = WIDTH // 128
TILES = COUNT * CHUNKS
SLOTS = COUNT * CORNERS
CARD = 37
PARTS, PART, KEEP = 8, 1024, 3


def call(kernel, outs, specs, scratch=(), us=2):
    return pl.pallas_call(
        kernel,
        in_specs=specs,
        out_specs=[VMEM] * len(outs),
        out_shape=outs,
        scratch_shapes=list(scratch),
        compiler_params=PARAMS,
        cost_estimate=pl.CostEstimate(flops=us * 500_000_000, bytes_accessed=us * 3_000_000, transcendentals=0),
    )


def in_hbm(x):
    return pltpu.with_memory_space_constraint(x, pltpu.HBM)


def shape(*dims):
    return jax.ShapeDtypeStruct(dims, F32)


def halves(x):
    high = x.astype(BF16)
    return high, (x - high.astype(F32)).astype(BF16)


def product(vector, matrix):
    vh, vl = halves(vector)
    mh, ml = halves(matrix)
    first = jnp.dot(jnp.concatenate([vh, vl], 0), mh, preferred_element_type=F32)
    return first[:8] + first[8:] + jnp.dot(vh, ml, preferred_element_type=F32)


def lanes(shape_=(8, 128)):
    return lax.broadcasted_iota(jnp.int32, shape_, 1)


def sublanes(shape_=(8, 128)):
    return lax.broadcasted_iota(jnp.int32, shape_, 0)


def put_tiles(ref, p, row):
    for c in range(CHUNKS):
        ref[p * CHUNKS + c] = row[:, c * 128 : (c + 1) * 128]


def get_row(tiles, p):
    return jnp.concatenate([tiles[p * CHUNKS + c] for c in range(CHUNKS)], axis=1)


def jump(pool, table):
    quarter = lanes() // 32
    out = []
    for t in range(TILES):
        p, c = divmod(t, CHUNKS)
        other = None
        for q in range(4):
            f = c * 4 + q
            face = pltpu.roll(pool[table[p, f]], table[8 + p, f], 1)
            other = face if other is None else jnp.where(quarter == q, face, other)
        out.append(pool[TILES + t] - other)
    return out


def fill_pool(pool, a_ref, x_ref, b_ref):
    for e, ref in enumerate((a_ref, x_ref, b_ref)):
        for t in range(TILES):
            pool[e * TILES + t] = ref[t]


def mate_places(core, partner, table_ref):
    region = (partner >= COUNT * FACES).astype(jnp.int32) + (partner >= 2 * COUNT * FACES).astype(jnp.int32)
    within = partner - region * (COUNT * FACES)
    particle = jnp.zeros_like(within)
    for p in range(1, COUNT):
        particle = particle + (within >= p * FACES).astype(jnp.int32)
    face = within - particle * FACES
    region = jnp.where(core[0] == 1, region, 2 - region)
    table_ref[0:8, 0:FACES] = region * TILES + particle * CHUNKS + (face >> 2)
    table_ref[8:16, 0:FACES] = ((lanes((COUNT, FACES)) - face) & 3) * 32


def index_row(index):
    wide = jnp.concatenate([index.astype(F32)] * 16, axis=1)
    keep = lanes() // 8 == sublanes()
    return jnp.broadcast_to(jnp.sum(jnp.where(keep, wide, 0.0), axis=0, keepdims=True), (8, 128))


def copies_of(source, held, sems, first=0):
    return [pltpu.make_async_copy(source.at[i], held.at[i], sems.at[first + i]) for i in range(source.shape[0])]


def fetch(source, held, sems, first=0):
    copies = copies_of(source, held, sems, first)
    for copy in copies:
        copy.start()
    return copies


def multiply(x, copies, held, out_ref):
    for p in range(COUNT):
        copies[p].wait()
        put_tiles(out_ref, p, product(get_row(x, p), held[p]))


def start_kernel(
    core, loads_ref, index_ref, partner_ref, inverse_ref, out_ref, table_ref, loads, index, partner, held, sems
):
    small = [
        pltpu.make_async_copy(source, to, sems.at[COUNT + i])
        for i, (source, to) in enumerate(((loads_ref, loads), (index_ref, index), (partner_ref, partner)))
    ]
    for copy in small:
        copy.start()
    copies = fetch(inverse_ref, held, sems)
    for copy in small:
        copy.wait()
    out_ref[TILES] = index_row(index[...])
    mate_places(core, partner[...], table_ref)
    for p in range(COUNT):
        copies[p].wait()
        put_tiles(out_ref, p, product(loads[p], held[p]))


def product_kernel(x_ref, matrix_ref, out_ref, held, sems):
    copies = fetch(matrix_ref, held, sems)
    multiply(x_ref, copies, held, out_ref)


def column_to_row(columns):
    lane, sub = lanes(), sublanes()
    row = jnp.zeros((8, 128), F32)
    for i, column in enumerate(columns):
        row = jnp.where(lane == i * 8 + sub, jnp.broadcast_to(column, (8, 128)), row)
    return jnp.sum(row, axis=0, keepdims=True)


def case_sum(first, second):
    total = first[0] * second[0]
    for t in range(1, TILES):
        total = total + first[t] * second[t]
    return jnp.sum(total, axis=1, keepdims=True)


def contributions(r, map_ref):
    lane = lanes()
    contrib = jnp.zeros((8, 128), F32)
    for p in range(COUNT):
        for j in range(CORNERS):
            part = r[p * CHUNKS] * map_ref[p, j : j + 1, 0:128]
            for c in range(1, CHUNKS):
                part = part + r[p * CHUNKS + c] * map_ref[p, j : j + 1, c * 128 : (c + 1) * 128]
            total = jnp.sum(part, axis=1, keepdims=True)
            contrib = jnp.where(lane == p * CORNERS + j, jnp.broadcast_to(total, (8, 128)), contrib)
    turned = pltpu.roll(pltpu.roll(contrib, 64, 1), 4, 0)
    return jnp.where(lane < 64, contrib, turned)


def send(r, map_ref, columns, pay_ref):
    pay = contributions(r, map_ref)
    pay = jnp.where(sublanes() < 4, pay, jnp.broadcast_to(column_to_row(columns), (8, 128)))[0:5]
    for at in range(0, pay_ref.shape[0], 5):
        pay_ref[at : at + 5, :] = pay


def send_first_kernel(table, a_ref, x_ref, b_ref, map_ref, inverse_ref, r_ref, card_ref, pool):
    fill_pool(pool, a_ref, x_ref, b_ref)
    r = jump(pool, table)
    for t in range(TILES):
        r_ref[t] = r[t]
    inverse = inverse_ref[...]
    pay = contributions(r, map_ref)
    card = jnp.concatenate([inverse[:32], inverse[32:]], axis=1)
    tail = jnp.where(sublanes() < 1, x_ref[TILES], pltpu.roll(pay, 1, 0))[0:5]
    for at in range(0, card_ref.shape[0], CARD):
        card_ref[at : at + 32, :] = card
        card_ref[at + 32 : at + CARD, :] = tail


def multiply_held(x, matrix_ref, out_ref):
    for p in range(COUNT):
        put_tiles(out_ref, p, product(get_row(x, p), matrix_ref[p]))


def send_second_kernel(table, a_ref, x_ref, b_ref, map_ref, schur_ref, r0_ref, z0_ref, w_ref, pay_ref, q_ref, pool):
    fill_pool(pool, a_ref, x_ref, b_ref)
    w = jump(pool, table)
    for t in range(TILES):
        w_ref[t] = w[t]
    send(w, map_ref, [case_sum(r0_ref, z0_ref), case_sum(z0_ref, w)], pay_ref)
    multiply_held(w, schur_ref, q_ref)


def send_third_kernel(
    table, a_ref, x_ref, b_ref, map_ref, schur_ref, r1_ref, z1_ref, z0_ref, w0_ref, v_ref, pay_ref, q_ref, pool
):
    fill_pool(pool, a_ref, x_ref, b_ref)
    v = jump(pool, table)
    for t in range(TILES):
        v_ref[t] = v[t]
    columns = [case_sum(r1_ref, z1_ref), case_sum(z1_ref, v), case_sum(z0_ref, v), case_sum(z1_ref, w0_ref)]
    send(v, map_ref, columns, pay_ref)
    multiply_held(v, schur_ref, q_ref)


def gather_rows(mine, ids, own_ref, other_ref, rows, names):
    def pick(j, carry):
        row = ids[j >> 6, 0, j & 63].astype(jnp.int32)
        owner = row >> 6
        at = (owner >> 1) * CARD + (row & 31)
        same = (owner & 1) == mine
        here = own_ref[pl.ds(at, 1), :]
        there = other_ref[pl.ds(at, 1), :]
        rows[pl.ds(j, 1), :] = jnp.where(same, here, there)
        names[pl.ds(j, 1), :] = jnp.full((1, 128), row, jnp.int32)
        return carry

    lax.fori_loop(0, 3 * SLOTS, pick, 0, unroll=16)


def place(pair, q, gathered):
    straight = (sublanes() < 4) == (lanes() < 64)
    tile = jnp.where(straight, pair, pltpu.roll(pltpu.roll(pair, 64, 1), 4, 0))
    high, low = halves(tile)
    gathered[:, q * 128 : (q + 1) * 128] = jnp.concatenate([high, low], axis=0)


def unpack(got_ref, gathered):
    for q in range(PARTS * PART // 128):
        at = 10 * q
        place(jnp.concatenate([got_ref[at : at + 4, :], got_ref[at + 5 : at + 9, :]], axis=0), q, gathered)
    return jnp.sum(got_ref[pl.ds(4, PARTS * PART // SLOTS, stride=5), :], axis=0, keepdims=True)


def partial_solve(weights, gathered, c):
    return lax.dot_general(weights[...], gathered[:, c * PART : (c + 1) * PART], NT, preferred_element_type=F32)


def into_pool(out, maps, pool):
    count = 3 * SLOTS
    sol = out[:count] + out[count:]
    sol = sol.T
    sol = sol[:8] + sol[8:]
    own = sublanes((64, 64)) // 8 == lanes((64, 64)) // 8
    for e, map_ref in enumerate(maps):
        part = sol[:, e * SLOTS : (e + 1) * SLOTS]
        spread = jnp.where(own, jnp.concatenate([part] * COUNT, axis=0), 0.0)
        sh, sl = halves(spread)
        ch, cl = halves(map_ref[...].reshape(SLOTS, WIDTH))
        two = jnp.dot(jnp.concatenate([sh, sl], axis=0), ch, preferred_element_type=F32)
        full = two[:64] + two[64:] + jnp.dot(sh, cl, preferred_element_type=F32)
        for p in range(COUNT):
            for c in range(CHUNKS):
                t = e * TILES + p * CHUNKS + c
                pool[t] = pool[t] + full[p * 8 : (p + 1) * 8, c * 128 : (c + 1) * 128]


def hold_kernel(after_ref, source_ref, held_ref, sems):
    del after_ref
    for copy in fetch(source_ref, held_ref, sems):
        copy.wait()


def keep_kernel(after_ref, weights_ref, kept_ref, sems):
    del after_ref
    copies = [pltpu.make_async_copy(weights_ref.at[c], kept_ref.at[c], sems.at[c]) for c in range(KEEP)]
    for copy in copies:
        copy.start()
    for copy in copies:
        copy.wait()


def coarse_kernel(got_ref, kept_ref, weights_ref, out_ref, sums_ref, gathered, weights, sems):
    copies = [
        pltpu.make_async_copy(weights_ref.at[c], weights.at[c - KEEP], sems.at[c - KEEP]) for c in range(KEEP, PARTS)
    ]
    for copy in copies:
        copy.start()
    sums_ref[...] = jnp.broadcast_to(unpack(got_ref, gathered), (8, 128))
    out = partial_solve(kept_ref.at[0], gathered, 0)
    for c in range(1, PARTS):
        if c >= KEEP:
            copies[c - KEEP].wait()
        out = out + partial_solve(kept_ref.at[c] if c < KEEP else weights.at[c - KEEP], gathered, c)
    out_ref[...] = out


def totals(sums, count):
    lane, sub = lanes(), sublanes()
    row = jnp.broadcast_to(sums, (8, 128))
    return [
        jnp.broadcast_to(jnp.sum(jnp.where(lane == i * 8 + sub, row, 0.0), axis=1, keepdims=True), (8, 128))
        for i in range(count)
    ]


def solve_first_kernel(
    core, table, ia_ref, ix_ref, ib_ref, own_ref, other_ref, am_ref, m_ref, bm_ref, a_ref, x_ref, b_ref, inverse_ref,
    z_ref, u_ref, weights_ref, pool, gathered, weights, held, sems, rows, names, index, ids,
):
    mine = core[0]
    small = [
        pltpu.make_async_copy(ref.at[TILES], ids.at[e], sems.at[COUNT + PARTS + e])
        for e, ref in enumerate((ia_ref, ix_ref, ib_ref))
    ]
    for copy in small:
        copy.start()
    copies = fetch(inverse_ref, held, sems)
    for copy in small:
        copy.wait()
    gather_rows(mine, ids, own_ref, other_ref, rows, names)
    fill_pool(pool, a_ref, x_ref, b_ref)
    chips = PARTS * PART // 128
    own = own_ref[pl.ds(32, chips, stride=CARD), :]
    other = other_ref[pl.ds(32, chips, stride=CARD), :]
    first = jnp.where(mine == 0, own, other)
    second = jnp.where(mine == 0, other, own)
    index[...] = jnp.where(lanes((chips, 128)) < 64, first, pltpu.roll(second, 64, 1)).astype(jnp.int32)
    for q in range(chips):
        at = q * CARD + 33
        own, other = own_ref[at : at + 4, :], other_ref[at : at + 4, :]
        first = jnp.where(mine == 0, own, other)
        second = jnp.where(mine == 0, other, own)
        place(jnp.concatenate([first, second], axis=0), q, gathered)
    upper = (names[...] & 63) >= 32
    kept = jnp.where(upper == (lanes((3 * SLOTS, 128)) >= 64), rows[...], 0.0)
    high, low = halves(kept)
    both = jnp.concatenate([high, low], axis=0)
    names[...] = names[...] >> 6
    spot = sublanes((128, 256)) & 63

    def spread(q, carry):
        row = jnp.concatenate([index[pl.ds(2 * q, 1), :], index[pl.ds(2 * q + 1, 1), :]], axis=1)
        onehot = (spot == (row & 63)).astype(F32).astype(BF16)
        full = jnp.dot(both, onehot, preferred_element_type=F32)
        block = row >> 6
        named = names[...]
        hit = jnp.concatenate([named, named], axis=1) == block
        at = pl.ds(pl.multiple_of((q & 3) * 256, 256), 256)
        weights[q >> 2, 0 : 3 * SLOTS, at] = jnp.where(hit, full[: 3 * SLOTS], 0.0).astype(BF16)
        weights[q >> 2, 3 * SLOTS :, at] = jnp.where(hit, full[3 * SLOTS :], 0.0).astype(BF16)
        return carry

    stores = []
    out = None
    for part in range(PARTS):
        lax.fori_loop(part * 4, part * 4 + 4, spread, 0, unroll=4)
        store = pltpu.make_async_copy(weights.at[part], weights_ref.at[part], sems.at[COUNT + part])
        store.start()
        stores.append(store)
        term = partial_solve(weights.at[part], gathered, part)
        out = term if out is None else out + term
    into_pool(out, (am_ref, m_ref, bm_ref), pool)
    z = [0.5 * t for t in jump(pool, table)]
    for t in range(TILES):
        z_ref[t] = z[t]
    multiply(z, copies, held, u_ref)
    for store in stores:
        store.wait()


def solve_second_kernel(
    table, out_ref, sums_ref, am_ref, m_ref, bm_ref, a_ref, x_ref, b_ref, inverse_ref, r0_ref, z0_ref, w0_ref,
    y_ref, r_ref, z_ref, scale_ref, u_ref, pool,
):
    fill_pool(pool, a_ref, x_ref, b_ref)
    into_pool(out_ref[...], (am_ref, m_ref, bm_ref), pool)
    energy, curve = totals(sums_ref[0:1, :], 2)
    step = energy / curve
    scale_ref[0] = energy
    scale_ref[1] = curve
    scale_ref[2] = step
    y = jump(pool, table)
    z = []
    for t in range(TILES):
        half = 0.5 * y[t]
        y_ref[t] = half
        r_ref[t] = r0_ref[t] - step * w0_ref[t]
        z.append(z0_ref[t] - step * half)
        z_ref[t] = z[t]
    multiply_held(z, inverse_ref, u_ref)


def solve_third_kernel(
    table, out_ref, sums_ref, am_ref, m_ref, bm_ref, a_ref, x_ref, b_ref,
    scale_ref, z0_ref, w0_ref, y0_ref, r1_ref, z1_ref, v1_ref, multipliers_ref, residual_ref, preconditioned_ref,
    pool,
):
    fill_pool(pool, a_ref, x_ref, b_ref)
    into_pool(out_ref[...], (am_ref, m_ref, bm_ref), pool)
    energy, zv, pv, zw = totals(sums_ref[0:1, :], 4)
    first = scale_ref[2]
    grow = energy / scale_ref[0]
    second = energy / (zv + grow * (pv + zw) + grow * grow * scale_ref[1])
    y = jump(pool, table)
    for p in range(COUNT):
        for c in range(CHUNKS):
            t = p * CHUNKS + c
            at = slice(c * 128, (c + 1) * 128)
            multipliers_ref[p, :, at] = first * z0_ref[t] + second * (z1_ref[t] + grow * z0_ref[t])
            residual_ref[p, :, at] = r1_ref[t] - second * (v1_ref[t] + grow * w0_ref[t])
            preconditioned_ref[p, :, at] = z1_ref[t] - second * (0.5 * y[t] + grow * y0_ref[t])


def shards(loads, local_inverse, schur, corner_map, corner_index, partner, coarse_inverse):
    tiles = lax.axis_size("tile")
    devices = lax.axis_size(GT)
    inner_swap = [(i, i ^ 1) for i in range(tiles)]
    outer_swap = [(i, (i - 1) % tiles if i % 2 == 0 else (i + 1) % tiles) for i in range(tiles)]
    same_core = [[2 * i + c for i in range(devices // 2)] for c in range(2)]
    core = lax.axis_index("tile") % 2

    def both(x):
        return lax.ppermute(x, "tile", inner_swap), lax.ppermute(x, "tile", outer_swap)

    field = shape(TILES, 8, 128)
    pool = pltpu.VMEM((3 * TILES, 8, 128), F32)
    gathered = pltpu.VMEM((16, devices * SLOTS), BF16)
    pay = shape(devices * 5, 128)
    sems = pltpu.SemaphoreType.DMA((COUNT,))

    core = core.astype(jnp.int32).reshape(1)
    held = pltpu.VMEM((COUNT, WIDTH, WIDTH), F32)
    solver = pltpu.VMEM((PARTS, 6 * SLOTS, PART), BF16)
    inverse, stiff = in_hbm(local_inverse), in_hbm(schur)
    u, table = call(
        start_kernel,
        [shape(TILES + 1, 8, 128), jax.ShapeDtypeStruct((16, 128), jnp.int32)],
        [SMEM] + [ANY] * 4,
        [
            pltpu.VMEM((COUNT, CASES, WIDTH), F32),
            pltpu.VMEM((COUNT, CORNERS), jnp.int32),
            pltpu.VMEM((COUNT, FACES), jnp.int32),
            held,
            pltpu.SemaphoreType.DMA((COUNT + 3,)),
        ],
        us=4,
    )(core, in_hbm(loads), in_hbm(corner_index), in_hbm(partner), inverse)
    ua, ub = both(u)
    indices = (ua, u, ub)

    def spread(x):
        return lax.all_to_all(x.reshape(devices, -1), GT, 0, 0, tiled=True).reshape(-1, 128)

    def through(x):
        (q,) = call(product_kernel, [field], [VMEM, ANY], [held, sems], us=3)(x, stiff)
        qa, qb = both(q)
        return qa, q, qb

    r0, card = call(send_first_kernel, [field, shape(devices // 2 * CARD, 128)], [SMEM] + [VMEM] * 5, [pool])(
        table, ua, u, ub, corner_map, coarse_inverse
    )
    own_cards = lax.all_to_all(
        card.reshape(devices // 2, -1), GT, 0, 0, tiled=True, axis_index_groups=same_core
    ).reshape(-1, 128)
    pooled = through(r0)
    ma, mb = both(corner_map)
    maps = (ma, corner_map, mb)
    own_cards, pooled, maps = lax.optimization_barrier((own_cards, pooled, maps))
    other_cards = lax.ppermute(own_cards, "tile", inner_swap)
    z0, u, weights = pl.pallas_call(
        solve_first_kernel,
        in_specs=[SMEM] * 2 + [ANY] * 3 + [VMEM] * 8 + [ANY],
        out_specs=[VMEM, VMEM, ANY],
        out_shape=[field, field, pltpu.HBM((PARTS, 6 * SLOTS, PART), BF16)],
        scratch_shapes=[
            pool,
            gathered,
            solver,
            held,
            pltpu.SemaphoreType.DMA((COUNT + PARTS + 3,)),
            pltpu.VMEM((3 * SLOTS, 128), F32),
            pltpu.VMEM((3 * SLOTS, 128), jnp.int32),
            pltpu.VMEM((devices // 2, 128), jnp.int32),
            pltpu.SMEM((3, 8, 128), F32),
        ],
        compiler_params=PARAMS,
        cost_estimate=pl.CostEstimate(flops=4_000_000_000, bytes_accessed=20_000_000, transcendentals=0),
    )(core, table, *indices, own_cards, other_cards, *maps, *pooled, inverse)
    weights = in_hbm(weights)
    rest = pltpu.VMEM((PARTS - KEEP, 6 * SLOTS, PART), BF16)
    kept_shape = jax.ShapeDtypeStruct((KEEP, 6 * SLOTS, PART), BF16)
    coarse_scratch = [gathered, rest, pltpu.SemaphoreType.DMA((PARTS - KEEP,))]

    def hold(after):
        return call(hold_kernel, [shape(COUNT, WIDTH, WIDTH)], [ANY] * 2, [sems], us=2)(after, stiff)[0]

    def keep(after):
        return call(keep_kernel, [kept_shape], [ANY] * 2, [pltpu.SemaphoreType.DMA((KEEP,))], us=2)(after, weights)[0]

    coarse_out = [shape(6 * SLOTS, 16), shape(8, 128)]
    ua, ub = both(u)
    w0, parts, q = call(send_second_kernel, [field, pay, field], [SMEM] + [VMEM] * 7, [pool], us=3)(
        table, ua, u, ub, corner_map, hold(u), r0, z0
    )
    qa, qb = both(q)
    out, sums = call(coarse_kernel, coarse_out, [VMEM, VMEM, ANY], coarse_scratch, us=20)(spread(parts), keep(q), weights)
    y0, r1, z1, scale, u = call(
        solve_second_kernel, [field, field, field, shape(3, 8, 128), field], [SMEM] + [VMEM] * 12, [pool], us=3
    )(table, out, sums, *maps, qa, q, qb, local_inverse, r0, z0, w0)
    ua, ub = both(u)
    v1, parts, q = call(send_third_kernel, [field, pay, field], [SMEM] + [VMEM] * 9, [pool], us=3)(
        table, ua, u, ub, corner_map, hold(u), r1, z1, z0, w0
    )
    qa, qb = both(q)
    out, sums = call(coarse_kernel, coarse_out, [VMEM, VMEM, ANY], coarse_scratch, us=20)(spread(parts), keep(q), weights)
    return tuple(
        call(solve_third_kernel, [shape(COUNT, CASES, WIDTH)] * 3, [SMEM] + [VMEM] * 15, [pool], us=2)(
            table, out, sums, *maps, qa, q, qb, scale, z0, w0, y0, r1, z1, v1
        )
    )


def solution(mesh):
    three = P(GT, None, None)
    two = P(GT, None)
    return jax.shard_map(
        shards,
        mesh=mesh,
        in_specs=(three, three, three, three, two, two, two),
        out_specs=(three, three, three),
        check_vma=False,
    )
```
